32 devices in a mesh: dp: 16 (over z, y, core), tensor: 2 (over x).
Axes of the slice: x: 2, y: 2, z: 4, core: 2. Of those that a mesh axis runs over, the one named last changes fastest.
Arguments:
- tokens: bfloat16 [49152, 1024], P(('dp', 'tensor')), may hold values from -6 to 6
- lengths: int32 [48], replicated, may hold values from 1 to 1024, 36864 in all
- order: int32 [48], replicated, may hold values from 0 to 47, each once
- gain_attn: float32 [1024], replicated, may hold values from 0.25 to 1.75
- w_qkv: bfloat16 [1024, 3, 1024], P(None, None, 'tensor'), may hold values from -0.1875 to 0.1875
- w_out: bfloat16 [1024, 1024], P('tensor'), may hold values from -0.75 to 0.75
- gain_mlp: float32 [1024], replicated, may hold values from 0.25 to 1.75
- w_in: bfloat16 [1024, 2, 2624], P(None, None, 'tensor'), may hold values from -0.1875 to 0.1875
- w_down: bfloat16 [2624, 1024], P('tensor'), may hold values from -0.25 to 0.25
- cotangent: bfloat16 [49152, 1024], P(('dp', 'tensor')), may hold values from -6 to 6
Outputs:
- output: bfloat16 [49152, 1024], P(('dp', 'tensor'))
- input_grad: float32 [49152, 1024], P(('dp', 'tensor'))
- grad_gain_attn: float32 [1024], replicated
- grad_w_qkv: float32 [1024, 3, 1024], P(None, None, 'tensor')
- grad_w_out: float32 [1024, 1024], P('tensor')
- grad_gain_mlp: float32 [1024], replicated
- grad_w_in: float32 [1024, 2, 2624], P(None, None, 'tensor')
- grad_w_down: float32 [2624, 1024], P('tensor')
The draws below stay inside these ranges and needn't reach their ends.
Inputs may be any that keep to these rules, and one draw needn't show every extreme that they name: The lengths sum to 36864 and the largest equals 1024. `order`: each sequence number appears exactly once.
All inputs are finite; a program needn't handle non-finite values.
Results may differ from the reference program's by a relative error of at most 0.02.
Values may be sent and summed in bfloat16 or wider, within the bound.
A program may use at most 320 MiB of HBM per device.

```python
import math
import jax
import jax.numpy as jnp
import numpy as np
from jax import lax

D = 1024
HEADS = 16
HEAD_DIM = 64
FF = 2624
HALF = 64
MAXLEN = 1024
SEQ_DEV = 3
QBLOCK = 512
SLOTS = 48
TOKENS = 49152
N_DP = 16


def levels(own_key, shape, shards, low, top_value):
    level = 1.0
    for dim, blocks in shards:
        draws = jax.random.uniform(jax.random.fold_in(jax.random.fold_in(own_key, 6), dim), (blocks,), jnp.float32, low / len(shards), top_value / len(shards))
        level = level * jnp.repeat(jnp.exp(draws), shape[dim] // blocks).reshape((-1,) + (1,) * (len(shape) - 1 - dim))
    return level


def profile(amount, total, reach, slope):
    weights = [(1 << 20) // math.isqrt(grade ** slope) + 1 for grade in range(2, amount + 1)]
    rest, given = total - reach - (amount - 1), [1] * (amount - 1)
    while rest > 0:
        free = [i for i in range(amount - 1) if given[i] < reach]
        mass, remaining = sum([weights[i] for i in free]), rest
        for i in free:
            extra = min(reach - given[i], max(1, remaining * weights[i] // mass), rest)
            given[i] = given[i] + extra
            rest = rest - extra
    return np.array([reach] + given)


def uneven_parts(stream_key, count, total, reach, slope):
    if count == 2:
        one = jax.random.randint(stream_key, (), max(1, total - reach), min(reach, total - 1) + 1)
        return jnp.stack([one, total - one])
    tallies = jnp.asarray(profile(count, total, reach, slope), jnp.int32)
    twos = (count - 1) // 2
    donor, receiver = tallies[1:1 + 2 * twos:2], tallies[2:2 + 2 * twos:2]
    margin = jnp.minimum(donor - 1, reach - receiver)
    shifted = jax.random.randint(jax.random.fold_in(stream_key, 1), (twos,), 0, 1 << 20) % (margin + 1)
    tallies = tallies.at[1:1 + 2 * twos:2].set(donor - shifted).at[2:2 + 2 * twos:2].set(receiver + shifted)
    return tallies[jax.random.permutation(jax.random.fold_in(stream_key, 2), count)]


def scatter_about(stream_key, extent, width, limit, split=(), kind=jnp.bfloat16):
    level = levels(stream_key, extent, split, -0.22, 0.18) if split else 1.0
    values = jax.random.normal(stream_key, extent, jnp.float32) * width * level
    return jnp.minimum(jnp.maximum(values, -limit), limit).astype(kind)


def setup_inputs(seed: int = 0) -> dict:
    keys = jax.random.split(jax.random.key(seed), 11)
    return {
        "tokens": scatter_about(keys[0], (TOKENS, D), 1.0, 6.0, ((0, 32),)),
        "lengths": uneven_parts(keys[1], SLOTS, SLOTS * MAXLEN * 3 // 4, MAXLEN, 2).astype(jnp.int32),
        "order": jax.random.permutation(keys[2], SLOTS).astype(jnp.int32),
        "gain_attn": jnp.clip(1.0 + 0.15 * jax.random.normal(keys[3], (D,), jnp.float32), 0.25, 1.75),
        "w_qkv": scatter_about(keys[4], (D, 3, D), D ** -0.5, 0.1875, ((2, 2),)),
        "w_out": scatter_about(keys[5], (D, D), (D // 16) ** -0.5, 0.75, ((0, 2),)),
        "gain_mlp": jnp.clip(1.0 + 0.15 * jax.random.normal(keys[6], (D,), jnp.float32), 0.25, 1.75),
        "w_in": scatter_about(keys[7], (D, 2, FF), D ** -0.5, 0.1875, ((2, 2),)),
        "w_down": scatter_about(keys[8], (FF, D), (FF // 4) ** -0.5, 0.25, ((0, 2),)),
        "cotangent": scatter_about(keys[9], (TOKENS, D), 1.0, 6.0, ((0, 32),)),
    }


@jax.custom_vjp
def low(v):
    return lax.optimization_barrier(v.astype(jnp.bfloat16)).astype(jnp.float32)

@jax.custom_vjp
def low_back(v):
    return v

def low_keep(v):
    return (low(v), None)

def low_pass(kept, grad):
    return (grad,)

def back_keep(v):
    return (v, None)

def back_low(kept, grad):
    return (low(grad),)
low.defvjp(low_keep, low_pass)
low_back.defvjp(back_keep, back_low)

def layer_norm(values, gain):
    center = values - lax.optimization_barrier(jnp.mean(values, -1, keepdims=True))
    spread = lax.optimization_barrier(jnp.mean(center * center, -1, keepdims=True))
    return center * lax.rsqrt(spread + 1e-05) * gain

def allowed_pairs(offset, length):
    query_pos = offset + jnp.arange(QBLOCK, dtype=jnp.int32)
    key_pos = offset - HALF + jnp.arange(QBLOCK + 2 * HALF, dtype=jnp.int32)
    nearby = jnp.abs(query_pos[:, None] - key_pos[None, :]) <= HALF
    inside = (key_pos >= 0) & (key_pos < MAXLEN)
    living = (key_pos[None, :] < length) | (query_pos[:, None] == key_pos[None, :])
    return nearby & inside[None, :] & living

def band_attend(queries, keyset, values, length):
    scale_qk = HEAD_DIM ** (-0.5)
    pad_width = ((HALF, HALF), (0, 0), (0, 0))
    keys_pad = jnp.pad(keyset, pad_width)
    values_pad = jnp.pad(values, pad_width)
    window = QBLOCK + 2 * HALF

    def one_block(block_id):
        offset = block_id * QBLOCK
        query_blk = lax.dynamic_slice_in_dim(queries, offset, QBLOCK, 0)
        keys_blk = lax.dynamic_slice_in_dim(keys_pad, offset, window, 0)
        values_blk = lax.dynamic_slice_in_dim(values_pad, offset, window, 0)
        scores = jnp.einsum('qhd,khd->hqk', query_blk, keys_blk, precision=lax.Precision.HIGHEST) * scale_qk
        scores = low_back(scores)
        scores = jnp.where(allowed_pairs(offset, length)[None], scores, -1e+30)
        row_max = lax.optimization_barrier(jnp.max(scores, -1, keepdims=True))
        expons = jnp.exp(scores - row_max)
        attn_prob = low(expons / lax.optimization_barrier(jnp.sum(expons, -1, keepdims=True)))
        return jnp.einsum('hqk,khd->qhd', attn_prob, values_blk, precision=lax.Precision.HIGHEST)
    block_ids = jnp.arange(MAXLEN // QBLOCK, dtype=jnp.int32)
    attended = lax.map(jax.checkpoint(one_block), block_ids)
    return attended.reshape(MAXLEN, HEADS * HEAD_DIM)

def layer_forward(params, tokens_f, slot_len):
    gain_attn, w_qkv, w_out, gain_mlp, w_in, w_down = params
    row_count = tokens_f.shape[0]
    slot_count = row_count // MAXLEN
    position = jnp.arange(MAXLEN, dtype=jnp.int32)
    keep_row = (position[None, :] < slot_len[:, None]).astype(jnp.float32).reshape(row_count, 1)
    normed = low(layer_norm(tokens_f, gain_attn))
    packed = jnp.dot(normed, w_qkv.reshape(D, 3 * D), precision=lax.Precision.HIGHEST)
    packed = low(low_back(packed)).reshape(slot_count, MAXLEN, 3, HEADS, HEAD_DIM)
    attended = jax.vmap(band_attend)(packed[:, :, 0], packed[:, :, 1], packed[:, :, 2], slot_len)
    attended = low(low_back(attended.reshape(row_count, D)))
    hidden_in = tokens_f + low_back(jnp.dot(attended, w_out, precision=lax.Precision.HIGHEST))
    normed_mlp = low(layer_norm(hidden_in, gain_mlp))
    lifted = jnp.dot(normed_mlp, w_in.reshape(D, 2 * FF), precision=lax.Precision.HIGHEST)
    lifted = low_back(lifted).reshape(row_count, 2, FF)
    gate_out = low(jax.nn.gelu(lifted[:, 0], approximate=False) * lifted[:, 1])
    branch = low_back(jnp.dot(gate_out, w_down, precision=lax.Precision.HIGHEST))
    return keep_row * (hidden_in + branch)

def reference(tokens, lengths, order, gain_attn, w_qkv, w_out, gain_mlp, w_in, w_down, cotangent):
    params = (gain_attn.astype(jnp.float32), w_qkv.astype(jnp.float32), w_out.astype(jnp.float32), gain_mlp.astype(jnp.float32), w_in.astype(jnp.float32), w_down.astype(jnp.float32))
    slot_len = lengths[order].astype(jnp.int32)
    group_rows = SEQ_DEV * MAXLEN
    token_groups = tokens.astype(jnp.float32).reshape(N_DP, group_rows, D)
    grad_groups = cotangent.astype(jnp.float32).reshape(N_DP, group_rows, D)
    len_groups = slot_len.reshape(N_DP, SEQ_DEV)

    def one_group(summed, group_item):
        tokens_f, grad_f, lens_here = group_item
        result, pullback = jax.vjp(lambda weights, values: layer_forward(weights, values, lens_here), params, tokens_f)
        weight_grads, token_grad = pullback(grad_f)
        summed = jax.tree.map(jnp.add, summed, weight_grads)
        return (summed, (result.astype(jnp.bfloat16), token_grad))
    blank = jax.tree.map(jnp.zeros_like, params)
    summed, (results, token_grads) = lax.scan(one_group, blank, (token_groups, grad_groups, len_groups))
    return (results.reshape(TOKENS, D), token_grads.reshape(TOKENS, D), summed[0], summed[1], summed[2], summed[3], summed[4], summed[5])
```

```python
import math
import jax
import jax.numpy as jnp
from jax import lax
from jax.experimental import pallas as pl
from jax.experimental.pallas import tpu as pltpu
from jax.sharding import PartitionSpec as P

HEAD_DIM = 64
HALF = 64
MAXLEN = 1024
BQ = 128
LOW = jnp.bfloat16
NEG = -1e30


def cols_dot(left, right):
    return lax.dot_general(left, right, (((1,), (1,)), ((), ())), preferred_element_type=jnp.float32)


def rows_dot(left, right):
    return lax.dot_general(left, right, (((0,), (0,)), ((), ())), preferred_element_type=jnp.float32)


def plain_dot(left, right):
    return lax.dot_general(left, right, (((1,), (0,)), ((), ())), preferred_element_type=jnp.float32)


def window_masks(pos0, length):
    j = lax.broadcasted_iota(jnp.int32, (BQ, 2 * BQ), 0)
    i = lax.broadcasted_iota(jnp.int32, (BQ, 2 * BQ), 1) % BQ
    near = i <= j
    key_pos = pos0 - HALF + j + jnp.where(near, 0, BQ)
    top = jnp.minimum(length, MAXLEN)
    own = j == (i + HALF) % BQ
    bias = jnp.where(((key_pos >= 0) & (key_pos < top)) | own, 0.0, NEG)
    lane = lax.broadcasted_iota(jnp.int32, (1, 2 * BQ), 1) % BQ
    last_bias = jnp.where(pos0 + HALF + lane < top, 0.0, NEG)
    return near, i == j, bias, last_bias


def split_heads(pair):
    lane = lax.broadcasted_iota(jnp.int32, pair.shape, 1)
    zero = jnp.zeros_like(pair)
    return jnp.concatenate([jnp.where(lane < HEAD_DIM, pair, zero), jnp.where(lane >= HEAD_DIM, pair, zero)], 0)


def join_heads(wide, scale=None):
    first, second = wide[:HEAD_DIM, :BQ], wide[HEAD_DIM:, BQ:]
    if scale is not None:
        first, second = first * scale[:, :BQ], second * scale[:, BQ:]
    return jnp.concatenate([first, second], 0).T


def fold(near, diag, wide):
    low = wide[BQ:]
    return jnp.where(near, wide[:BQ], low), jnp.sum(jnp.where(diag, low, 0.0), 0, keepdims=True)


def unfold(near, diag, tile, last):
    zero = jnp.zeros_like(tile)
    return jnp.concatenate(
        [jnp.where(near, tile, zero), jnp.where(near, jnp.where(diag, last, zero), tile)], 0
    ).astype(LOW)


def window_rows(before, here, after, c):
    return jnp.concatenate([before[:, c], here[:, c], after[:, c]], 0)


def attend_kernel(place, q, kb, kh, ka, vb, vh, va, out_ref, log_ref):
    blk = pl.program_id(0)
    near, diag, bias, last_bias = window_masks(place[0, blk], place[1, blk])
    for pair in range(out_ref.shape[1] // BQ):
        c = slice(pair * BQ, (pair + 1) * BQ)
        queries = split_heads(q[:, c] * 0.125)
        keyset = window_rows(kb, kh, ka, c)
        values = window_rows(vb, vh, va, c)
        scores, last = fold(near, diag, cols_dot(keyset, queries))
        scores, last = scores + bias, last + last_bias
        row_max = jnp.maximum(jnp.max(scores, 0, keepdims=True), last)
        expons, last = jnp.exp(scores - row_max), jnp.exp(last - row_max)
        summed = jnp.sum(expons, 0, keepdims=True) + last
        probs = unfold(near, diag, expons, last)
        out_ref[:, c] = join_heads(rows_dot(values, probs), 1.0 / summed).astype(LOW)
        log_ref[0, pair:pair + 1] = row_max + jnp.log(summed)


def attend_back_kernel(
    place, q, kb, kh, ka, vb, vh, va, g_ref, log_ref, dq_ref, dk_ref, dv_ref, edge_ref, carry, tail, dq_keep
):
    step = pl.program_id(0)
    steps = pl.num_programs(0)
    width = g_ref.shape[1]

    @pl.when(step == 0)
    def _():
        carry[...] = jnp.zeros_like(carry)
        tail[...] = jnp.zeros_like(tail)
        dq_keep[...] = jnp.zeros_like(dq_keep)

    dq_ref[...] = dq_keep[...]
    dk_ref[:HALF] = tail[:, :width]
    dv_ref[:HALF] = tail[:, width:]

    @pl.when(step < steps - 1)
    def _():
        near, diag, bias, last_bias = window_masks(place[0, step], place[1, step])
        for pair in range(width // BQ):
            c = slice(pair * BQ, (pair + 1) * BQ)
            v = slice(width + pair * BQ, width + (pair + 1) * BQ)
            queries = split_heads(q[:, c] * 0.125)
            keyset = window_rows(kb, kh, ka, c)
            values = window_rows(vb, vh, va, c)
            grads = split_heads(g_ref[:, c])
            log_row = log_ref[0, pair:pair + 1]
            scores, last = fold(near, diag, cols_dot(keyset, queries))
            expons, last = jnp.exp(scores + (bias - log_row)), jnp.exp(last + (last_bias - log_row))
            prob_grad, last_grad = fold(near, diag, cols_dot(values, grads))
            inner = jnp.sum(expons * prob_grad, 0, keepdims=True) + last * last_grad
            score_grad = unfold(near, diag, expons * (prob_grad - inner), last * (last_grad - inner))
            probs = unfold(near, diag, expons, last)
            dq_keep[:, c] = join_heads(rows_dot(keyset, score_grad) * 0.125).astype(LOW)
            for lanes, out, grad in ((c, dk_ref, plain_dot(score_grad, queries)), (v, dv_ref, plain_dot(probs, grads))):
                done = (carry[:, lanes] + grad[:BQ]).astype(LOW)
                carry[:, lanes] = grad[BQ:]
                out[HALF:, c] = done[:HALF]
                tail[:, lanes] = done[HALF:]
                edge_ref[0, :, lanes] = jnp.where(step == 0, done[:HALF], edge_ref[0, :, lanes])

    @pl.when(step == steps - 1)
    def _():
        done = carry[...].astype(LOW)
        dk_ref[HALF:] = done[:HALF, :width]
        dv_ref[HALF:] = done[:HALF, width:]
        edge_ref[1] = done[HALF:]


def window_specs(width, blocks):
    last = blocks - 1
    here = lambda b, _: (jnp.minimum(b, last), 0)
    before = lambda b, _: (jnp.where(b == 0, 2 * blocks, 2 * jnp.minimum(b, last) - 1), 0)
    after = lambda b, _: (jnp.where(b >= last, 2 * blocks + 1, 2 * b + 2), 0)
    one = [pl.BlockSpec((HALF, width), before), pl.BlockSpec((BQ, width), here), pl.BlockSpec((HALF, width), after)]
    return [one[1]] + one + one


def attend(place, q, k, v):
    blocks, width = k.shape[0] // BQ - 1, k.shape[1]
    pairs = width // BQ
    return pl.pallas_call(
        attend_kernel,
        grid_spec=pltpu.PrefetchScalarGridSpec(
            num_scalar_prefetch=1,
            grid=(blocks,),
            in_specs=window_specs(width, blocks),
            out_specs=[
                pl.BlockSpec((BQ, width), lambda b, _: (b, 0)),
                pl.BlockSpec((1, pairs, 2 * BQ), lambda b, _: (b, 0, 0)),
            ],
        ),
        out_shape=[
            jax.ShapeDtypeStruct((blocks * BQ, width), LOW),
            jax.ShapeDtypeStruct((blocks, pairs, 2 * BQ), jnp.float32),
        ],
        compiler_params=pltpu.CompilerParams(vmem_limit_bytes=48 << 20),
        cost_estimate=pl.CostEstimate(
            flops=blocks * pairs * BQ * BQ * BQ * 256, bytes_accessed=blocks * BQ * width * 16, transcendentals=0
        ),
        name="attend",
    )(place, q, k, k, k, v, v, v)


def attend_back(place, q, k, v, grads, logs):
    blocks, width = grads.shape[0] // BQ, k.shape[1]
    pairs = width // BQ
    here = lambda b, _: (jnp.minimum(b, blocks - 1), 0)
    done = pl.BlockSpec((BQ, width), lambda b, _: (jnp.maximum(b - 1, 0), 0))
    return pl.pallas_call(
        attend_back_kernel,
        grid_spec=pltpu.PrefetchScalarGridSpec(
            num_scalar_prefetch=1,
            grid=(blocks + 1,),
            in_specs=window_specs(width, blocks)
            + [
                pl.BlockSpec((BQ, width), here),
                pl.BlockSpec((1, pairs, 2 * BQ), lambda b, _: (jnp.minimum(b, blocks - 1), 0, 0)),
            ],
            out_specs=[done, done, done, pl.BlockSpec((2, HALF, 2 * width), lambda b, _: (0, 0, 0))],
            scratch_shapes=[
                pltpu.VMEM((BQ, 2 * width), jnp.float32),
                pltpu.VMEM((HALF, 2 * width), LOW),
                pltpu.VMEM((BQ, width), LOW),
            ],
        ),
        out_shape=[jax.ShapeDtypeStruct((blocks * BQ, width), LOW)] * 3
        + [jax.ShapeDtypeStruct((2, HALF, 2 * width), LOW)],
        compiler_params=pltpu.CompilerParams(vmem_limit_bytes=48 << 20),
        cost_estimate=pl.CostEstimate(
            flops=blocks * pairs * BQ * BQ * BQ * 512, bytes_accessed=blocks * BQ * width * 26, transcendentals=0
        ),
        name="attend_back",
    )(place, q, k, k, k, v, v, v, grads, logs)


AXES = ("dp", "tensor")
EPS = 1e-05


def erf_parts(first, second):
    first, second = first.astype(jnp.float32), second.astype(jnp.float32)
    phi_sum = 0.5 * (1.0 + lax.erf(first * (2.0 ** -0.5)))
    density = jnp.exp(-0.5 * first * first) * ((2.0 * math.pi) ** -0.5)
    gelu = first * phi_sum
    return (gelu * second).astype(LOW), (second * (phi_sum + first * density)).astype(LOW), gelu.astype(LOW)


def norm_parts(values):
    center = values - jnp.mean(values, -1, keepdims=True)
    rate = lax.rsqrt(jnp.mean(center * center, -1, keepdims=True) + EPS)
    return center * rate, rate


def norm_back(values, gain, grad):
    unit, rate = norm_parts(values)
    pulled = grad * gain
    mean_one = jnp.mean(pulled, -1, keepdims=True)
    mean_two = jnp.mean(pulled * unit, -1, keepdims=True)
    return rate * (pulled - mean_one - unit * mean_two), jnp.sum(grad * unit, 0)


class Links:
    def __init__(self, dp, tensor):
        self.dp, self.tensor = dp, tensor

    def move(self, value, bit=0, across=0):
        pairs = [
            (d * self.tensor + t, (d ^ bit) * self.tensor + (t ^ across))
            for d in range(self.dp) for t in range(self.tensor)
        ]
        return lax.ppermute(value, AXES, pairs)

    def shift(self, value, by):
        pairs = [
            (d * self.tensor + t, d * self.tensor + t + by)
            for d in range(self.dp) for t in range(self.tensor) if 0 <= t + by < self.tensor
        ]
        return lax.ppermute(value, AXES, pairs)


def cut(value, index, count, axis):
    size = value.shape[axis] // 4
    return lax.dynamic_slice_in_dim(value, index * size, count * size, axis)


def fetch_other(links, value, axis, me):
    direct = links.move(cut(value, me, 1, axis), across=1)
    relayed = links.move(direct, bit=2)
    return jnp.concatenate([direct, relayed, links.move(direct, bit=1), links.move(relayed, bit=1)], axis)


def partner_order(value, me):
    a, b, c, d = jnp.split(value, 4, -1)
    odd = me % 2 == 1
    a, b, c, d = jnp.where(odd, b, a), jnp.where(odd, a, b), jnp.where(odd, d, c), jnp.where(odd, c, d)
    low, high = jnp.concatenate([a, b], -1), jnp.concatenate([c, d], -1)
    swap = me // 2 == 1
    return jnp.concatenate([jnp.where(swap, high, low), jnp.where(swap, low, high)], -1)


def reduce_grad(links, own, other, axis, me):
    core, row = me // 2, me % 2
    got_other = links.move(cut(other, 2, 2, axis), bit=1)
    got_own = links.move(cut(own, 2 * (1 - core), 2, axis), bit=1)
    far = cut(other, 0, 2, axis) + got_other
    near = cut(own, 2 * core, 2, axis) + got_own
    got = links.move(far, across=1)
    half = near.shape[axis] // 2
    keep = lax.dynamic_slice_in_dim(near, row * half, half, axis) + lax.slice_in_dim(got, 0, half, axis=axis)
    send = lax.dynamic_slice_in_dim(near, (1 - row) * half, half, axis) + lax.slice_in_dim(got, half, 2 * half, axis=axis)
    total = keep + links.move(send, bit=2)
    bit = 4
    while bit < links.dp:
        total = total + links.move(total, bit=bit)
        bit = 2 * bit
    second = links.move(total, bit=2)
    quarters = [total, second, links.move(total, bit=1), links.move(second, bit=1)]
    out = []
    for place in range(4):
        piece = quarters[3]
        for k in range(3):
            piece = jnp.where(me == place ^ k, quarters[k], piece)
        out.append(piece.astype(jnp.float32))
    return jnp.concatenate(out, axis)


def on_device(tokens, lengths, order, gain_attn, w_qkv, w_out, gain_mlp, w_in, w_down, cotangent):
    rows, model = tokens.shape
    dp, tensor = lax.axis_size("dp"), lax.axis_size("tensor")
    dp_id, tensor_id = lax.axis_index("dp"), lax.axis_index("tensor")
    links = Links(dp, tensor)
    paired = tensor == 2 and dp >= 4 and dp & (dp - 1) == 0
    me = 2 * (dp_id % 2) + dp_id // 2 % 2

    slot_count = rows * tensor // MAXLEN
    my_order = lax.dynamic_slice_in_dim(order, dp_id * slot_count, slot_count, 0)
    chosen = my_order[:, None] == jnp.arange(lengths.shape[0], dtype=jnp.int32)[None, :]
    slot_len = jnp.sum(jnp.where(chosen, lengths[None, :], 0), 1)
    slots = jnp.arange(slot_count, dtype=jnp.int32)[None, :]
    row_index = tensor_id * rows + jnp.arange(rows, dtype=jnp.int32)
    row_len = jnp.sum(jnp.where((row_index // MAXLEN)[:, None] == slots, slot_len[None, :], 0), 1)
    keep_row = (row_index % MAXLEN < row_len).astype(jnp.float32)[:, None]
    place = jnp.stack([row_index[::BQ] % MAXLEN, row_len[::BQ]])

    w_qkv = w_qkv.transpose(1, 0, 2)
    w_in = w_in.transpose(1, 2, 0)

    if paired:
        w_all = [
            (w_qkv, w_out, w_in, w_down),
            tuple(fetch_other(links, w, axis, me) for w, axis in ((w_qkv, 2), (w_out, 0), (w_in, 1), (w_down, 0))),
        ]
    else:
        full = [
            lax.all_gather(w, "tensor", axis=axis, tiled=True)
            for w, axis in ((w_qkv, 2), (w_out, 0), (w_in, 1), (w_down, 0))
        ]
        w_all = [tuple(full)]

    around = jnp.concatenate([tokens, links.shift(tokens[rows - HALF:], 1), links.shift(tokens[:HALF], -1)], 0)
    normed = (norm_parts(around.astype(jnp.float32))[0] * gain_attn).astype(LOW)
    normed_own = normed[:rows]
    tokens_f = tokens.astype(jnp.float32)

    saved = []
    branch = None
    for wqkv, wout, _, _ in w_all:
        q, k, v = (plain_dot(normed, wqkv[i]).astype(LOW) for i in range(3))
        attended, logs = attend(place, q, k, v)
        part = plain_dot(attended, wout)
        branch = part if branch is None else branch + part
        saved.append((q, k, v, attended, logs))
    hidden_in = tokens_f + branch
    normed_mlp = (norm_parts(hidden_in)[0] * gain_mlp).astype(LOW)
    out_grad = keep_row * cotangent.astype(jnp.float32)
    out_low = out_grad.astype(LOW)

    gates = []
    branch = None
    for _, _, win, wdown in w_all:
        gate_out, slope, gelu = erf_parts(cols_dot(normed_mlp, win[0]).astype(LOW), cols_dot(normed_mlp, win[1]).astype(LOW))
        part = plain_dot(gate_out, wdown)
        branch = part if branch is None else branch + part
        gates.append((gate_out, slope, gelu))
    output = (keep_row * (hidden_in + branch)).astype(LOW)

    down_grads = [rows_dot(gate_out, out_low).astype(LOW) for gate_out, _, _ in gates]
    in_grads = []
    mlp_grad = None
    for (_, _, win, wdown), (_, slope, gelu) in zip(w_all, gates):
        gate_grad = cols_dot(out_low, wdown)
        lift = ((gate_grad * slope).astype(LOW), (gate_grad * gelu).astype(LOW))
        in_grads.append([rows_dot(g, normed_mlp).astype(LOW) for g in lift])
        for g, w in zip(lift, win):
            part = plain_dot(g, w)
            mlp_grad = part if mlp_grad is None else mlp_grad + part
    hidden_part, gain_mlp_grad = norm_back(hidden_in, gain_mlp, mlp_grad)
    hidden_grad = out_grad + hidden_part
    hidden_low = hidden_grad.astype(LOW)

    out_grads, edges, pulled = [], [], []
    for (wqkv, wout, _, _), (q, k, v, attended, logs) in zip(w_all, saved):
        out_grads.append(rows_dot(attended, hidden_low).astype(LOW))
        attended_grad = cols_dot(hidden_low, wout).astype(LOW)
        dq, dk, dv, edge = attend_back(place, q, k, v, attended_grad, logs)
        width = dk.shape[1]
        edge = [edge[side, :, part * width:(part + 1) * width] for side in range(2) for part in range(2)]
        if paired:
            edge = [partner_order(e, me) for e in edge]
        edges.append([links.shift(e, 1 if side else -1) for e, side in zip(edge, (0, 0, 1, 1))])
        pulled.append((dq, dk, dv))
    if paired:
        edges = edges[::-1]
    qkv_grads = []
    attn_grad = None
    for (wqkv, _, _, _), (dq, dk, dv), (dk_after, dv_after, dk_before, dv_before) in zip(w_all, pulled, edges):
        dk = dk.at[:HALF].add(dk_before).at[rows - HALF:].add(dk_after)
        dv = dv.at[:HALF].add(dv_before).at[rows - HALF:].add(dv_after)
        qkv_grads.append(jnp.stack([rows_dot(normed_own, g).astype(LOW) for g in (dq, dk, dv)]))
        for g, w in zip((dq, dk, dv), wqkv):
            part = cols_dot(g, w)
            attn_grad = part if attn_grad is None else attn_grad + part
    input_part, gain_attn_grad = norm_back(tokens_f, gain_attn, attn_grad)
    input_grad = hidden_grad + input_part

    if paired:
        grad_w_down = reduce_grad(links, down_grads[0], down_grads[1], 0, me)
        grad_w_in = jnp.stack([reduce_grad(links, in_grads[0][i], in_grads[1][i], 0, me) for i in range(2)])
        grad_w_out = reduce_grad(links, out_grads[0], out_grads[1], 0, me)
        grad_w_qkv = reduce_grad(links, qkv_grads[0], qkv_grads[1], 2, me)
    else:
        grad_w_down, grad_w_in, grad_w_out, grad_w_qkv = (
            lax.psum(lax.psum_scatter(g, "tensor", scatter_dimension=axis, tiled=True), "dp").astype(jnp.float32)
            for g, axis in ((down_grads[0], 0), (jnp.stack(in_grads[0]), 1), (out_grads[0], 0), (qkv_grads[0], 2))
        )
    gain_total = lax.psum(jnp.stack((gain_attn_grad, gain_mlp_grad)), AXES)
    return (
        output,
        input_grad,
        gain_total[0],
        grad_w_qkv.transpose(1, 0, 2),
        grad_w_out,
        gain_total[1],
        grad_w_in.transpose(2, 0, 1),
        grad_w_down,
    )


def solution(mesh):
    split = P(AXES, None)
    wide = P(None, None, "tensor")
    tall = P("tensor", None)
    return jax.shard_map(
        on_device,
        mesh=mesh,
        in_specs=(split, P(), P(), P(), wide, tall, P(), wide, tall, split),
        out_specs=(split, split, P(), wide, tall, P(), wide, tall),
        check_vma=False,
    )
```

```python
import functools
import math

import jax
import jax.numpy as jnp
from jax import lax
from jax.experimental import pallas as pl
from jax.experimental.pallas import tpu as pltpu
from jax.sharding import PartitionSpec as P

AXES = ("dp", "tensor")
EPS = 1e-05
HEAD_DIM = 64
HALF = 64
MAXLEN = 1024
BQ = 128
LOW = jnp.bfloat16
NEG = -1e30


def cols_dot(left, right):
    return lax.dot_general(left, right, (((1,), (1,)), ((), ())), preferred_element_type=jnp.float32)


def rows_dot(left, right):
    return lax.dot_general(left, right, (((0,), (0,)), ((), ())), preferred_element_type=jnp.float32)


def plain_dot(left, right):
    return lax.dot_general(left, right, (((1,), (0,)), ((), ())), preferred_element_type=jnp.float32)


def norm_parts(values):
    center = values - jnp.mean(values, -1, keepdims=True)
    rate = lax.rsqrt(jnp.mean(center * center, -1, keepdims=True) + EPS)
    return center * rate, rate


def shaped(shape, dtype=LOW):
    return jax.ShapeDtypeStruct(shape, dtype)


def run(body, name, grid, ins, outs, after=(), place=None, scratch=(), flops=0, vmem=56, seen=False):
    extra = [a for a in after if a is not None]
    count = len(ins)

    def kernel(*refs):
        lead = refs[:1] if place is not None else ()
        refs = refs[len(lead):]
        body(*lead, *refs[:count], *refs[count + len(extra):])

    def spec(block, index):
        if place is not None and not seen:
            return pl.BlockSpec(block, lambda *a: index(*a[:-1]))
        return pl.BlockSpec(block, index)

    call = pl.pallas_call(
        kernel,
        grid_spec=pltpu.PrefetchScalarGridSpec(
            num_scalar_prefetch=0 if place is None else 1,
            grid=grid,
            in_specs=[spec(b, m) for _, b, m in ins] + [pl.BlockSpec(memory_space=pl.ANY)] * len(extra),
            out_specs=[spec(b, m) for _, b, m in outs],
            scratch_shapes=list(scratch),
        ),
        out_shape=[s for s, _, _ in outs],
        compiler_params=pltpu.CompilerParams(vmem_limit_bytes=vmem << 20),
        cost_estimate=pl.CostEstimate(flops=1000, bytes_accessed=1000, transcendentals=0),
        name=name,
    )
    lead = () if place is None else (place,)
    return call(*lead, *[a for a, _, _ in ins], *extra)


def window_masks(pos0, length):
    j = lax.broadcasted_iota(jnp.int32, (BQ, 2 * BQ), 0)
    i = lax.broadcasted_iota(jnp.int32, (BQ, 2 * BQ), 1) % BQ
    near = i <= j
    key_pos = pos0 - HALF + j + jnp.where(near, 0, BQ)
    top = jnp.minimum(length, MAXLEN)
    own = j == (i + HALF) % BQ
    bias = jnp.where(((key_pos >= 0) & (key_pos < top)) | own, 0.0, NEG)
    lane = lax.broadcasted_iota(jnp.int32, (1, 2 * BQ), 1) % BQ
    last_bias = jnp.where(pos0 + HALF + lane < top, 0.0, NEG)
    return near, i == j, bias, last_bias


def split_heads(pair):
    lane = lax.broadcasted_iota(jnp.int32, pair.shape, 1)
    zero = jnp.zeros_like(pair)
    return jnp.concatenate([jnp.where(lane < HEAD_DIM, pair, zero), jnp.where(lane >= HEAD_DIM, pair, zero)], 0)


def join_heads(wide, scale=None):
    first, second = wide[:HEAD_DIM, :BQ], wide[HEAD_DIM:, BQ:]
    if scale is not None:
        first, second = first * scale[:, :BQ], second * scale[:, BQ:]
    return jnp.concatenate([first, second], 0).T


def fold(near, diag, wide):
    low = wide[BQ:]
    return jnp.where(near, wide[:BQ], low), jnp.sum(jnp.where(diag, low, 0.0), 0, keepdims=True)


def unfold(near, diag, tile, last):
    zero = jnp.zeros_like(tile)
    return jnp.concatenate(
        [jnp.where(near, tile, zero), jnp.where(near, jnp.where(diag, last, zero), tile)], 0
    ).astype(LOW)


def window_rows(before, here, after, c):
    return jnp.concatenate([before[:, c], here[:, c], after[:, c]], 0)


def attend_kernel(place, q, kb, kh, ka, vb, vh, va, out_ref, log_ref):
    blk = pl.program_id(0)
    near, diag, bias, last_bias = window_masks(place[0, blk], place[1, blk])
    for pair in range(out_ref.shape[1] // BQ):
        c = slice(pair * BQ, (pair + 1) * BQ)
        queries = split_heads(q[:, c] * 0.125)
        keyset = window_rows(kb, kh, ka, c)
        values = window_rows(vb, vh, va, c)
        scores, last = fold(near, diag, cols_dot(keyset, queries))
        scores, last = scores + bias, last + last_bias
        row_max = jnp.maximum(jnp.max(scores, 0, keepdims=True), last)
        expons, last = jnp.exp(scores - row_max), jnp.exp(last - row_max)
        summed = jnp.sum(expons, 0, keepdims=True) + last
        probs = unfold(near, diag, expons, last)
        out_ref[:, c] = join_heads(rows_dot(values, probs), 1.0 / summed).astype(LOW)
        log_ref[0, pair:pair + 1] = row_max + jnp.log(summed)


def attend_back_kernel(place, q, kb, kh, ka, vb, vh, va, g_ref, log_ref, d_ref, edge_ref, carry, tail, dq_keep):
    step = pl.program_id(0)
    steps = pl.num_programs(0)
    width = g_ref.shape[1]

    @pl.when(step == 0)
    def _():
        carry[...] = jnp.zeros_like(carry)
        tail[...] = jnp.zeros_like(tail)
        dq_keep[...] = jnp.zeros_like(dq_keep)

    d_ref[:, :width] = dq_keep[...]
    d_ref[:HALF, width:] = tail[...]

    @pl.when(step < steps - 1)
    def _():
        near, diag, bias, last_bias = window_masks(place[0, step], place[1, step])
        for pair in range(width // BQ):
            c = slice(pair * BQ, (pair + 1) * BQ)
            v = slice(width + pair * BQ, width + (pair + 1) * BQ)
            queries = split_heads(q[:, c] * 0.125)
            keyset = window_rows(kb, kh, ka, c)
            values = window_rows(vb, vh, va, c)
            grads = split_heads(g_ref[:, c])
            log_row = log_ref[0, pair:pair + 1]
            scores, last = fold(near, diag, cols_dot(keyset, queries))
            expons, last = jnp.exp(scores + (bias - log_row)), jnp.exp(last + (last_bias - log_row))
            prob_grad, last_grad = fold(near, diag, cols_dot(values, grads))
            inner = jnp.sum(expons * prob_grad, 0, keepdims=True) + last * last_grad
            score_grad = unfold(near, diag, expons * (prob_grad - inner), last * (last_grad - inner))
            probs = unfold(near, diag, expons, last)
            dq_keep[:, c] = join_heads(rows_dot(keyset, score_grad) * 0.125).astype(LOW)
            for lanes, grad in ((c, plain_dot(score_grad, queries)), (v, plain_dot(probs, grads))):
                done = (carry[:, lanes] + grad[:BQ]).astype(LOW)
                carry[:, lanes] = grad[BQ:]
                d_ref[HALF:, lanes.start + width:lanes.stop + width] = done[:HALF]
                tail[:, lanes] = done[HALF:]
                edge_ref[0, :, lanes] = jnp.where(step == 0, done[:HALF], edge_ref[0, :, lanes])

    @pl.when(step == steps - 1)
    def _():
        done = carry[...].astype(LOW)
        d_ref[HALF:, width:] = done[:HALF]
        edge_ref[1] = done[HALF:]


def window_specs(q, k, v, blocks):
    last, width = blocks - 1, k.shape[1]
    here = lambda b: (jnp.minimum(b, last), 0)
    before = lambda b: (jnp.where(b == 0, 2 * blocks, 2 * jnp.minimum(b, last) - 1), 0)
    after = lambda b: (jnp.where(b >= last, 2 * blocks + 1, 2 * b + 2), 0)
    specs = [(q, (BQ, width), here)]
    for value in (k, v):
        specs += [(value, (HALF, width), before), (value, (BQ, width), here), (value, (HALF, width), after)]
    return specs


def attend(place, q, k, v, after=()):
    blocks, width = k.shape[0] // BQ - 1, k.shape[1]
    pairs = width // BQ
    return run(
        attend_kernel, "attend", (blocks,), window_specs(q, k, v, blocks),
        [
            (shaped((blocks * BQ, width)), (BQ, width), lambda b: (b, 0)),
            (shaped((blocks, pairs, 2 * BQ), jnp.float32), (1, pairs, 2 * BQ), lambda b: (b, 0, 0)),
        ],
        after, place, flops=blocks * pairs * BQ * BQ * BQ * 256,
    )


def attend_back(place, q, k, v, grads, logs, after=()):
    blocks, width = grads.shape[0] // BQ, k.shape[1]
    pairs = width // BQ
    last = blocks - 1
    return run(
        attend_back_kernel, "attend_back", (blocks + 1,),
        window_specs(q, k, v, blocks)
        + [
            (grads, (BQ, width), lambda b: (jnp.minimum(b, last), 0)),
            (logs, (1, pairs, 2 * BQ), lambda b: (jnp.minimum(b, last), 0, 0)),
        ],
        [
            (shaped((blocks * BQ, 3 * width)), (BQ, 3 * width), lambda b: (jnp.maximum(b - 1, 0), 0)),
            (shaped((2, HALF, 2 * width)), (2, HALF, 2 * width), lambda b: (0, 0, 0)),
        ],
        after, place,
        scratch=[
            pltpu.VMEM((BQ, 2 * width), jnp.float32),
            pltpu.VMEM((HALF, 2 * width), LOW),
            pltpu.VMEM((BQ, width), LOW),
        ],
        flops=blocks * pairs * BQ * BQ * BQ * 512,
    )


def norm_kernel(tokens, before, after, gain, out):
    step, tile = pl.program_id(0), tokens.shape[0]

    @pl.when(step < pl.num_programs(0) - 1)
    def _():
        out[...] = (norm_parts(tokens[...].astype(jnp.float32))[0] * gain[...]).astype(LOW)

    @pl.when(step == pl.num_programs(0) - 1)
    def _():
        values = jnp.concatenate([before[...], after[...]], 0).astype(jnp.float32)
        out[:BQ] = (norm_parts(values)[0] * gain[...]).astype(LOW)


def norm_rows(tokens, before, after, gain):
    rows, model = tokens.shape
    tile = 3 * BQ
    blocks = rows // tile
    full = lambda i: (0, 0)
    return run(
        norm_kernel, "norm_rows", (blocks + 1,),
        [
            (tokens, (tile, model), lambda i: (jnp.minimum(i, blocks - 1), 0)),
            (before, (HALF, model), full), (after, (HALF, model), full), (gain, (1, model), full),
        ],
        [(shaped((rows + BQ, model)), (tile, model), lambda i: (i, 0))],
    )[0]


def project_kernel(normed, weights, *outs):
    for i, out in enumerate(outs):
        out[...] = plain_dot(normed[...], weights[i]).astype(LOW)


def project(normed, weights, after=()):
    rows, model = normed.shape
    width = weights.shape[2]
    tile = rows // 4 if rows % 64 == 0 else rows
    return run(
        project_kernel, "project", (rows // tile,),
        [(normed, (tile, model), lambda i: (i, 0)), (weights, (3, model, width), lambda i: (0, 0, 0))],
        [(shaped((rows, width)), (tile, width), lambda i: (i, 0))] * 3,
        after, flops=6 * rows * model * width,
    )


def project_parts_kernel(normed, mine, other, *outs):
    size = mine.shape[2]
    for i, out in enumerate(outs):
        out[:, :size] = plain_dot(normed[...], mine[i]).astype(LOW)
        out[:, size:] = plain_dot(normed[...], other[i]).astype(LOW)


def project_parts(normed, parts, after=()):
    rows, model = normed.shape
    size = parts[0].shape[2]
    tile = rows // 4
    return run(
        project_parts_kernel, "project_parts", (rows // tile,),
        [(normed, (tile, model), lambda i: (i, 0))] + [(p, (3, model, size), lambda i: (0, 0, 0)) for p in parts],
        [(shaped((rows, 2 * size)), (tile, 2 * size), lambda i: (i, 0))] * 3,
        after,
    )


def out_rows(part):
    size = part.shape[2]
    return jnp.concatenate([part[3, k * size:(k + 1) * size] for k in range(part.shape[1] // size)], 1)


def row_tile(rows):
    return 256 if rows % 256 == 0 else 128


def keep_rows(place, step, tile):
    row = lax.broadcasted_iota(jnp.int32, (BQ, 1), 0)
    parts = []
    for i in range(tile // BQ):
        b = step * (tile // BQ) + i
        parts.append(jnp.where(row + place[0, b] < place[1, b], 1.0, 0.0))
    return jnp.concatenate(parts, 0)


def mix_kernel(tokens, gain, attended, weights, *refs):
    attended_more, parts, (hidden, normed) = refs[:1], refs[1:-2], refs[-2:]
    total = tokens[...].astype(jnp.float32) + plain_dot(attended[...], weights[...])
    for side, part in enumerate(parts):
        size = part.shape[2]
        total = total + plain_dot(attended_more[0][:, side * size:(side + 1) * size], out_rows(part))
    hidden[...] = total
    normed[...] = (norm_parts(total)[0] * gain[...]).astype(LOW)


def mix(tokens, gain, attended, weights, more=None, parts=(), after=()):
    rows, model = tokens.shape
    tile = row_tile(rows)
    row, full = (lambda i: (i, 0)), (lambda i: (0, 0))
    width = weights.shape[0]
    return run(
        mix_kernel, "mix", (rows // tile,),
        [(tokens, (tile, model), row), (gain, (1, model), full), (attended, (tile, width), row), (weights, weights.shape, full)]
        + [(attended if more is None else more, (tile, width), row)]
        + [(p, p.shape, lambda i: (0, 0, 0)) for p in parts],
        [(shaped((rows, model), jnp.float32), (tile, model), row), (shaped((rows, model)), (tile, model), row)],
        after,
    )


def gelu_parts(value):
    size = jnp.abs(value)
    bell = jnp.exp(-0.5 * value * value)
    t = 1.0 / (1.0 + (0.3275911 * 2.0 ** -0.5) * size)
    series = t * (0.254829592 + t * (-0.284496736 + t * (1.421413741 + t * (-1.453152027 + t * 1.061405429))))
    tail = 0.5 * series * bell
    below = jnp.where(value < 0, tail, 1.0 - tail)
    return value * below, below + value * bell * ((2.0 * math.pi) ** -0.5)


def mlp_body(place, normed, cotangent, win, wdown, gate_ref, lift_ref):
    tile = normed.shape[0]
    kept = keep_rows(place, pl.program_id(0), tile)
    out_grad = kept * cotangent[...].astype(jnp.float32)
    out_low = out_grad.astype(LOW)
    first = cols_dot(normed[...], win[0])
    second = cols_dot(normed[...], win[1])
    gelu, slope = gelu_parts(first)
    gate = (gelu * second).astype(LOW)
    gate_ref[0] = gate
    branch = plain_dot(gate, wdown[...])
    grad = cols_dot(out_low, wdown[...])
    lift1 = (grad * second * slope).astype(LOW)
    lift2 = (grad * gelu).astype(LOW)
    lift_ref[0] = lift1
    lift_ref[1] = lift2
    pulled = plain_dot(lift1, win[0]) + plain_dot(lift2, win[1])
    return kept, out_grad, out_low, branch, pulled


def mlp_first_kernel(place, normed, cotangent, win, wdown, gate_ref, lift_ref, low_ref, branch_ref, pulled_ref):
    _, _, out_low, branch, pulled = mlp_body(place, normed, cotangent, win, wdown, gate_ref, lift_ref)
    low_ref[...] = out_low
    branch_ref[...] = branch
    pulled_ref[...] = pulled


def norm_back_rows(values, gain, grad):
    unit, rate = norm_parts(values)
    pulled = grad * gain
    mean_one = jnp.mean(pulled, -1, keepdims=True)
    mean_two = jnp.mean(pulled * unit, -1, keepdims=True)
    return rate * (pulled - mean_one - unit * mean_two), jnp.sum(grad * unit, 0, keepdims=True)


def add_gain(gain_ref, part):
    @pl.when(pl.program_id(0) == 0)
    def _():
        gain_ref[...] = jnp.zeros_like(gain_ref)

    gain_ref[...] += part


def mlp_last_kernel(fetched, place, normed, cotangent, *refs):
    if fetched:
        pieces, refs = refs[:8], refs[8:]
        win, wdown = refs[-2:]

        @pl.when(pl.program_id(0) == 0)
        def _():
            units, model = pieces[0].shape[1:]
            for part in range(4):
                rows = slice(part // 2 * units, (part // 2 + 1) * units)
                columns = pl.ds(pl.multiple_of((place[2, 1] ^ (part % 2)) * model, model), model)
                for side in range(2):
                    win[side, rows, columns] = pieces[part][side]
                wdown[rows, columns] = pieces[4 + part][0]
    else:
        (win, wdown), refs = refs[:2], refs[2:]
    hidden, gain, branch_in, pulled_in, weights = refs[:5]
    parts, refs = (refs[5:7], refs[7:]) if fetched else ((), refs[5:])
    gate_ref, lift_ref, out_ref, grad_ref, low_ref, gain_ref, attn = refs[:7]
    kept, out_grad, _, branch, pulled = mlp_body(place, normed, cotangent, win, wdown, gate_ref, lift_ref)
    out_ref[...] = (kept * (hidden[...] + (branch_in[...] + branch))).astype(LOW)
    back, gain_part = norm_back_rows(hidden[...], gain[...], pulled_in[...] + pulled)
    total = out_grad + back
    grad_ref[...] = total
    low = total.astype(LOW)
    low_ref[...] = low
    attn[...] = cols_dot(low, weights[...]).astype(LOW)
    for side, part in enumerate(parts):
        size = part.shape[2]
        refs[7][:, side * size:(side + 1) * size] = cols_dot(low, out_rows(part)).astype(LOW)
    add_gain(gain_ref, gain_part)


def mlp_specs(normed, cotangent, units):
    rows, model = normed.shape
    tile = row_tile(rows)
    row = lambda i: (i, 0)
    ins = [(normed, (tile, model), row), (cotangent, (tile, model), row)]
    outs = [
        (shaped((1, rows, units)), (1, tile, units), lambda i: (0, i, 0)),
        (shaped((2, rows, units)), (2, tile, units), lambda i: (0, i, 0)),
    ]
    return rows, model, tile, row, ins, outs


def whole(value):
    return (value, value.shape, lambda i: (0,) * value.ndim)


def mlp_first(place, normed, cotangent, win, wdown, after=()):
    rows, model, tile, row, ins, outs = mlp_specs(normed, cotangent, wdown.shape[0])
    outs = outs + [(shaped((rows, model)), (tile, model), row)]
    outs = outs + [(shaped((rows, model), jnp.float32), (tile, model), row)] * 2
    return run(mlp_first_kernel, "mlp_first", (rows // tile,), ins + [whole(win), whole(wdown)], outs, after, place)


def mlp_last(place, normed, cotangent, weights, hidden, gain, branch, pulled, w_out, parts=(), after=()):
    fetched = len(weights) == 8
    units = 2 * weights[4].shape[1] if fetched else weights[1].shape[0]
    rows, model, tile, row, ins, outs = mlp_specs(normed, cotangent, units)
    block = (tile, model)
    ins = ins + [whole(w) for w in weights]
    ins = ins + [(hidden, block, row), whole(gain), (branch, block, row), (pulled, block, row), whole(w_out)]
    ins = ins + [whole(p) for p in parts]
    outs = outs + [
        (shaped((rows, model)), block, row), (shaped((rows, model), jnp.float32), block, row),
        (shaped((rows, model)), block, row), (shaped((1, model), jnp.float32), (1, model), lambda i: (0, 0)),
    ]
    width = w_out.shape[0]
    outs = outs + [(shaped((rows, width)), (tile, width), row)] * (2 if fetched else 1)
    scratch = [pltpu.VMEM((2, units, model), LOW), pltpu.VMEM((units, model), LOW)] if fetched else []
    return run(
        functools.partial(mlp_last_kernel, fetched), "mlp_last", (rows // tile,), ins, outs, after, place, scratch, vmem=60
    )


def store_halves(value, core, keep, send, index):
    size = value.shape[0] // 2
    low, high = value[:size].astype(LOW), value[size:].astype(LOW)
    if core is None:
        keep[index], send[index] = low, high
    else:
        keep[index] = jnp.where(core == 0, low, high)
        send[index] = jnp.where(core == 0, high, low)


def outer_kernel(own, flags, left, right, keep, send):
    store_halves(rows_dot(left[0], right[...]), flags[0] if own else None, keep, send, 0)


def outer(flags, own, left, right, after=(), side=None):
    sides, rows, units = left.shape
    model = right.shape[1]
    tile = min(512, model)
    first = 0 if side is None else side
    sides = sides if side is None else 1
    out = (shaped((sides, units // 2, model)), (1, units // 2, tile), lambda s, j: (s, 0, j))
    return run(
        functools.partial(outer_kernel, own), "outer", (sides, model // tile),
        [(left, (1, rows, units), lambda s, j: (s + first, 0, 0)), (right, (rows, tile), lambda s, j: (0, j))],
        [out, out], after, flags,
    )


def outer_down_kernel(own, flags, gate, attended, low, hidden, keep, send):
    first, second = rows_dot(gate[0], low[...]), rows_dot(attended[...], hidden[...])
    core = flags[0] if own else None
    size = first.shape[0] // 2
    store_halves(first, core, keep.at[:, :size], send.at[:, :size], 0)
    store_halves(second, core, keep.at[:, size:], send.at[:, size:], 0)


def outer_down(flags, own, gate, attended, low, hidden, after=()):
    _, rows, units = gate.shape
    width, model = attended.shape[1], low.shape[1]
    tile = min(512, model)
    part = lambda j: (0, j)
    out = (shaped((1, (units + width) // 2, model)), (1, (units + width) // 2, tile), lambda j: (0, 0, j))
    return run(
        functools.partial(outer_down_kernel, own), "outer_down", (model // tile,),
        [(gate, (1, rows, units), lambda j: (0, 0, 0)), (attended, (rows, width), lambda j: (0, 0)),
         (low, (rows, tile), part), (hidden, (rows, tile), part)],
        [out, out], after, flags,
    )


def outer_attn_kernel(own, flags, normed, grads, keep, send):
    width = grads.shape[1] // 3
    size = width // 2
    for i in range(3):
        value = rows_dot(normed[...], grads[:, i * width:(i + 1) * width])
        low, high = value[:, :size].astype(LOW), value[:, size:].astype(LOW)
        if own:
            low, high = jnp.where(flags[0] == 0, low, high), jnp.where(flags[0] == 0, high, low)
        keep[i] = low
        send[i] = high


def outer_attn(flags, own, normed, grads, after=()):
    rows, width = grads.shape[0], grads.shape[1] // 3
    model = normed.shape[1]
    tile = min(512, model)
    out = (shaped((3, model, width // 2)), (3, tile, width // 2), lambda i: (0, i, 0))
    return run(
        functools.partial(outer_attn_kernel, own), "outer_attn", (model // tile,),
        [(normed, (rows, tile), lambda i: (0, i)), (grads, (rows, 3 * width), lambda i: (0, 0))],
        [out, out], after, flags,
    )


def pull_kernel(tokens, hidden_grad, gain, grads, weights, *refs):
    more, parts, (out, gain_ref) = refs[:1], refs[1:-2], refs[-2:]
    width = weights.shape[2]
    total = None
    for i in range(3):
        terms = [cols_dot(grads[:, i * width:(i + 1) * width], weights[i])]
        for side, part in enumerate(parts):
            size = part.shape[2]
            first = i * width + side * size
            terms.append(cols_dot(more[0][:, first:first + size], part[i]))
        for term in terms:
            total = term if total is None else total + term
    back, gain_part = norm_back_rows(tokens[...].astype(jnp.float32), gain[...], total)
    out[...] = hidden_grad[...] + back
    add_gain(gain_ref, gain_part)


def pull(tokens, hidden_grad, gain, grads, weights, more=None, parts=(), after=()):
    rows, model = tokens.shape
    tile = row_tile(rows)
    row = lambda i: (i, 0)
    size = grads.shape[1]
    return run(
        pull_kernel, "pull", (rows // tile,),
        [(tokens, (tile, model), row), (hidden_grad, (tile, model), row), whole(gain), (grads, (tile, size), row), whole(weights)]
        + [(grads if more is None else more, (tile, size), row)]
        + [(p, (3,) + p.shape[1:], lambda i: (0, 0, 0)) for p in parts],
        [(shaped((rows, model), jnp.float32), (tile, model), row), (shaped((1, model), jnp.float32), (1, model), lambda i: (0, 0))],
        after,
    )


def assemble_call(body, mine, other, core, outs, after):
    same = lambda i, s: (0,) * mine.ndim
    return pl.pallas_call(
        lambda *refs: body(*refs[:3], *refs[3 + len(after):]),
        grid_spec=pltpu.PrefetchScalarGridSpec(
            num_scalar_prefetch=1, grid=(2,),
            in_specs=[pl.BlockSpec(mine.shape, same)] * 2 + [pl.BlockSpec(memory_space=pl.ANY)] * len(after),
            out_specs=[
                pl.BlockSpec(block, functools.partial(lambda axis, rank, i, s: tuple((i ^ s[0]) * (d == axis) for d in range(rank)), axis, len(block)))
                for _, block, axis in outs
            ],
        ),
        out_shape=[shaped(shape, jnp.float32) for shape, _, _ in outs],
        compiler_params=pltpu.CompilerParams(vmem_limit_bytes=56 << 20),
        name="assemble",
    )(jnp.reshape(core, (1,)).astype(jnp.int32), mine, other, *after)


def assemble_kernel(side, mine, other, out):
    out[...] = jnp.where(pl.program_id(0) == 0, mine[...], other[...]).astype(jnp.float32)


def assemble(mine, other, core, axis, after=()):
    shape = tuple(2 * n if d == axis else n for d, n in enumerate(mine.shape))
    return assemble_call(assemble_kernel, mine, other, core, [(shape, mine.shape, axis)], after)[0]


def assemble_down_kernel(side, mine, other, down, out):
    chosen = jnp.where(pl.program_id(0) == 0, mine[0], other[0]).astype(jnp.float32)
    size = down.shape[0]
    down[...] = chosen[:size]
    out[...] = chosen[size:]


def assemble_down(mine, other, core, units, after=()):
    _, rows, model = mine.shape
    sizes = (units // 2, rows - units // 2)
    return assemble_call(
        assemble_down_kernel, mine, other, core, [((2 * n, model), (n, model), 0) for n in sizes], after
    )


class Links:
    def __init__(self, dp, tensor):
        self.dp, self.tensor = dp, tensor
        self.id = lax.axis_index("dp")
        self.core, self.row = self.id % 2, self.id // 2 % 2

    def send(self, value, target):
        pairs = [
            (d * self.tensor + t, to)
            for d in range(self.dp) for t in range(self.tensor)
            for to in [target(d, t)] if to is not None
        ]
        return lax.ppermute(value, AXES, pairs)

    def cross(self, value):
        return self.send(value, lambda d, t: d * self.tensor + (1 - t))

    def flip(self, value, even, odd=None):
        bits = (even, even if odd is None else odd)
        return self.send(value, lambda d, t: (d ^ bits[d % 2]) * self.tensor + t)

    def shift(self, value, by):
        return self.send(value, lambda d, t: d * self.tensor + t + by if 0 <= t + by < self.tensor else None)

    def bit_of(self, even, odd):
        return jnp.where(self.core == 0, (self.id & even) // even, (self.id & odd) // odd)


def tie(value, *others):
    return lax.optimization_barrier((value,) + others)[0]


def half(value, index, axis):
    size = value.shape[axis] // 2
    if isinstance(index, int):
        return lax.slice_in_dim(value, index * size, (index + 1) * size, axis=axis)
    return lax.dynamic_slice_in_dim(value, index * size, size, axis)


def order(bit, first, second, axis):
    return jnp.where(bit == 0, jnp.concatenate([first, second], axis), jnp.concatenate([second, first], axis))


class Summing:
    ROW_FIRST = ((2, 2, 1), (4, 4, 2), (8, 8, 3))
    SPLIT = ((2, 4, 4), (4, 8, 5), (8, 2, 6))

    def __init__(self, links, flags, axis, steps):
        self.links, self.flags, self.axis, self.steps = links, flags, axis, steps

    def cores_other(self, keep, send):
        self.keep_other, self.got_other = keep, self.links.flip(send, 1)

    def cores_own(self, keep, send):
        self.keep_own, self.got_own = keep, self.links.flip(send, 1)

    def add_other(self, *after):
        self.far = tie(self.keep_other, *after) + self.got_other
        self.crossed = self.links.cross(self.far)

    def add_own(self, *after):
        self.near = tie(self.keep_own, *after) + self.got_own

    def across(self, *after, parts=None):
        self.split(0, self.near, self.crossed if parts is None else jnp.concatenate(parts, 0), after)

    def split(self, step, a, b, after):
        even, odd, which = self.steps[step]
        a, bit = tie(a, *after), self.flags[which]
        part = lambda k: half(a, k, self.axis) + half(b, k, self.axis)
        self.held, self.moved = part(bit), self.links.flip(part(1 - bit), even, odd)

    def scatter(self, *after):
        self.split(1, self.held, self.moved, after)

    def both(self, *after):
        self.held = tie(self.held, *after) + self.moved
        self.moved = self.links.flip(self.held, *self.steps[2][:2])

    def both_add(self, *after):
        self.held = tie(self.held, *after) + self.moved
        self.moved = self.links.flip(self.held, *self.steps[1][:2])

    def gather(self, *after):
        self.held = order(self.flags[self.steps[1][2]], tie(self.held, *after), self.moved, self.axis)
        self.moved = self.links.flip(self.held, *self.steps[0][:2])

    def last(self, *after):
        self.held = order(self.flags[self.steps[0][2]], tie(self.held, *after), self.moved, self.axis)
        self.moved = self.links.flip(self.held, 1)
        return self.held, self.moved, self.links.core


def on_device(tokens, lengths, order_, gain_attn, w_qkv, w_out, gain_mlp, w_in, w_down, cotangent):
    rows, model = tokens.shape
    dp, tensor = lax.axis_size("dp"), lax.axis_size("tensor")
    tensor_id = lax.axis_index("tensor")
    links = Links(dp, tensor)
    paired = tensor == 2 and dp == 16

    slot_count = rows * tensor // MAXLEN
    my_order = lax.dynamic_slice_in_dim(order_, links.id * slot_count, slot_count, 0)
    chosen = my_order[:, None] == jnp.arange(lengths.shape[0], dtype=jnp.int32)[None, :]
    slot_len = jnp.sum(jnp.where(chosen, lengths[None, :], 0), 1)
    slots = jnp.arange(slot_count, dtype=jnp.int32)[None, :]
    block_row = tensor_id * rows + BQ * jnp.arange(rows // BQ, dtype=jnp.int32)
    block_len = jnp.sum(jnp.where((block_row // MAXLEN)[:, None] == slots, slot_len[None, :], 0), 1)
    place = jnp.stack([block_row % MAXLEN, block_len])

    w_qkv = w_qkv.transpose(1, 0, 2)
    w_in = w_in.transpose(1, 2, 0)
    gain_attn, gain_mlp = gain_attn[None], gain_mlp[None]
    if not paired:
        before, after = links.shift(tokens[rows - HALF:], 1), links.shift(tokens[:HALF], -1)
        return general(
            links, place, tokens, before, after, gain_attn, w_qkv, w_out, gain_mlp, w_in, w_down, cotangent
        )

    start = jnp.where(tensor_id == 0, rows - HALF, 0)
    border = links.cross(lax.dynamic_slice_in_dim(tokens, start, HALF, 0))
    core = links.core
    bits = [links.id // bit % 2 for bit in (1, 2, 4, 8)]
    split_bits = [jnp.where(core == 0, bits[i], bits[j]) for i, j in ((1, 2), (2, 3), (3, 1))]
    flags = jnp.stack(bits + split_bits).astype(jnp.int32)
    place = jnp.concatenate([place, jnp.pad(flags, (0, place.shape[1] - flags.shape[0]))[None]], 0)
    width, units = w_out.shape[0], w_down.shape[0]
    size = width // 2
    out_half = half(tie(w_out, border), core, 0)
    stacked = jnp.concatenate([out_half[:, k * size:(k + 1) * size] for k in range(model // size)], 0)
    piece = jnp.concatenate([half(tie(w_qkv, border), core, 2), stacked[None]], 0)
    attn_direct = links.cross(piece)

    normed = norm_rows(tokens, border, border, gain_attn)
    quarter = lambda w, a, b: half(half(w, core, a), bits[1], b)
    in_direct = links.cross(quarter(tie(w_in, normed), 1, 2))
    down_direct = links.cross(quarter(tie(w_down, normed)[None], 1, 2))
    q0, k0, v0 = project(normed, w_qkv)
    attended0, logs0 = attend(place, q0, k0, v0)
    attn_parts = (attn_direct, links.flip(tie(attn_direct, attended0), 1))
    q1, k1, v1 = project_parts(normed, attn_parts, after=[attended0])
    attended1, logs1 = attend(place, q1, k1, v1)
    in_direct = tie(in_direct, attended1)
    in_relayed = links.flip(in_direct, 2)
    in_core = links.flip(in_direct, 1)
    hidden, normed_mlp = mix(tokens, gain_mlp, attended0, w_out, attended1, attn_parts, after=[in_direct])
    gate0, lift0, out_low, branch, pulled = mlp_first(place, normed_mlp, cotangent, w_in, w_down, after=[in_core])
    down_direct = tie(down_direct, hidden)
    down_relayed = links.flip(down_direct, 2)
    down_core = links.flip(down_direct, 1)
    in_relayed = tie(in_relayed, branch)
    down_relayed = tie(down_relayed, in_relayed)
    weights = (
        in_direct, in_relayed, in_core, links.flip(in_relayed, 1),
        down_direct, down_relayed, down_core, links.flip(down_relayed, 1),
    )
    gate1, lift1, output, hidden_grad, hidden_low, gain_mlp_grad, back0, back1 = mlp_last(
        place, normed_mlp, cotangent, weights, hidden, gain_mlp, branch, pulled, w_out, attn_parts
    )
    inner = Summing(links, flags, 2, Summing.ROW_FIRST)
    inner_a, inner_b = (Summing(links, flags, 2, Summing.ROW_FIRST) for _ in range(2))
    down = Summing(links, flags, 2, Summing.SPLIT)
    attn = Summing(links, flags, 1, Summing.SPLIT)

    inner_a.cores_other(*outer(flags, False, lift1, normed_mlp, after=[back1], side=0))
    inner_b.cores_other(*outer(flags, False, lift1, normed_mlp, after=[inner_a.keep_other], side=1))
    inner_a.add_other(inner_b.keep_other)
    inner.cores_own(*outer(flags, True, lift0, normed_mlp, after=[inner_a.far]))
    inner_b.add_other(inner.keep_own)
    d1, edge1 = attend_back(place, q1, k1, v1, back1, logs1, after=[inner_b.far])
    inner.add_own(d1, inner_a.crossed)
    down.cores_other(*outer_down(flags, False, gate1, attended1, out_low, hidden_low, after=[inner.near]))
    d0, edge0 = attend_back(place, q0, k0, v0, back0, logs0, after=[down.keep_other])
    down.add_other(d0)
    inner.across(down.far, parts=[inner_a.crossed, inner_b.crossed])

    swap = lambda e: jnp.where(core == 0, e, jnp.concatenate([e[:, size:], e[:, :size]], 1))
    edge_out = lambda e: jnp.concatenate([swap(e[:, :width]), swap(e[:, width:])], 1)
    edges = jnp.stack([edge_out(jnp.where(tensor_id == 0, e[1], e[0])) for e in (edge1, edge0)])
    edges = links.cross(edges)

    def add_edge(d, edge):
        held = lax.dynamic_slice(d, (start, width), (HALF, 2 * width))
        return lax.dynamic_update_slice(d, held + edge, (start, width))

    d1, d0 = add_edge(d1, edges[1]), add_edge(d0, edges[0])
    attn.cores_other(*outer_attn(flags, False, normed, d1, after=[inner.held]))
    attn.cores_own(*outer_attn(flags, True, normed, d0, after=[attn.keep_other]))
    attn.add_other(attn.keep_own)
    down.cores_own(*outer_down(flags, True, gate0, attended0, out_low, hidden_low, after=[attn.far]))
    inner.scatter(down.keep_own)
    attn.add_own(inner.held)
    down.add_own(attn.near)
    input_grad, gain_attn_grad = pull(
        tokens, hidden_grad, gain_attn, d0, w_qkv, d1, attn_parts, after=[down.near, inner.held]
    )
    inner.both(input_grad)
    down.across(inner.held)
    gain_total = jnp.concatenate((gain_attn_grad, gain_mlp_grad))
    gain_total = gain_total + tie(links.cross(gain_total), down.held)
    attn.across(down.held, gain_total)
    down.scatter(attn.held)
    gain_total = gain_total + tie(links.flip(gain_total, 1), down.held)
    inner.both_add(down.held)
    attn.scatter(inner.held, gain_total)
    gain_total = gain_total + tie(links.flip(gain_total, 2), attn.held)
    down.both(attn.held)
    inner.gather(down.held)
    attn.both(inner.held, gain_total)
    gain_total = gain_total + tie(links.flip(gain_total, 4), attn.held)
    down.both_add(attn.held)
    grads_in = inner.last(down.held)
    attn.both_add(grads_in[0], gain_total)
    gain_total = gain_total + tie(links.flip(gain_total, 8), attn.held)
    down.gather(attn.held)
    grad_w_in = assemble(*grads_in, 1, after=[down.held])
    attn.gather(grad_w_in, gain_total)
    grads_down = down.last(attn.held)
    grads_attn = attn.last(grads_down[0])
    grad_w_down, grad_w_out = assemble_down(*grads_down, units, after=[grads_attn[0]])
    grad_w_qkv = assemble(*grads_attn, 2, after=[grad_w_down])
    return (
        output,
        input_grad,
        gain_total[0],
        grad_w_qkv.transpose(1, 0, 2),
        grad_w_out,
        gain_total[1],
        grad_w_in.transpose(2, 0, 1),
        grad_w_down,
    )


def general(links, place, tokens, before, after, gain_attn, w_qkv, w_out, gain_mlp, w_in, w_down, cotangent):
    rows = tokens.shape[0]
    w_qkv, w_out, w_in, w_down = (
        lax.all_gather(w, "tensor", axis=axis, tiled=True)
        for w, axis in ((w_qkv, 2), (w_out, 0), (w_in, 1), (w_down, 0))
    )
    normed = norm_rows(tokens, before, after, gain_attn)
    q, k, v = project(normed, w_qkv)
    attended, logs = attend(place, q, k, v)
    hidden, normed_mlp = mix(tokens, gain_mlp, attended, w_out)
    blank = jnp.zeros_like(hidden)
    gate, lift, output, hidden_grad, hidden_low, gain_mlp_grad, back = mlp_last(
        place, normed_mlp, cotangent, (w_in, w_down), hidden, gain_mlp, blank, blank, w_out
    )
    position = jnp.repeat(place[0], BQ) + jnp.tile(jnp.arange(BQ, dtype=jnp.int32), place.shape[1])
    out_low = jnp.where((position < jnp.repeat(place[1], BQ))[:, None], cotangent, jnp.zeros_like(cotangent))
    flags = jnp.zeros((1,), jnp.int32)
    units, width = w_down.shape[0], w_out.shape[0]
    low, high = outer_down(flags, False, gate, attended, out_low, hidden_low)
    down = jnp.concatenate([low[0, :units // 2], high[0, :units // 2]], 0)
    out = jnp.concatenate([low[0, units // 2:], high[0, units // 2:]], 0)
    inner = jnp.concatenate(outer(flags, False, lift, normed_mlp), 1)
    d, edge = attend_back(place, q, k, v, back, logs)
    d = d.at[:HALF, width:].add(links.shift(edge[1], 1)).at[rows - HALF:, width:].add(links.shift(edge[0], -1))
    qkv = jnp.concatenate(outer_attn(flags, False, normed, d), 2)
    input_grad, gain_attn_grad = pull(tokens, hidden_grad, gain_attn, d, w_qkv)
    down, inner, out, qkv = (
        lax.psum(lax.psum_scatter(g, "tensor", scatter_dimension=axis, tiled=True), "dp").astype(jnp.float32)
        for g, axis in ((down, 0), (inner, 1), (out, 0), (qkv, 2))
    )
    gain_total = lax.psum(jnp.concatenate((gain_attn_grad, gain_mlp_grad)), AXES)
    return (
        output, input_grad, gain_total[0], qkv.transpose(1, 0, 2), out, gain_total[1],
        inner.transpose(2, 0, 1), down,
    )


def solution(mesh):
    split = P(AXES, None)
    wide = P(None, None, "tensor")
    tall = P("tensor", None)
    return jax.shard_map(
        on_device,
        mesh=mesh,
        in_specs=(split, P(), P(), P(), wide, tall, P(), wide, tall, split),
        out_specs=(split, split, P(), wide, tall, P(), wide, tall),
        check_vma=False,
    )
```

```python
import functools
import math

import jax
import jax.numpy as jnp
from jax import lax
from jax.experimental import pallas as pl
from jax.experimental.pallas import tpu as pltpu
from jax.sharding import PartitionSpec as P

AXES = ("dp", "tensor")
EPS = 1e-05
HEAD_DIM = 64
HALF = 64
MAXLEN = 1024
BQ = 128
LOW = jnp.bfloat16
NEG = -1e30


def cols_dot(left, right):
    return lax.dot_general(left, right, (((1,), (1,)), ((), ())), preferred_element_type=jnp.float32)


def rows_dot(left, right):
    return lax.dot_general(left, right, (((0,), (0,)), ((), ())), preferred_element_type=jnp.float32)


def plain_dot(left, right):
    return lax.dot_general(left, right, (((1,), (0,)), ((), ())), preferred_element_type=jnp.float32)


def norm_parts(values):
    center = values - jnp.mean(values, -1, keepdims=True)
    rate = lax.rsqrt(jnp.mean(center * center, -1, keepdims=True) + EPS)
    return center * rate, rate


COST = {
    "norm_rows": 6, "project": 9, "project_parts": 9, "attend": 20, "mix": 11, "mlp_first": 39, "mlp_last": 49, "outer": 9,
    "attend_back": 25, "trade_outer": 9, "trade_down": 12, "trade_attn": 10, "outer_down": 12, "outer_attn": 10, "pull": 18,
}
SCALE = 100


def shaped(shape, dtype=LOW):
    return jax.ShapeDtypeStruct(shape, dtype)


def run(body, name, grid, ins, outs, after=(), place=None, scratch=(), flops=0, vmem=56, seen=False, collective=None):
    extra = [a for a in after if a is not None]
    count = len(ins)

    def kernel(*refs):
        lead = refs[:1] if place is not None else ()
        refs = refs[len(lead):]
        body(*lead, *refs[:count], *refs[count + len(extra):])

    def spec(block, index):
        if place is not None and not seen:
            return pl.BlockSpec(block, lambda *a: index(*a[:-1]))
        return pl.BlockSpec(block, index)

    call = pl.pallas_call(
        kernel,
        grid_spec=pltpu.PrefetchScalarGridSpec(
            num_scalar_prefetch=0 if place is None else 1,
            grid=grid,
            in_specs=[spec(b, m) for _, b, m in ins] + [pl.BlockSpec(memory_space=pl.ANY)] * len(extra),
            out_specs=[spec(b, m) for _, b, m in outs],
            scratch_shapes=list(scratch),
        ),
        out_shape=[s for s, _, _ in outs],
        compiler_params=pltpu.CompilerParams(
            vmem_limit_bytes=vmem << 20, collective_id=collective, has_side_effects=collective is not None
        ),
        cost_estimate=pl.CostEstimate(flops=int(COST[name] * SCALE), bytes_accessed=1000, transcendentals=0),
        name=name,
    )
    lead = () if place is None else (place,)
    return call(*lead, *[a for a, _, _ in ins], *extra)


def window_masks(pos0, length):
    j = lax.broadcasted_iota(jnp.int32, (BQ, 2 * BQ), 0)
    i = lax.broadcasted_iota(jnp.int32, (BQ, 2 * BQ), 1) % BQ
    near = i <= j
    key_pos = pos0 - HALF + j + jnp.where(near, 0, BQ)
    top = jnp.minimum(length, MAXLEN)
    own = j == (i + HALF) % BQ
    bias = jnp.where(((key_pos >= 0) & (key_pos < top)) | own, 0.0, NEG)
    lane = lax.broadcasted_iota(jnp.int32, (1, 2 * BQ), 1) % BQ
    last_bias = jnp.where(pos0 + HALF + lane < top, 0.0, NEG)
    return near, i == j, bias, last_bias


def split_heads(pair):
    lane = lax.broadcasted_iota(jnp.int32, pair.shape, 1)
    zero = jnp.zeros_like(pair)
    return jnp.concatenate([jnp.where(lane < HEAD_DIM, pair, zero), jnp.where(lane >= HEAD_DIM, pair, zero)], 0)


def join_heads(wide, scale=None):
    first, second = wide[:HEAD_DIM, :BQ], wide[HEAD_DIM:, BQ:]
    if scale is not None:
        first, second = first * scale[:, :BQ], second * scale[:, BQ:]
    return jnp.concatenate([first, second], 0).T


def fold(near, diag, wide):
    low = wide[BQ:]
    return jnp.where(near, wide[:BQ], low), jnp.sum(jnp.where(diag, low, 0.0), 0, keepdims=True)


def unfold(near, diag, tile, last):
    zero = jnp.zeros_like(tile)
    return jnp.concatenate(
        [jnp.where(near, tile, zero), jnp.where(near, jnp.where(diag, last, zero), tile)], 0
    ).astype(LOW)


def window_rows(before, here, after, c):
    return jnp.concatenate([before[:, c], here[:, c], after[:, c]], 0)


def attend_kernel(place, q, kb, kh, ka, vb, vh, va, out_ref, log_ref):
    blk = pl.program_id(0)
    near, diag, bias, last_bias = window_masks(place[0, blk], place[1, blk])
    for pair in range(out_ref.shape[1] // BQ):
        c = slice(pair * BQ, (pair + 1) * BQ)
        queries = split_heads(q[:, c] * 0.125)
        keyset = window_rows(kb, kh, ka, c)
        values = window_rows(vb, vh, va, c)
        scores, last = fold(near, diag, cols_dot(keyset, queries))
        scores, last = scores + bias, last + last_bias
        row_max = jnp.maximum(jnp.max(scores, 0, keepdims=True), last)
        expons, last = jnp.exp(scores - row_max), jnp.exp(last - row_max)
        summed = jnp.sum(expons, 0, keepdims=True) + last
        probs = unfold(near, diag, expons, last)
        out_ref[:, c] = join_heads(rows_dot(values, probs), 1.0 / summed).astype(LOW)
        log_ref[0, pair:pair + 1] = row_max + jnp.log(summed)


def attend_back_kernel(place, q, kb, kh, ka, vb, vh, va, g_ref, log_ref, d_ref, edge_ref, carry, tail, dq_keep):
    step = pl.program_id(0)
    steps = pl.num_programs(0)
    width = g_ref.shape[1]

    @pl.when(step == 0)
    def _():
        carry[...] = jnp.zeros_like(carry)
        tail[...] = jnp.zeros_like(tail)
        dq_keep[...] = jnp.zeros_like(dq_keep)

    d_ref[:, :width] = dq_keep[...]
    d_ref[:HALF, width:] = tail[...]

    @pl.when(step < steps - 1)
    def _():
        near, diag, bias, last_bias = window_masks(place[0, step], place[1, step])
        for pair in range(width // BQ):
            c = slice(pair * BQ, (pair + 1) * BQ)
            v = slice(width + pair * BQ, width + (pair + 1) * BQ)
            queries = split_heads(q[:, c] * 0.125)
            keyset = window_rows(kb, kh, ka, c)
            values = window_rows(vb, vh, va, c)
            grads = split_heads(g_ref[:, c])
            log_row = log_ref[0, pair:pair + 1]
            scores, last = fold(near, diag, cols_dot(keyset, queries))
            expons, last = jnp.exp(scores + (bias - log_row)), jnp.exp(last + (last_bias - log_row))
            prob_grad, last_grad = fold(near, diag, cols_dot(values, grads))
            inner = jnp.sum(expons * prob_grad, 0, keepdims=True) + last * last_grad
            score_grad = unfold(near, diag, expons * (prob_grad - inner), last * (last_grad - inner))
            probs = unfold(near, diag, expons, last)
            dq_keep[:, c] = join_heads(rows_dot(keyset, score_grad) * 0.125).astype(LOW)
            for lanes, grad in ((c, plain_dot(score_grad, queries)), (v, plain_dot(probs, grads))):
                done = (carry[:, lanes] + grad[:BQ]).astype(LOW)
                carry[:, lanes] = grad[BQ:]
                d_ref[HALF:, lanes.start + width:lanes.stop + width] = done[:HALF]
                tail[:, lanes] = done[HALF:]
                edge_ref[0, :, lanes] = jnp.where(step == 0, done[:HALF], edge_ref[0, :, lanes])

    @pl.when(step == steps - 1)
    def _():
        done = carry[...].astype(LOW)
        d_ref[HALF:, width:] = done[:HALF]
        edge_ref[1] = done[HALF:]


def window_specs(q, k, v, blocks):
    last, width = blocks - 1, k.shape[1]
    here = lambda b: (jnp.minimum(b, last), 0)
    before = lambda b: (jnp.where(b == 0, 2 * blocks, 2 * jnp.minimum(b, last) - 1), 0)
    after = lambda b: (jnp.where(b >= last, 2 * blocks + 1, 2 * b + 2), 0)
    specs = [(q, (BQ, width), here)]
    for value in (k, v):
        specs += [(value, (HALF, width), before), (value, (BQ, width), here), (value, (HALF, width), after)]
    return specs


def attend(place, q, k, v, after=()):
    blocks, width = k.shape[0] // BQ - 1, k.shape[1]
    pairs = width // BQ
    return run(
        attend_kernel, "attend", (blocks,), window_specs(q, k, v, blocks),
        [
            (shaped((blocks * BQ, width)), (BQ, width), lambda b: (b, 0)),
            (shaped((blocks, pairs, 2 * BQ), jnp.float32), (1, pairs, 2 * BQ), lambda b: (b, 0, 0)),
        ],
        after, place, flops=blocks * pairs * BQ * BQ * BQ * 256,
    )


def attend_back(place, q, k, v, grads, logs, after=()):
    blocks, width = grads.shape[0] // BQ, k.shape[1]
    pairs = width // BQ
    last = blocks - 1
    return run(
        attend_back_kernel, "attend_back", (blocks + 1,),
        window_specs(q, k, v, blocks)
        + [
            (grads, (BQ, width), lambda b: (jnp.minimum(b, last), 0)),
            (logs, (1, pairs, 2 * BQ), lambda b: (jnp.minimum(b, last), 0, 0)),
        ],
        [
            (shaped((blocks * BQ, 3 * width)), (BQ, 3 * width), lambda b: (jnp.maximum(b - 1, 0), 0)),
            (shaped((2, HALF, 2 * width)), (2, HALF, 2 * width), lambda b: (0, 0, 0)),
        ],
        after, place,
        scratch=[
            pltpu.VMEM((BQ, 2 * width), jnp.float32),
            pltpu.VMEM((HALF, 2 * width), LOW),
            pltpu.VMEM((BQ, width), LOW),
        ],
        flops=blocks * pairs * BQ * BQ * BQ * 512,
    )


def norm_kernel(tokens, before, after, gain, out):
    step, tile = pl.program_id(0), tokens.shape[0]

    @pl.when(step < pl.num_programs(0) - 1)
    def _():
        out[...] = (norm_parts(tokens[...].astype(jnp.float32))[0] * gain[...]).astype(LOW)

    @pl.when(step == pl.num_programs(0) - 1)
    def _():
        values = jnp.concatenate([before[...], after[...]], 0).astype(jnp.float32)
        out[:BQ] = (norm_parts(values)[0] * gain[...]).astype(LOW)


def norm_rows(tokens, before, after, gain):
    rows, model = tokens.shape
    tile = 3 * BQ
    blocks = rows // tile
    full = lambda i: (0, 0)
    return run(
        norm_kernel, "norm_rows", (blocks + 1,),
        [
            (tokens, (tile, model), lambda i: (jnp.minimum(i, blocks - 1), 0)),
            (before, (HALF, model), full), (after, (HALF, model), full), (gain, (1, model), full),
        ],
        [(shaped((rows + BQ, model)), (tile, model), lambda i: (i, 0))],
    )[0]


def project_kernel(normed, weights, *outs):
    for i, out in enumerate(outs):
        out[...] = plain_dot(normed[...], weights[i]).astype(LOW)


def project(normed, weights, after=()):
    rows, model = normed.shape
    width = weights.shape[2]
    tile = rows // 4 if rows % 64 == 0 else rows
    return run(
        project_kernel, "project", (rows // tile,),
        [(normed, (tile, model), lambda i: (i, 0)), (weights, (3, model, width), lambda i: (0, 0, 0))],
        [(shaped((rows, width)), (tile, width), lambda i: (i, 0))] * 3,
        after, flops=6 * rows * model * width,
    )


def project_parts_kernel(normed, mine, other, *outs):
    size = mine.shape[2]
    for i, out in enumerate(outs):
        out[:, :size] = plain_dot(normed[...], mine[i]).astype(LOW)
        out[:, size:] = plain_dot(normed[...], other[i]).astype(LOW)


def project_parts(normed, parts, after=()):
    rows, model = normed.shape
    size = parts[0].shape[2]
    tile = rows // 4
    return run(
        project_parts_kernel, "project_parts", (rows // tile,),
        [(normed, (tile, model), lambda i: (i, 0))] + [(p, (3, model, size), lambda i: (0, 0, 0)) for p in parts],
        [(shaped((rows, 2 * size)), (tile, 2 * size), lambda i: (i, 0))] * 3,
        after,
    )


def out_rows(part):
    size = part.shape[2]
    return jnp.concatenate([part[3, k * size:(k + 1) * size] for k in range(part.shape[1] // size)], 1)


def row_tile(rows):
    return 256 if rows % 256 == 0 else 128


def keep_rows(place, step, tile):
    row = lax.broadcasted_iota(jnp.int32, (BQ, 1), 0)
    parts = []
    for i in range(tile // BQ):
        b = step * (tile // BQ) + i
        parts.append(jnp.where(row + place[0, b] < place[1, b], 1.0, 0.0))
    return jnp.concatenate(parts, 0)


def mix_kernel(tokens, gain, attended, weights, *refs):
    attended_more, parts, (hidden, normed) = refs[:1], refs[1:-2], refs[-2:]
    total = tokens[...].astype(jnp.float32) + plain_dot(attended[...], weights[...])
    for side, part in enumerate(parts):
        size = part.shape[2]
        total = total + plain_dot(attended_more[0][:, side * size:(side + 1) * size], out_rows(part))
    hidden[...] = total
    normed[...] = (norm_parts(total)[0] * gain[...]).astype(LOW)


def mix(tokens, gain, attended, weights, more=None, parts=(), after=()):
    rows, model = tokens.shape
    tile = row_tile(rows)
    row, full = (lambda i: (i, 0)), (lambda i: (0, 0))
    width = weights.shape[0]
    return run(
        mix_kernel, "mix", (rows // tile,),
        [(tokens, (tile, model), row), (gain, (1, model), full), (attended, (tile, width), row), (weights, weights.shape, full)]
        + [(attended if more is None else more, (tile, width), row)]
        + [(p, p.shape, lambda i: (0, 0, 0)) for p in parts],
        [(shaped((rows, model), jnp.float32), (tile, model), row), (shaped((rows, model)), (tile, model), row)],
        after,
    )


def gelu_parts(value):
    size = jnp.abs(value)
    bell = jnp.exp(-0.5 * value * value)
    t = 1.0 / (1.0 + (0.3275911 * 2.0 ** -0.5) * size)
    series = t * (0.254829592 + t * (-0.284496736 + t * (1.421413741 + t * (-1.453152027 + t * 1.061405429))))
    tail = 0.5 * series * bell
    below = jnp.where(value < 0, tail, 1.0 - tail)
    return value * below, below + value * bell * ((2.0 * math.pi) ** -0.5)


def mlp_body(place, normed, cotangent, win, wdown, gate_ref, lift_ref):
    tile = normed.shape[0]
    kept = keep_rows(place, pl.program_id(0), tile)
    out_grad = kept * cotangent[...].astype(jnp.float32)
    out_low = out_grad.astype(LOW)
    first = cols_dot(normed[...], win[0])
    second = cols_dot(normed[...], win[1])
    gelu, slope = gelu_parts(first)
    gate = (gelu * second).astype(LOW)
    gate_ref[0] = gate
    branch = plain_dot(gate, wdown[...])
    grad = cols_dot(out_low, wdown[...])
    lift1 = (grad * second * slope).astype(LOW)
    lift2 = (grad * gelu).astype(LOW)
    lift_ref[0] = lift1
    lift_ref[1] = lift2
    pulled = plain_dot(lift1, win[0]) + plain_dot(lift2, win[1])
    return kept, out_grad, out_low, branch, pulled


def mlp_first_kernel(place, normed, cotangent, win, wdown, gate_ref, lift_ref, low_ref, branch_ref, pulled_ref):
    _, _, out_low, branch, pulled = mlp_body(place, normed, cotangent, win, wdown, gate_ref, lift_ref)
    low_ref[...] = out_low
    branch_ref[...] = branch
    pulled_ref[...] = pulled


def norm_back_rows(values, gain, grad):
    unit, rate = norm_parts(values)
    pulled = grad * gain
    mean_one = jnp.mean(pulled, -1, keepdims=True)
    mean_two = jnp.mean(pulled * unit, -1, keepdims=True)
    return rate * (pulled - mean_one - unit * mean_two), jnp.sum(grad * unit, 0, keepdims=True)


def add_gain(gain_ref, part):
    @pl.when(pl.program_id(0) == 0)
    def _():
        gain_ref[...] = jnp.zeros_like(gain_ref)

    gain_ref[...] += part


def mlp_last_kernel(fetched, place, normed, cotangent, *refs):
    if fetched:
        pieces, refs = refs[:8], refs[8:]
        win, wdown = refs[-2:]

        @pl.when(pl.program_id(0) == 0)
        def _():
            units, model = pieces[0].shape[1:]
            for part in range(4):
                rows = slice(part // 2 * units, (part // 2 + 1) * units)
                columns = pl.ds(pl.multiple_of((place[2, 1] ^ (part % 2)) * model, model), model)
                for side in range(2):
                    win[side, rows, columns] = pieces[part][side]
                wdown[rows, columns] = pieces[4 + part][0]
    else:
        (win, wdown), refs = refs[:2], refs[2:]
    hidden, gain, branch_in, pulled_in, weights = refs[:5]
    parts, refs = (refs[5:7], refs[7:]) if fetched else ((), refs[5:])
    gate_ref, lift_ref, out_ref, grad_ref, low_ref, gain_ref, attn = refs[:7]
    kept, out_grad, _, branch, pulled = mlp_body(place, normed, cotangent, win, wdown, gate_ref, lift_ref)
    out_ref[...] = (kept * (hidden[...] + (branch_in[...] + branch))).astype(LOW)
    back, gain_part = norm_back_rows(hidden[...], gain[...], pulled_in[...] + pulled)
    total = out_grad + back
    grad_ref[...] = total
    low = total.astype(LOW)
    low_ref[...] = low
    attn[...] = cols_dot(low, weights[...]).astype(LOW)
    for side, part in enumerate(parts):
        size = part.shape[2]
        refs[7][:, side * size:(side + 1) * size] = cols_dot(low, out_rows(part)).astype(LOW)
    add_gain(gain_ref, gain_part)


def mlp_specs(normed, cotangent, units):
    rows, model = normed.shape
    tile = row_tile(rows)
    row = lambda i: (i, 0)
    ins = [(normed, (tile, model), row), (cotangent, (tile, model), row)]
    outs = [
        (shaped((1, rows, units)), (1, tile, units), lambda i: (0, i, 0)),
        (shaped((2, rows, units)), (2, tile, units), lambda i: (0, i, 0)),
    ]
    return rows, model, tile, row, ins, outs


def whole(value):
    return (value, value.shape, lambda i: (0,) * value.ndim)


def mlp_first(place, normed, cotangent, win, wdown, after=()):
    rows, model, tile, row, ins, outs = mlp_specs(normed, cotangent, wdown.shape[0])
    outs = outs + [(shaped((rows, model)), (tile, model), row)]
    outs = outs + [(shaped((rows, model), jnp.float32), (tile, model), row)] * 2
    return run(mlp_first_kernel, "mlp_first", (rows // tile,), ins + [whole(win), whole(wdown)], outs, after, place)


def mlp_last(place, normed, cotangent, weights, hidden, gain, branch, pulled, w_out, parts=(), after=()):
    fetched = len(weights) == 8
    units = 2 * weights[4].shape[1] if fetched else weights[1].shape[0]
    rows, model, tile, row, ins, outs = mlp_specs(normed, cotangent, units)
    block = (tile, model)
    ins = ins + [whole(w) for w in weights]
    ins = ins + [(hidden, block, row), whole(gain), (branch, block, row), (pulled, block, row), whole(w_out)]
    ins = ins + [whole(p) for p in parts]
    outs = outs + [
        (shaped((rows, model)), block, row), (shaped((rows, model), jnp.float32), block, row),
        (shaped((rows, model)), block, row), (shaped((1, model), jnp.float32), (1, model), lambda i: (0, 0)),
    ]
    width = w_out.shape[0]
    outs = outs + [(shaped((rows, width)), (tile, width), row)] * (2 if fetched else 1)
    scratch = [pltpu.VMEM((2, units, model), LOW), pltpu.VMEM((units, model), LOW)] if fetched else []
    return run(
        functools.partial(mlp_last_kernel, fetched), "mlp_last", (rows // tile,), ins, outs, after, place, scratch, vmem=60
    )


def store_halves(value, core, keep, send, index):
    size = value.shape[0] // 2
    low, high = value[:size].astype(LOW), value[size:].astype(LOW)
    if core is None:
        keep[index], send[index] = low, high
    else:
        keep[index] = jnp.where(core == 0, low, high)
        send[index] = jnp.where(core == 0, high, low)


def outer_kernel(own, flags, left, right, keep, send):
    store_halves(rows_dot(left[0], right[...]), flags[0] if own else None, keep, send, 0)


def outer(flags, own, left, right, after=(), side=None):
    sides, rows, units = left.shape
    model = right.shape[1]
    tile = min(512, model)
    first = 0 if side is None else side
    sides = sides if side is None else 1
    out = (shaped((sides, units // 2, model)), (1, units // 2, tile), lambda s, j: (s, 0, j))
    return run(
        functools.partial(outer_kernel, own), "outer", (sides, model // tile),
        [(left, (1, rows, units), lambda s, j: (s + first, 0, 0)), (right, (rows, tile), lambda s, j: (0, j))],
        [out, out], after, flags,
    )


def outer_down_kernel(own, flags, gate, attended, low, hidden, keep, send):
    first, second = rows_dot(gate[0], low[...]), rows_dot(attended[...], hidden[...])
    core = flags[0] if own else None
    size = first.shape[0] // 2
    store_halves(first, core, keep.at[:, :size], send.at[:, :size], 0)
    store_halves(second, core, keep.at[:, size:], send.at[:, size:], 0)


def outer_down(flags, own, gate, attended, low, hidden, after=()):
    _, rows, units = gate.shape
    width, model = attended.shape[1], low.shape[1]
    tile = min(512, model)
    part = lambda j: (0, j)
    out = (shaped((1, (units + width) // 2, model)), (1, (units + width) // 2, tile), lambda j: (0, 0, j))
    return run(
        functools.partial(outer_down_kernel, own), "outer_down", (model // tile,),
        [(gate, (1, rows, units), lambda j: (0, 0, 0)), (attended, (rows, width), lambda j: (0, 0)),
         (low, (rows, tile), part), (hidden, (rows, tile), part)],
        [out, out], after, flags,
    )


def outer_attn_kernel(own, flags, normed, grads, keep, send):
    width = grads.shape[1] // 3
    size = width // 2
    for i in range(3):
        value = rows_dot(normed[...], grads[:, i * width:(i + 1) * width])
        low, high = value[:, :size].astype(LOW), value[:, size:].astype(LOW)
        if own:
            low, high = jnp.where(flags[0] == 0, low, high), jnp.where(flags[0] == 0, high, low)
        keep[i] = low
        send[i] = high


def outer_attn(flags, own, normed, grads, after=()):
    rows, width = grads.shape[0], grads.shape[1] // 3
    model = normed.shape[1]
    tile = min(512, model)
    out = (shaped((3, model, width // 2)), (3, tile, width // 2), lambda i: (0, i, 0))
    return run(
        functools.partial(outer_attn_kernel, own), "outer_attn", (model // tile,),
        [(normed, (rows, tile), lambda i: (0, i)), (grads, (rows, 3 * width), lambda i: (0, 0))],
        [out, out], after, flags,
    )


def trade_kernel(tiles, compute, store, *refs):
    ins, out = refs[:-6], refs[-6]
    keep, send, got, send_sems, got_sems = refs[-5:]
    step = pl.program_id(0)
    me = lax.axis_index("dp")
    other = {"dp": me + 1 - 2 * (me % 2)}

    @pl.when(step == 0)
    def _():
        barrier = pltpu.get_barrier_semaphore()
        pl.semaphore_signal(barrier, inc=1, device_id=other, device_id_type=pl.DeviceIdType.MESH)
        pl.semaphore_wait(barrier, 1)

    def move(tile):
        return pltpu.make_async_remote_copy(
            src_ref=send.at[tile], dst_ref=got.at[tile], send_sem=send_sems.at[tile], recv_sem=got_sems.at[tile],
            device_id=other, device_id_type=pl.DeviceIdType.MESH,
        )

    compute(me % 2, ins, keep.at[step], send.at[step])
    move(step).start()

    @pl.when(step == tiles - 1)
    def _():
        for tile in range(tiles):
            move(tile).wait()
            store(out, tile, keep[tile] + got[tile])


def trade(name, collective, tiles, tile_shape, compute, store, ins, shape, after=()):
    buffer = pltpu.VMEM((tiles,) + tile_shape, LOW)
    return run(
        functools.partial(trade_kernel, tiles, compute, store), name, (tiles,), ins,
        [(shaped(shape), shape, lambda t: (0,) * len(shape))], after,
        scratch=[buffer, buffer, buffer, pltpu.SemaphoreType.DMA((tiles,)), pltpu.SemaphoreType.DMA((tiles,))],
        collective=collective,
    )[0]


def keep_and_send(own, core, value, axis, keep, send, index):
    size = value.shape[axis] // 2
    low = lax.slice_in_dim(value, 0, size, axis=axis).astype(LOW)
    high = lax.slice_in_dim(value, size, 2 * size, axis=axis).astype(LOW)
    if own:
        low, high = jnp.where(core == 0, low, high), jnp.where(core == 0, high, low)
    keep[index] = low
    send[index] = high


def store_columns(count, out, tile, value):
    size = value.shape[-1]
    out[tile // count, :, tile % count * size:(tile % count + 1) * size] = value


def trade_outer(collective, own, left, right, sides, after=()):
    _, rows, units = left.shape
    model = right.shape[1]
    tile, count = min(512, model), model // min(512, model)
    first = sides[0]

    def compute(core, ins, keep, send):
        keep_and_send(own, core, rows_dot(ins[0][0], ins[1][...]), 0, keep, send, slice(None))

    return trade(
        "trade_outer", collective, len(sides) * count, (units // 2, tile), compute, functools.partial(store_columns, count),
        [(left, (1, rows, units), lambda t: (first + t // count, 0, 0)), (right, (rows, tile), lambda t: (0, t % count))],
        (len(sides), units // 2, model), after,
    )


def trade_down(collective, own, gate, attended, low, hidden, after=()):
    _, rows, units = gate.shape
    width, model = attended.shape[1], low.shape[1]
    tile, count = min(512, model), model // min(512, model)
    part = lambda t: (0, t)
    size = units // 2

    def compute(core, ins, keep, send):
        gate, attended, low, hidden = ins
        keep_and_send(own, core, rows_dot(gate[0], low[...]), 0, keep, send, slice(0, size))
        keep_and_send(own, core, rows_dot(attended[...], hidden[...]), 0, keep, send, slice(size, size + width // 2))

    return trade(
        "trade_down", collective, count, (size + width // 2, tile), compute, functools.partial(store_columns, count),
        [(gate, (1, rows, units), lambda t: (0, 0, 0)), (attended, (rows, width), lambda t: (0, 0)),
         (low, (rows, tile), part), (hidden, (rows, tile), part)],
        (1, size + width // 2, model), after,
    )


def trade_attn(collective, own, normed, grads, after=()):
    rows, width = grads.shape[0], grads.shape[1] // 3
    model = normed.shape[1]
    tile, count = min(512, model), model // min(512, model)

    def compute(core, ins, keep, send):
        for i in range(3):
            value = rows_dot(ins[0][...], ins[1][:, i * width:(i + 1) * width])
            keep_and_send(own, core, value, 1, keep, send, i)

    def store(out, t, value):
        out[:, t * tile:(t + 1) * tile] = value

    return trade(
        "trade_attn", collective, count, (3, tile, width // 2), compute, store,
        [(normed, (rows, tile), lambda t: (0, t)), (grads, (rows, 3 * width), lambda t: (0, 0))],
        (3, model, width // 2), after,
    )


def pull_kernel(tokens, hidden_grad, gain, grads, weights, *refs):
    more, parts, (out, gain_ref) = refs[:1], refs[1:-2], refs[-2:]
    width = weights.shape[2]
    total = None
    for i in range(3):
        terms = [cols_dot(grads[:, i * width:(i + 1) * width], weights[i])]
        for side, part in enumerate(parts):
            size = part.shape[2]
            first = i * width + side * size
            terms.append(cols_dot(more[0][:, first:first + size], part[i]))
        for term in terms:
            total = term if total is None else total + term
    back, gain_part = norm_back_rows(tokens[...].astype(jnp.float32), gain[...], total)
    out[...] = hidden_grad[...] + back
    add_gain(gain_ref, gain_part)


def pull(tokens, hidden_grad, gain, grads, weights, more=None, parts=(), after=()):
    rows, model = tokens.shape
    tile = row_tile(rows)
    row = lambda i: (i, 0)
    size = grads.shape[1]
    return run(
        pull_kernel, "pull", (rows // tile,),
        [(tokens, (tile, model), row), (hidden_grad, (tile, model), row), whole(gain), (grads, (tile, size), row), whole(weights)]
        + [(grads if more is None else more, (tile, size), row)]
        + [(p, (3,) + p.shape[1:], lambda i: (0, 0, 0)) for p in parts],
        [(shaped((rows, model), jnp.float32), (tile, model), row), (shaped((1, model), jnp.float32), (1, model), lambda i: (0, 0))],
        after,
    )


def assemble_call(body, mine, other, core, outs, after):
    same = lambda i, s: (0,) * mine.ndim
    return pl.pallas_call(
        lambda *refs: body(*refs[:3], *refs[3 + len(after):]),
        grid_spec=pltpu.PrefetchScalarGridSpec(
            num_scalar_prefetch=1, grid=(2,),
            in_specs=[pl.BlockSpec(mine.shape, same)] * 2 + [pl.BlockSpec(memory_space=pl.ANY)] * len(after),
            out_specs=[
                pl.BlockSpec(block, functools.partial(lambda axis, rank, i, s: tuple((i ^ s[0]) * (d == axis) for d in range(rank)), axis, len(block)))
                for _, block, axis in outs
            ],
        ),
        out_shape=[shaped(shape, jnp.float32) for shape, _, _ in outs],
        compiler_params=pltpu.CompilerParams(vmem_limit_bytes=56 << 20),
        name="assemble",
    )(jnp.reshape(core, (1,)).astype(jnp.int32), mine, other, *after)


def assemble_kernel(side, mine, other, out):
    out[...] = jnp.where(pl.program_id(0) == 0, mine[...], other[...]).astype(jnp.float32)


def assemble(mine, other, core, axis, after=()):
    shape = tuple(2 * n if d == axis else n for d, n in enumerate(mine.shape))
    return assemble_call(assemble_kernel, mine, other, core, [(shape, mine.shape, axis)], after)[0]


def assemble_down_kernel(side, mine, other, down, out):
    chosen = jnp.where(pl.program_id(0) == 0, mine[0], other[0]).astype(jnp.float32)
    size = down.shape[0]
    down[...] = chosen[:size]
    out[...] = chosen[size:]


def assemble_down(mine, other, core, units, after=()):
    _, rows, model = mine.shape
    sizes = (units // 2, rows - units // 2)
    return assemble_call(
        assemble_down_kernel, mine, other, core, [((2 * n, model), (n, model), 0) for n in sizes], after
    )


class Links:
    def __init__(self, dp, tensor):
        self.dp, self.tensor = dp, tensor
        self.id = lax.axis_index("dp")
        self.core, self.row = self.id % 2, self.id // 2 % 2

    def send(self, value, target):
        pairs = [
            (d * self.tensor + t, to)
            for d in range(self.dp) for t in range(self.tensor)
            for to in [target(d, t)] if to is not None
        ]
        return lax.ppermute(value, AXES, pairs)

    def cross(self, value):
        return self.send(value, lambda d, t: d * self.tensor + (1 - t))

    def flip(self, value, even, odd=None):
        bits = (even, even if odd is None else odd)
        return self.send(value, lambda d, t: (d ^ bits[d % 2]) * self.tensor + t)

    def shift(self, value, by):
        return self.send(value, lambda d, t: d * self.tensor + t + by if 0 <= t + by < self.tensor else None)

    def bit_of(self, even, odd):
        return jnp.where(self.core == 0, (self.id & even) // even, (self.id & odd) // odd)


def tie(value, *others):
    return lax.optimization_barrier((value,) + others)[0]


def half(value, index, axis):
    size = value.shape[axis] // 2
    if isinstance(index, int):
        return lax.slice_in_dim(value, index * size, (index + 1) * size, axis=axis)
    return lax.dynamic_slice_in_dim(value, index * size, size, axis)


def order(bit, first, second, axis):
    return jnp.where(bit == 0, jnp.concatenate([first, second], axis), jnp.concatenate([second, first], axis))


class Summing:
    ROW_FIRST = ((2, 2, 1), (4, 4, 2), (8, 8, 3))
    SPLIT = ((2, 4, 4), (4, 8, 5), (8, 2, 6))

    def __init__(self, links, flags, axis, steps):
        self.links, self.flags, self.axis, self.steps = links, flags, axis, steps

    def send_far(self, far):
        self.far, self.crossed = far, self.links.cross(far)

    def across(self, *after, parts=None):
        self.split(0, self.near, self.crossed if parts is None else jnp.concatenate(parts, 0), after)

    def split(self, step, a, b, after):
        even, odd, which = self.steps[step]
        a, bit = tie(a, *after), self.flags[which]
        part = lambda k: half(a, k, self.axis) + half(b, k, self.axis)
        self.held, self.moved = part(bit), self.links.flip(part(1 - bit), even, odd)

    def scatter(self, *after):
        self.split(1, self.held, self.moved, after)

    def both(self, *after):
        self.held = tie(self.held, *after) + self.moved
        self.moved = self.links.flip(self.held, *self.steps[2][:2])

    def both_add(self, *after):
        self.held = tie(self.held, *after) + self.moved
        self.moved = self.links.flip(self.held, *self.steps[1][:2])

    def gather(self, *after):
        self.held = order(self.flags[self.steps[1][2]], tie(self.held, *after), self.moved, self.axis)
        self.moved = self.links.flip(self.held, *self.steps[0][:2])

    def last(self, *after):
        self.held = order(self.flags[self.steps[0][2]], tie(self.held, *after), self.moved, self.axis)
        self.moved = self.links.flip(self.held, 1)
        return self.held, self.moved, self.links.core


def on_device(tokens, lengths, order_, gain_attn, w_qkv, w_out, gain_mlp, w_in, w_down, cotangent):
    rows, model = tokens.shape
    dp, tensor = lax.axis_size("dp"), lax.axis_size("tensor")
    tensor_id = lax.axis_index("tensor")
    links = Links(dp, tensor)
    paired = tensor == 2 and dp == 16

    slot_count = rows * tensor // MAXLEN
    my_order = lax.dynamic_slice_in_dim(order_, links.id * slot_count, slot_count, 0)
    chosen = my_order[:, None] == jnp.arange(lengths.shape[0], dtype=jnp.int32)[None, :]
    slot_len = jnp.sum(jnp.where(chosen, lengths[None, :], 0), 1)
    slots = jnp.arange(slot_count, dtype=jnp.int32)[None, :]
    block_row = tensor_id * rows + BQ * jnp.arange(rows // BQ, dtype=jnp.int32)
    block_len = jnp.sum(jnp.where((block_row // MAXLEN)[:, None] == slots, slot_len[None, :], 0), 1)
    place = jnp.stack([block_row % MAXLEN, block_len])

    w_qkv = w_qkv.transpose(1, 0, 2)
    w_in = w_in.transpose(1, 2, 0)
    gain_attn, gain_mlp = gain_attn[None], gain_mlp[None]
    if not paired:
        before, after = links.shift(tokens[rows - HALF:], 1), links.shift(tokens[:HALF], -1)
        return general(
            links, place, tokens, before, after, gain_attn, w_qkv, w_out, gain_mlp, w_in, w_down, cotangent
        )

    start = jnp.where(tensor_id == 0, rows - HALF, 0)
    border = links.cross(lax.dynamic_slice_in_dim(tokens, start, HALF, 0))
    core = links.core
    bits = [links.id // bit % 2 for bit in (1, 2, 4, 8)]
    split_bits = [jnp.where(core == 0, bits[i], bits[j]) for i, j in ((1, 2), (2, 3), (3, 1))]
    flags = jnp.stack(bits + split_bits).astype(jnp.int32)
    place = jnp.concatenate([place, jnp.pad(flags, (0, place.shape[1] - flags.shape[0]))[None]], 0)
    width, units = w_out.shape[0], w_down.shape[0]
    size = width // 2
    out_half = half(tie(w_out, border), core, 0)
    stacked = jnp.concatenate([out_half[:, k * size:(k + 1) * size] for k in range(model // size)], 0)
    piece = jnp.concatenate([half(tie(w_qkv, border), core, 2), stacked[None]], 0)
    attn_direct = links.cross(piece)

    normed = norm_rows(tokens, border, border, gain_attn)
    quarter = lambda w, a, b: half(half(w, core, a), bits[1], b)
    in_direct = links.cross(quarter(tie(w_in, normed), 1, 2))
    down_direct = links.cross(quarter(tie(w_down, normed)[None], 1, 2))
    q0, k0, v0 = project(normed, w_qkv)
    attended0, logs0 = attend(place, q0, k0, v0)
    attn_parts = (attn_direct, links.flip(tie(attn_direct, attended0), 1))
    q1, k1, v1 = project_parts(normed, attn_parts, after=[attended0])
    attended1, logs1 = attend(place, q1, k1, v1)
    in_direct = tie(in_direct, attended1)
    in_relayed = links.flip(in_direct, 2)
    in_core = links.flip(in_direct, 1)
    hidden, normed_mlp = mix(tokens, gain_mlp, attended0, w_out, attended1, attn_parts, after=[in_direct])
    gate0, lift0, out_low, branch, pulled = mlp_first(place, normed_mlp, cotangent, w_in, w_down, after=[in_core])
    down_direct = tie(down_direct, hidden)
    down_relayed = links.flip(down_direct, 2)
    down_core = links.flip(down_direct, 1)
    in_relayed = tie(in_relayed, branch)
    down_relayed = tie(down_relayed, in_relayed)
    weights = (
        in_direct, in_relayed, in_core, links.flip(in_relayed, 1),
        down_direct, down_relayed, down_core, links.flip(down_relayed, 1),
    )
    gate1, lift1, output, hidden_grad, hidden_low, gain_mlp_grad, back0, back1 = mlp_last(
        place, normed_mlp, cotangent, weights, hidden, gain_mlp, branch, pulled, w_out, attn_parts
    )
    inner = Summing(links, flags, 2, Summing.ROW_FIRST)
    inner_a, inner_b = (Summing(links, flags, 2, Summing.ROW_FIRST) for _ in range(2))
    down = Summing(links, flags, 2, Summing.SPLIT)
    attn = Summing(links, flags, 1, Summing.SPLIT)

    inner_a.send_far(trade_outer(0, False, lift1, normed_mlp, [0], after=[back1]))
    inner_b.send_far(trade_outer(1, False, lift1, normed_mlp, [1], after=[inner_a.far]))
    inner.near = trade_outer(2, True, lift0, normed_mlp, [0, 1], after=[inner_b.far])
    d1, edge1 = attend_back(place, q1, k1, v1, back1, logs1, after=[inner.near])
    down.send_far(trade_down(3, False, gate1, attended1, out_low, hidden_low, after=[d1, inner_a.crossed]))
    d0, edge0 = attend_back(place, q0, k0, v0, back0, logs0, after=[down.far])
    inner.across(d0, parts=[inner_a.crossed, inner_b.crossed])

    swap = lambda e: jnp.where(core == 0, e, jnp.concatenate([e[:, size:], e[:, :size]], 1))
    edge_out = lambda e: jnp.concatenate([swap(e[:, :width]), swap(e[:, width:])], 1)
    edges = jnp.stack([edge_out(jnp.where(tensor_id == 0, e[1], e[0])) for e in (edge1, edge0)])
    edges = links.cross(edges)
    down.near = trade_down(4, True, gate0, attended0, out_low, hidden_low, after=[inner.held])
    edges = tie(edges, down.near)

    def add_edge(d, edge):
        held = lax.dynamic_slice(d, (start, width), (HALF, 2 * width))
        return lax.dynamic_update_slice(d, held + edge, (start, width))

    d1, d0 = add_edge(d1, edges[1]), add_edge(d0, edges[0])
    attn.send_far(trade_attn(5, False, normed, d1))
    attn.near = trade_attn(6, True, normed, d0, after=[attn.far])
    inner.scatter(attn.near)
    down.across(inner.held)
    input_grad, gain_attn_grad = pull(tokens, hidden_grad, gain_attn, d0, w_qkv, d1, attn_parts, after=[down.held])
    inner.both(input_grad)
    gain_total = jnp.concatenate((gain_attn_grad, gain_mlp_grad))
    attn.across(inner.held)
    down.scatter(attn.held)
    inner.both_add(down.held)
    gain_total = gain_total + tie(links.cross(gain_total), attn.held)
    attn.scatter(inner.held)
    gain_total = gain_total + tie(links.flip(gain_total, 1), attn.held)
    down.both(attn.held, gain_total)
    inner.gather(down.held)
    attn.both(inner.held)
    down.both_add(attn.held)
    attn.both_add(down.held)
    gain_total = gain_total + tie(links.flip(gain_total, 2), attn.held)
    grads_in = inner.last(attn.held)
    down.gather(grads_in[0])
    attn.gather(down.held, gain_total)
    grad_w_in = assemble(*grads_in, 1, after=[attn.held])
    gain_total = gain_total + tie(links.flip(gain_total, 4), grad_w_in)
    grads_down = down.last(grad_w_in)
    grads_attn = attn.last(grads_down[0], gain_total)
    grad_w_down, grad_w_out = assemble_down(*grads_down, units, after=[grads_attn[0]])
    gain_total = gain_total + tie(links.flip(gain_total, 8), grad_w_down)
    grad_w_qkv = assemble(*grads_attn, 2, after=[grad_w_down])
    return (
        output,
        input_grad,
        gain_total[0],
        grad_w_qkv.transpose(1, 0, 2),
        grad_w_out,
        gain_total[1],
        grad_w_in.transpose(2, 0, 1),
        grad_w_down,
    )


def general(links, place, tokens, before, after, gain_attn, w_qkv, w_out, gain_mlp, w_in, w_down, cotangent):
    rows = tokens.shape[0]
    w_qkv, w_out, w_in, w_down = (
        lax.all_gather(w, "tensor", axis=axis, tiled=True)
        for w, axis in ((w_qkv, 2), (w_out, 0), (w_in, 1), (w_down, 0))
    )
    normed = norm_rows(tokens, before, after, gain_attn)
    q, k, v = project(normed, w_qkv)
    attended, logs = attend(place, q, k, v)
    hidden, normed_mlp = mix(tokens, gain_mlp, attended, w_out)
    blank = jnp.zeros_like(hidden)
    gate, lift, output, hidden_grad, hidden_low, gain_mlp_grad, back = mlp_last(
        place, normed_mlp, cotangent, (w_in, w_down), hidden, gain_mlp, blank, blank, w_out
    )
    position = jnp.repeat(place[0], BQ) + jnp.tile(jnp.arange(BQ, dtype=jnp.int32), place.shape[1])
    out_low = jnp.where((position < jnp.repeat(place[1], BQ))[:, None], cotangent, jnp.zeros_like(cotangent))
    flags = jnp.zeros((1,), jnp.int32)
    units, width = w_down.shape[0], w_out.shape[0]
    low, high = outer_down(flags, False, gate, attended, out_low, hidden_low)
    down = jnp.concatenate([low[0, :units // 2], high[0, :units // 2]], 0)
    out = jnp.concatenate([low[0, units // 2:], high[0, units // 2:]], 0)
    inner = jnp.concatenate(outer(flags, False, lift, normed_mlp), 1)
    d, edge = attend_back(place, q, k, v, back, logs)
    d = d.at[:HALF, width:].add(links.shift(edge[1], 1)).at[rows - HALF:, width:].add(links.shift(edge[0], -1))
    qkv = jnp.concatenate(outer_attn(flags, False, normed, d), 2)
    input_grad, gain_attn_grad = pull(tokens, hidden_grad, gain_attn, d, w_qkv)
    down, inner, out, qkv = (
        lax.psum(lax.psum_scatter(g, "tensor", scatter_dimension=axis, tiled=True), "dp").astype(jnp.float32)
        for g, axis in ((down, 0), (inner, 1), (out, 0), (qkv, 2))
    )
    gain_total = lax.psum(jnp.concatenate((gain_attn_grad, gain_mlp_grad)), AXES)
    return (
        output, input_grad, gain_total[0], qkv.transpose(1, 0, 2), out, gain_total[1],
        inner.transpose(2, 0, 1), down,
    )


def solution(mesh):
    split = P(AXES, None)
    wide = P(None, None, "tensor")
    tall = P("tensor", None)
    return jax.shard_map(
        on_device,
        mesh=mesh,
        in_specs=(split, P(), P(), P(), wide, tall, P(), wide, tall, split),
        out_specs=(split, split, P(), wide, tall, P(), wide, tall),
        check_vma=False,
    )
```

```python
import functools
import math

import jax
import jax.numpy as jnp
from jax import lax
from jax.experimental import pallas as pl
from jax.experimental.pallas import tpu as pltpu
from jax.sharding import PartitionSpec as P

AXES = ("dp", "tensor")
EPS = 1e-05
HEAD_DIM = 64
HALF = 64
MAXLEN = 1024
BQ = 128
LOW = jnp.bfloat16
NEG = -1e30


def cols_dot(left, right):
    return lax.dot_general(left, right, (((1,), (1,)), ((), ())), preferred_element_type=jnp.float32)


def rows_dot(left, right):
    return lax.dot_general(left, right, (((0,), (0,)), ((), ())), preferred_element_type=jnp.float32)


def plain_dot(left, right):
    return lax.dot_general(left, right, (((1,), (0,)), ((), ())), preferred_element_type=jnp.float32)


def norm_parts(values):
    center = values - jnp.mean(values, -1, keepdims=True)
    rate = lax.rsqrt(jnp.mean(center * center, -1, keepdims=True) + EPS)
    return center * rate, rate


COST = {
    "norm_rows": 6, "project": 9, "project_parts": 9, "attend": 20, "mix": 11, "mlp_first": 39, "mlp_last": 49, "outer": 9,
    "attend_back": 25, "trade_outer": 9, "trade_down": 12, "trade_attn": 10, "outer_down": 12, "outer_attn": 10, "pull": 18,
}
SCALE = 100


def shaped(shape, dtype=LOW):
    return jax.ShapeDtypeStruct(shape, dtype)


def run(body, name, grid, ins, outs, after=(), place=None, scratch=(), flops=0, vmem=56, seen=False, collective=None):
    extra = [a for a in after if a is not None]
    count = len(ins)

    def kernel(*refs):
        lead = refs[:1] if place is not None else ()
        refs = refs[len(lead):]
        body(*lead, *refs[:count], *refs[count + len(extra):])

    def spec(block, index):
        if place is not None and not seen:
            return pl.BlockSpec(block, lambda *a: index(*a[:-1]))
        return pl.BlockSpec(block, index)

    call = pl.pallas_call(
        kernel,
        grid_spec=pltpu.PrefetchScalarGridSpec(
            num_scalar_prefetch=0 if place is None else 1,
            grid=grid,
            in_specs=[spec(b, m) for _, b, m in ins] + [pl.BlockSpec(memory_space=pl.ANY)] * len(extra),
            out_specs=[spec(b, m) for _, b, m in outs],
            scratch_shapes=list(scratch),
        ),
        out_shape=[s for s, _, _ in outs],
        compiler_params=pltpu.CompilerParams(
            vmem_limit_bytes=vmem << 20, collective_id=collective, has_side_effects=collective is not None
        ),
        cost_estimate=pl.CostEstimate(flops=int(COST[name] * SCALE), bytes_accessed=1000, transcendentals=0),
        name=name,
    )
    lead = () if place is None else (place,)
    return call(*lead, *[a for a, _, _ in ins], *extra)


def window_masks(shared, ones, pos0, length):
    j = lax.broadcasted_iota(jnp.int32, (BQ, 2 * BQ), 0)
    i = lax.broadcasted_iota(jnp.int32, (BQ, 2 * BQ), 1) % BQ

    @pl.when(pl.program_id(0) == 0)
    def _():
        shared[0] = j + jnp.where(i <= j, 0, BQ)
        shared[1] = jnp.where(j == (i + HALF) % BQ, 1, 0)
        ones[0] = jnp.where(i <= j, 1.0, 0.0).astype(LOW)
        ones[1] = jnp.where(i == j, 1.0, 0.0).astype(LOW)

    key = shared[0]
    top = jnp.minimum(length, MAXLEN)
    bias = jnp.where(((key >= HALF - pos0) & (key < top - pos0 + HALF)) | (shared[1] > 0), 0.0, NEG)
    lane = lax.broadcasted_iota(jnp.int32, (1, 2 * BQ), 1) % BQ
    last_bias = jnp.where(pos0 + HALF + lane < top, 0.0, NEG)
    return key < BQ, i == j, bias, last_bias


def split_heads(pair):
    lane = lax.broadcasted_iota(jnp.int32, pair.shape, 1)
    zero = jnp.zeros_like(pair)
    return jnp.concatenate([jnp.where(lane < HEAD_DIM, pair, zero), jnp.where(lane >= HEAD_DIM, pair, zero)], 0)


def join_heads(wide, scale=None):
    first, second = wide[:HEAD_DIM, :BQ], wide[HEAD_DIM:, BQ:]
    if scale is not None:
        first, second = first * scale[:, :BQ], second * scale[:, BQ:]
    return jnp.concatenate([first, second], 0).T


def fold(near, diag, wide):
    low = wide[BQ:]
    return jnp.where(near, wide[:BQ], low), jnp.sum(jnp.where(diag, low, 0.0), 0, keepdims=True)


def unfold(ones, tile, last):
    tile = tile.astype(LOW)
    upper = tile * ones[0]
    return jnp.concatenate([upper, (tile - upper) + ones[1] * last.astype(LOW)], 0)


def window_rows(before, here, after, c):
    return jnp.concatenate([before[:, c], here[:, c], after[:, c]], 0)


def attend_kernel(place, q, kb, kh, ka, vb, vh, va, out_ref, log_ref, shared, ones):
    blk = pl.program_id(0)
    near, diag, bias, last_bias = window_masks(shared, ones, place[0, blk], place[1, blk])
    columns = [slice(p * BQ, (p + 1) * BQ) for p in range(out_ref.shape[1] // BQ)]

    def score(c):
        return cols_dot(window_rows(kb, kh, ka, c), split_heads(q[:, c] * 0.125))

    def soft(wide):
        scores, last = fold(near, diag, wide)
        scores, last = scores + bias, last + last_bias
        row_max = jnp.maximum(jnp.max(scores, 0, keepdims=True), last)
        expons, last = jnp.exp(scores - row_max), jnp.exp(last - row_max)
        summed = jnp.sum(expons, 0, keepdims=True) + last
        return unfold(ones, expons, last), row_max, summed

    wides = [score(c) for c in columns]
    softs = [soft(w) for w in wides]
    for pair, c in enumerate(columns):
        probs, row_max, summed = softs[pair]
        out_ref[:, c] = join_heads(rows_dot(window_rows(vb, vh, va, c), probs), 1.0 / summed).astype(LOW)
        log_ref[0, pair:pair + 1] = row_max + jnp.log(summed)


def attend_back_kernel(place, q, kb, kh, ka, vb, vh, va, g_ref, log_ref, d_ref, edge_ref, carry, tail, dq_keep, shared, ones):
    step = pl.program_id(0)
    steps = pl.num_programs(0)
    width = g_ref.shape[1]

    @pl.when(step == 0)
    def _():
        carry[...] = jnp.zeros_like(carry)
        tail[...] = jnp.zeros_like(tail)
        dq_keep[...] = jnp.zeros_like(dq_keep)

    d_ref[:, :width] = dq_keep[...]
    d_ref[:HALF, width:] = tail[...]

    @pl.when(step < steps - 1)
    def _():
        near, diag, bias, last_bias = window_masks(shared, ones, place[0, step], place[1, step])
        columns = [slice(p * BQ, (p + 1) * BQ) for p in range(width // BQ)]

        def start(c):
            queries = split_heads(q[:, c] * 0.125)
            grads = split_heads(g_ref[:, c])
            keyset = window_rows(kb, kh, ka, c)
            return queries, grads, keyset, cols_dot(keyset, queries), cols_dot(window_rows(vb, vh, va, c), grads)

        starts = [start(c) for c in columns]
        for pair, c in enumerate(columns):
            ready = starts[pair]
            v = slice(width + c.start, width + c.stop)
            queries, grads, keyset, wide, wide_grad = ready
            log_row = log_ref[0, pair:pair + 1]
            scores, last = fold(near, diag, wide)
            expons, last = jnp.exp(scores + (bias - log_row)), jnp.exp(last + (last_bias - log_row))
            prob_grad, last_grad = fold(near, diag, wide_grad)
            inner = jnp.sum(expons * prob_grad, 0, keepdims=True) + last * last_grad
            score_grad = unfold(ones, expons * (prob_grad - inner), last * (last_grad - inner))
            probs = unfold(ones, expons, last)
            dq_keep[:, c] = join_heads(rows_dot(keyset, score_grad) * 0.125).astype(LOW)
            for lanes, grad in ((c, plain_dot(score_grad, queries)), (v, plain_dot(probs, grads))):
                done = (carry[:, lanes] + grad[:BQ]).astype(LOW)
                carry[:, lanes] = grad[BQ:]
                d_ref[HALF:, lanes.start + width:lanes.stop + width] = done[:HALF]
                tail[:, lanes] = done[HALF:]

        @pl.when(step == 0)
        def _():
            edge_ref[0] = d_ref[HALF:, width:]

    @pl.when(step == steps - 1)
    def _():
        done = carry[...].astype(LOW)
        d_ref[HALF:, width:] = done[:HALF]
        edge_ref[1] = done[HALF:]


def window_specs(q, k, v, blocks):
    last, width = blocks - 1, k.shape[1]
    here = lambda b: (jnp.minimum(b, last), 0)
    before = lambda b: (jnp.where(b == 0, 2 * blocks, 2 * jnp.minimum(b, last) - 1), 0)
    after = lambda b: (jnp.where(b >= last, 2 * blocks + 1, 2 * b + 2), 0)
    specs = [(q, (BQ, width), here)]
    for value in (k, v):
        specs += [(value, (HALF, width), before), (value, (BQ, width), here), (value, (HALF, width), after)]
    return specs


def attend(place, q, k, v, after=()):
    blocks, width = k.shape[0] // BQ - 1, k.shape[1]
    pairs = width // BQ
    return run(
        attend_kernel, "attend", (blocks,), window_specs(q, k, v, blocks),
        [
            (shaped((blocks * BQ, width)), (BQ, width), lambda b: (b, 0)),
            (shaped((blocks, pairs, 2 * BQ), jnp.float32), (1, pairs, 2 * BQ), lambda b: (b, 0, 0)),
        ],
        after, place, scratch=[pltpu.VMEM((2, BQ, 2 * BQ), jnp.int32), pltpu.VMEM((2, BQ, 2 * BQ), LOW)],
    )


def attend_back(place, q, k, v, grads, logs, after=()):
    blocks, width = grads.shape[0] // BQ, k.shape[1]
    pairs = width // BQ
    last = blocks - 1
    return run(
        attend_back_kernel, "attend_back", (blocks + 1,),
        window_specs(q, k, v, blocks)
        + [
            (grads, (BQ, width), lambda b: (jnp.minimum(b, last), 0)),
            (logs, (1, pairs, 2 * BQ), lambda b: (jnp.minimum(b, last), 0, 0)),
        ],
        [
            (shaped((blocks * BQ, 3 * width)), (BQ, 3 * width), lambda b: (jnp.maximum(b - 1, 0), 0)),
            (shaped((2, HALF, 2 * width)), (2, HALF, 2 * width), lambda b: (0, 0, 0)),
        ],
        after, place,
        scratch=[
            pltpu.VMEM((BQ, 2 * width), jnp.float32),
            pltpu.VMEM((HALF, 2 * width), LOW),
            pltpu.VMEM((BQ, width), LOW),
            pltpu.VMEM((2, BQ, 2 * BQ), jnp.int32),
            pltpu.VMEM((2, BQ, 2 * BQ), LOW),
        ],
        flops=blocks * pairs * BQ * BQ * BQ * 512,
    )


def norm_kernel(tokens, before, after, gain, out):
    step, tile = pl.program_id(0), tokens.shape[0]

    @pl.when(step < pl.num_programs(0) - 1)
    def _():
        out[...] = (norm_parts(tokens[...].astype(jnp.float32))[0] * gain[...]).astype(LOW)

    @pl.when(step == pl.num_programs(0) - 1)
    def _():
        values = jnp.concatenate([before[...], after[...]], 0).astype(jnp.float32)
        out[:BQ] = (norm_parts(values)[0] * gain[...]).astype(LOW)


def norm_rows(tokens, before, after, gain):
    rows, model = tokens.shape
    tile = 3 * BQ
    blocks = rows // tile
    full = lambda i: (0, 0)
    return run(
        norm_kernel, "norm_rows", (blocks + 1,),
        [
            (tokens, (tile, model), lambda i: (jnp.minimum(i, blocks - 1), 0)),
            (before, (HALF, model), full), (after, (HALF, model), full), (gain, (1, model), full),
        ],
        [(shaped((rows + BQ, model)), (tile, model), lambda i: (i, 0))],
    )[0]


def project_kernel(normed, weights, *outs):
    for i, out in enumerate(outs):
        out[...] = plain_dot(normed[...], weights[i]).astype(LOW)


def project(normed, weights, after=()):
    rows, model = normed.shape
    width = weights.shape[2]
    tile = rows // 4 if rows % 64 == 0 else rows
    return run(
        project_kernel, "project", (rows // tile,),
        [(normed, (tile, model), lambda i: (i, 0)), (weights, (3, model, width), lambda i: (0, 0, 0))],
        [(shaped((rows, width)), (tile, width), lambda i: (i, 0))] * 3,
        after, flops=6 * rows * model * width,
    )


def project_parts_kernel(normed, mine, other, *outs):
    size = mine.shape[2]
    for i, out in enumerate(outs):
        out[:, :size] = plain_dot(normed[...], mine[i]).astype(LOW)
        out[:, size:] = plain_dot(normed[...], other[i]).astype(LOW)


def project_parts(normed, parts, after=()):
    rows, model = normed.shape
    size = parts[0].shape[2]
    tile = rows // 4
    return run(
        project_parts_kernel, "project_parts", (rows // tile,),
        [(normed, (tile, model), lambda i: (i, 0))] + [(p, (3, model, size), lambda i: (0, 0, 0)) for p in parts],
        [(shaped((rows, 2 * size)), (tile, 2 * size), lambda i: (i, 0))] * 3,
        after,
    )


def out_rows(part):
    size = part.shape[2]
    return jnp.concatenate([part[3, k * size:(k + 1) * size] for k in range(part.shape[1] // size)], 1)


def row_tile(rows):
    return 256 if rows % 256 == 0 else 128


def keep_rows(place, step, tile):
    row = lax.broadcasted_iota(jnp.int32, (BQ, 1), 0)
    parts = []
    for i in range(tile // BQ):
        b = step * (tile // BQ) + i
        parts.append(jnp.where(row + place[0, b] < place[1, b], 1.0, 0.0))
    return jnp.concatenate(parts, 0)


def mix_kernel(tokens, gain, attended, weights, *refs):
    attended_more, parts, (hidden, normed) = refs[:1], refs[1:-2], refs[-2:]
    total = tokens[...].astype(jnp.float32) + plain_dot(attended[...], weights[...])
    for side, part in enumerate(parts):
        size = part.shape[2]
        total = total + plain_dot(attended_more[0][:, side * size:(side + 1) * size], out_rows(part))
    hidden[...] = total
    normed[...] = (norm_parts(total)[0] * gain[...]).astype(LOW)


def mix(tokens, gain, attended, weights, more=None, parts=(), after=()):
    rows, model = tokens.shape
    tile = row_tile(rows)
    row, full = (lambda i: (i, 0)), (lambda i: (0, 0))
    width = weights.shape[0]
    return run(
        mix_kernel, "mix", (rows // tile,),
        [(tokens, (tile, model), row), (gain, (1, model), full), (attended, (tile, width), row), (weights, weights.shape, full)]
        + [(attended if more is None else more, (tile, width), row)]
        + [(p, p.shape, lambda i: (0, 0, 0)) for p in parts],
        [(shaped((rows, model), jnp.float32), (tile, model), row), (shaped((rows, model)), (tile, model), row)],
        after,
    )


def gelu_parts(value):
    size = jnp.abs(value)
    bell = jnp.exp(-0.5 * value * value)
    t = 1.0 / (1.0 + (0.3275911 * 2.0 ** -0.5) * size)
    series = t * (0.254829592 + t * (-0.284496736 + t * (1.421413741 + t * (-1.453152027 + t * 1.061405429))))
    tail = 0.5 * series * bell
    below = jnp.where(value < 0, tail, 1.0 - tail)
    return value * below, below + value * bell * ((2.0 * math.pi) ** -0.5)


def mlp_body(place, normed, cotangent, win, wdown, gate_ref, lift_ref):
    tile = normed.shape[0]
    kept = keep_rows(place, pl.program_id(0), tile)
    out_grad = kept * cotangent[...].astype(jnp.float32)
    out_low = out_grad.astype(LOW)
    first = cols_dot(normed[...], win[0])
    second = cols_dot(normed[...], win[1])
    gelu, slope = gelu_parts(first)
    gate = (gelu * second).astype(LOW)
    gate_ref[0] = gate
    branch = plain_dot(gate, wdown[...])
    grad = cols_dot(out_low, wdown[...])
    lift1 = (grad * second * slope).astype(LOW)
    lift2 = (grad * gelu).astype(LOW)
    lift_ref[0] = lift1
    lift_ref[1] = lift2
    pulled = plain_dot(lift1, win[0]) + plain_dot(lift2, win[1])
    return kept, out_grad, out_low, branch, pulled


def mlp_first_kernel(place, normed, cotangent, win, wdown, gate_ref, lift_ref, low_ref, branch_ref, pulled_ref):
    _, _, out_low, branch, pulled = mlp_body(place, normed, cotangent, win, wdown, gate_ref, lift_ref)
    low_ref[...] = out_low
    branch_ref[...] = branch
    pulled_ref[...] = pulled


def norm_back_rows(values, gain, grad):
    unit, rate = norm_parts(values)
    pulled = grad * gain
    mean_one = jnp.mean(pulled, -1, keepdims=True)
    mean_two = jnp.mean(pulled * unit, -1, keepdims=True)
    return rate * (pulled - mean_one - unit * mean_two), jnp.sum(grad * unit, 0, keepdims=True)


def add_gain(gain_ref, part):
    @pl.when(pl.program_id(0) == 0)
    def _():
        gain_ref[...] = jnp.zeros_like(gain_ref)

    gain_ref[...] += part


def mlp_last_kernel(fetched, place, normed, cotangent, *refs):
    if fetched:
        pieces, refs = refs[:6], refs[6:]
        win, wdown = refs[-2:]

        @pl.when(pl.program_id(0) == 0)
        def _():
            units, model = pieces[0].shape[1:]
            for part in range(4):
                rows = slice(part // 2 * units, (part // 2 + 1) * units)
                columns = pl.ds(pl.multiple_of((place[2, 1] ^ (part % 2)) * model, model), model)
                for side in range(2):
                    win[side, rows, columns] = pieces[part][side]
            for side in range(2):
                wdown[side * units:(side + 1) * units] = pieces[4 + side][...]
    else:
        (win, wdown), refs = refs[:2], refs[2:]
    hidden, gain, branch_in, pulled_in, weights = refs[:5]
    parts, refs = (refs[5:7], refs[7:]) if fetched else ((), refs[5:])
    gate_ref, lift_ref, out_ref, grad_ref, low_ref, gain_ref, attn = refs[:7]
    kept, out_grad, _, branch, pulled = mlp_body(place, normed, cotangent, win, wdown, gate_ref, lift_ref)
    out_ref[...] = (kept * (hidden[...] + (branch_in[...] + branch))).astype(LOW)
    back, gain_part = norm_back_rows(hidden[...], gain[...], pulled_in[...] + pulled)
    total = out_grad + back
    grad_ref[...] = total
    low = total.astype(LOW)
    low_ref[...] = low
    attn[...] = cols_dot(low, weights[...]).astype(LOW)
    for side, part in enumerate(parts):
        size = part.shape[2]
        refs[7][:, side * size:(side + 1) * size] = cols_dot(low, out_rows(part)).astype(LOW)
    add_gain(gain_ref, gain_part)


def mlp_specs(normed, cotangent, units):
    rows, model = normed.shape
    tile = row_tile(rows)
    row = lambda i: (i, 0)
    ins = [(normed, (tile, model), row), (cotangent, (tile, model), row)]
    outs = [
        (shaped((1, rows, units)), (1, tile, units), lambda i: (0, i, 0)),
        (shaped((2, rows, units)), (2, tile, units), lambda i: (0, i, 0)),
    ]
    return rows, model, tile, row, ins, outs


def whole(value):
    return (value, value.shape, lambda i: (0,) * value.ndim)


def mlp_first(place, normed, cotangent, win, wdown, after=()):
    rows, model, tile, row, ins, outs = mlp_specs(normed, cotangent, wdown.shape[0])
    outs = outs + [(shaped((rows, model)), (tile, model), row)]
    outs = outs + [(shaped((rows, model), jnp.float32), (tile, model), row)] * 2
    return run(mlp_first_kernel, "mlp_first", (rows // tile,), ins + [whole(win), whole(wdown)], outs, after, place)


def mlp_last(place, normed, cotangent, weights, hidden, gain, branch, pulled, w_out, parts=(), after=()):
    fetched = len(weights) == 6
    units = 2 * weights[4].shape[0] if fetched else weights[1].shape[0]
    rows, model, tile, row, ins, outs = mlp_specs(normed, cotangent, units)
    block = (tile, model)
    ins = ins + [whole(w) for w in weights]
    ins = ins + [(hidden, block, row), whole(gain), (branch, block, row), (pulled, block, row), whole(w_out)]
    ins = ins + [whole(p) for p in parts]
    outs = outs + [
        (shaped((rows, model)), block, row), (shaped((rows, model), jnp.float32), block, row),
        (shaped((rows, model)), block, row), (shaped((1, model), jnp.float32), (1, model), lambda i: (0, 0)),
    ]
    width = w_out.shape[0]
    outs = outs + [(shaped((rows, width)), (tile, width), row)] * (2 if fetched else 1)
    scratch = [pltpu.VMEM((2, units, model), LOW), pltpu.VMEM((units, model), LOW)] if fetched else []
    return run(
        functools.partial(mlp_last_kernel, fetched), "mlp_last", (rows // tile,), ins, outs, after, place, scratch, vmem=60
    )


def store_halves(value, core, keep, send, index):
    size = value.shape[0] // 2
    low, high = value[:size].astype(LOW), value[size:].astype(LOW)
    if core is None:
        keep[index], send[index] = low, high
    else:
        keep[index] = jnp.where(core == 0, low, high)
        send[index] = jnp.where(core == 0, high, low)


def outer_kernel(own, flags, left, right, keep, send):
    store_halves(rows_dot(left[0], right[...]), flags[0] if own else None, keep, send, 0)


def outer(flags, own, left, right, after=(), side=None):
    sides, rows, units = left.shape
    model = right.shape[1]
    tile = min(512, model)
    first = 0 if side is None else side
    sides = sides if side is None else 1
    out = (shaped((sides, units // 2, model)), (1, units // 2, tile), lambda s, j: (s, 0, j))
    return run(
        functools.partial(outer_kernel, own), "outer", (sides, model // tile),
        [(left, (1, rows, units), lambda s, j: (s + first, 0, 0)), (right, (rows, tile), lambda s, j: (0, j))],
        [out, out], after, flags,
    )


def outer_down_kernel(own, flags, gate, attended, low, hidden, keep, send):
    first, second = rows_dot(gate[0], low[...]), rows_dot(attended[...], hidden[...])
    core = flags[0] if own else None
    size = first.shape[0] // 2
    store_halves(first, core, keep.at[:, :size], send.at[:, :size], 0)
    store_halves(second, core, keep.at[:, size:], send.at[:, size:], 0)


def outer_down(flags, own, gate, attended, low, hidden, after=()):
    _, rows, units = gate.shape
    width, model = attended.shape[1], low.shape[1]
    tile = min(512, model)
    part = lambda j: (0, j)
    out = (shaped((1, (units + width) // 2, model)), (1, (units + width) // 2, tile), lambda j: (0, 0, j))
    return run(
        functools.partial(outer_down_kernel, own), "outer_down", (model // tile,),
        [(gate, (1, rows, units), lambda j: (0, 0, 0)), (attended, (rows, width), lambda j: (0, 0)),
         (low, (rows, tile), part), (hidden, (rows, tile), part)],
        [out, out], after, flags,
    )


def outer_attn_kernel(own, flags, normed, grads, keep, send):
    width = grads.shape[1] // 3
    size = width // 2
    for i in range(3):
        value = rows_dot(normed[...], grads[:, i * width:(i + 1) * width])
        low, high = value[:, :size].astype(LOW), value[:, size:].astype(LOW)
        if own:
            low, high = jnp.where(flags[0] == 0, low, high), jnp.where(flags[0] == 0, high, low)
        keep[i] = low
        send[i] = high


def outer_attn(flags, own, normed, grads, after=()):
    rows, width = grads.shape[0], grads.shape[1] // 3
    model = normed.shape[1]
    tile = min(512, model)
    out = (shaped((3, model, width // 2)), (3, tile, width // 2), lambda i: (0, i, 0))
    return run(
        functools.partial(outer_attn_kernel, own), "outer_attn", (model // tile,),
        [(normed, (rows, tile), lambda i: (0, i)), (grads, (rows, 3 * width), lambda i: (0, 0))],
        [out, out], after, flags,
    )


def trade_kernel(tiles, compute, store, *refs):
    ins, out = refs[:-6], refs[-6]
    keep, send, got, send_sems, got_sems = refs[-5:]
    step = pl.program_id(0)
    me = lax.axis_index("dp")
    other = {"dp": me + 1 - 2 * (me % 2)}

    @pl.when(step == 0)
    def _():
        barrier = pltpu.get_barrier_semaphore()
        pl.semaphore_signal(barrier, inc=1, device_id=other, device_id_type=pl.DeviceIdType.MESH)
        pl.semaphore_wait(barrier, 1)

    def move(tile):
        return pltpu.make_async_remote_copy(
            src_ref=send.at[tile], dst_ref=got.at[tile], send_sem=send_sems.at[tile], recv_sem=got_sems.at[tile],
            device_id=other, device_id_type=pl.DeviceIdType.MESH,
        )

    compute(me % 2, ins, keep.at[step], send.at[step])
    move(step).start()

    @pl.when(step == tiles - 1)
    def _():
        for tile in range(tiles):
            move(tile).wait()
            store(out, tile, keep[tile] + got[tile])


def trade(name, collective, tiles, tile_shape, compute, store, ins, shape, after=()):
    buffer = pltpu.VMEM((tiles,) + tile_shape, LOW)
    return run(
        functools.partial(trade_kernel, tiles, compute, store), name, (tiles,), ins,
        [(shaped(shape), shape, lambda t: (0,) * len(shape))], after,
        scratch=[buffer, buffer, buffer, pltpu.SemaphoreType.DMA((tiles,)), pltpu.SemaphoreType.DMA((tiles,))],
        collective=collective,
    )[0]


def keep_and_send(own, core, value, axis, keep, send, index):
    size = value.shape[axis] // 2
    low = lax.slice_in_dim(value, 0, size, axis=axis).astype(LOW)
    high = lax.slice_in_dim(value, size, 2 * size, axis=axis).astype(LOW)
    if own:
        low, high = jnp.where(core == 0, low, high), jnp.where(core == 0, high, low)
    keep[index] = low
    send[index] = high


def store_columns(count, out, tile, value):
    size = value.shape[-1]
    out[tile // count, :, tile % count * size:(tile % count + 1) * size] = value


def trade_outer(collective, own, left, right, sides, after=()):
    _, rows, units = left.shape
    model = right.shape[1]
    tile, count = min(512, model), model // min(512, model)
    first = sides[0]

    def compute(core, ins, keep, send):
        keep_and_send(own, core, rows_dot(ins[0][0], ins[1][...]), 0, keep, send, slice(None))

    return trade(
        "trade_outer", collective, len(sides) * count, (units // 2, tile), compute, functools.partial(store_columns, count),
        [(left, (1, rows, units), lambda t: (first + t // count, 0, 0)), (right, (rows, tile), lambda t: (0, t % count))],
        (len(sides), units // 2, model), after,
    )


def trade_down(collective, own, gate, attended, low, hidden, after=()):
    _, rows, units = gate.shape
    width, model = attended.shape[1], low.shape[1]
    tile, count = min(512, model), model // min(512, model)
    part = lambda t: (0, t)
    size = units // 2

    def compute(core, ins, keep, send):
        gate, attended, low, hidden = ins
        keep_and_send(own, core, rows_dot(gate[0], low[...]), 0, keep, send, slice(0, size))
        keep_and_send(own, core, rows_dot(attended[...], hidden[...]), 0, keep, send, slice(size, size + width // 2))

    return trade(
        "trade_down", collective, count, (size + width // 2, tile), compute, functools.partial(store_columns, count),
        [(gate, (1, rows, units), lambda t: (0, 0, 0)), (attended, (rows, width), lambda t: (0, 0)),
         (low, (rows, tile), part), (hidden, (rows, tile), part)],
        (1, size + width // 2, model), after,
    )


def trade_attn(collective, own, normed, grads, after=()):
    rows, width = grads.shape[0], grads.shape[1] // 3
    model = normed.shape[1]
    tile, count = min(512, model), model // min(512, model)

    def compute(core, ins, keep, send):
        for i in range(3):
            value = rows_dot(ins[0][...], ins[1][:, i * width:(i + 1) * width])
            keep_and_send(own, core, value, 1, keep, send, i)

    def store(out, t, value):
        out[:, t * tile:(t + 1) * tile] = value

    return trade(
        "trade_attn", collective, count, (3, tile, width // 2), compute, store,
        [(normed, (rows, tile), lambda t: (0, t)), (grads, (rows, 3 * width), lambda t: (0, 0))],
        (3, model, width // 2), after,
    )


def pull_kernel(tokens, hidden_grad, gain, grads, weights, *refs):
    more, parts, (out, gain_ref) = refs[:1], refs[1:-2], refs[-2:]
    width = weights.shape[2]
    total = None
    for i in range(3):
        terms = [cols_dot(grads[:, i * width:(i + 1) * width], weights[i])]
        for side, part in enumerate(parts):
            size = part.shape[2]
            first = i * width + side * size
            terms.append(cols_dot(more[0][:, first:first + size], part[i]))
        for term in terms:
            total = term if total is None else total + term
    back, gain_part = norm_back_rows(tokens[...].astype(jnp.float32), gain[...], total)
    out[...] = hidden_grad[...] + back
    add_gain(gain_ref, gain_part)


def pull(tokens, hidden_grad, gain, grads, weights, more=None, parts=(), after=()):
    rows, model = tokens.shape
    tile = row_tile(rows)
    row = lambda i: (i, 0)
    size = grads.shape[1]
    return run(
        pull_kernel, "pull", (rows // tile,),
        [(tokens, (tile, model), row), (hidden_grad, (tile, model), row), whole(gain), (grads, (tile, size), row), whole(weights)]
        + [(grads if more is None else more, (tile, size), row)]
        + [(p, (3,) + p.shape[1:], lambda i: (0, 0, 0)) for p in parts],
        [(shaped((rows, model), jnp.float32), (tile, model), row), (shaped((1, model), jnp.float32), (1, model), lambda i: (0, 0))],
        after,
    )


def assemble_call(body, mine, other, core, outs, after):
    same = lambda i, s: (0,) * mine.ndim
    return pl.pallas_call(
        lambda *refs: body(*refs[:3], *refs[3 + len(after):]),
        grid_spec=pltpu.PrefetchScalarGridSpec(
            num_scalar_prefetch=1, grid=(2,),
            in_specs=[pl.BlockSpec(mine.shape, same)] * 2 + [pl.BlockSpec(memory_space=pl.ANY)] * len(after),
            out_specs=[
                pl.BlockSpec(block, functools.partial(lambda axis, rank, i, s: tuple((i ^ s[0]) * (d == axis) for d in range(rank)), axis, len(block)))
                for _, block, axis in outs
            ],
        ),
        out_shape=[shaped(shape, jnp.float32) for shape, _, _ in outs],
        compiler_params=pltpu.CompilerParams(vmem_limit_bytes=56 << 20),
        name="assemble",
    )(jnp.reshape(core, (1,)).astype(jnp.int32), mine, other, *after)


def assemble_kernel(side, mine, other, out):
    out[...] = jnp.where(pl.program_id(0) == 0, mine[...], other[...]).astype(jnp.float32)


def assemble(mine, other, core, axis, after=()):
    shape = tuple(2 * n if d == axis else n for d, n in enumerate(mine.shape))
    return assemble_call(assemble_kernel, mine, other, core, [(shape, mine.shape, axis)], after)[0]


def assemble_down_kernel(side, mine, other, down, out):
    chosen = jnp.where(pl.program_id(0) == 0, mine[0], other[0]).astype(jnp.float32)
    size = down.shape[0]
    down[...] = chosen[:size]
    out[...] = chosen[size:]


def assemble_down(mine, other, core, units, after=()):
    _, rows, model = mine.shape
    sizes = (units // 2, rows - units // 2)
    return assemble_call(
        assemble_down_kernel, mine, other, core, [((2 * n, model), (n, model), 0) for n in sizes], after
    )


class Links:
    def __init__(self, dp, tensor):
        self.dp, self.tensor = dp, tensor
        self.id = lax.axis_index("dp")
        self.core, self.row = self.id % 2, self.id // 2 % 2

    def send(self, value, target):
        pairs = [
            (d * self.tensor + t, to)
            for d in range(self.dp) for t in range(self.tensor)
            for to in [target(d, t)] if to is not None
        ]
        return lax.ppermute(value, AXES, pairs)

    def cross(self, value):
        return self.send(value, lambda d, t: d * self.tensor + (1 - t))

    def flip(self, value, even, odd=None):
        bits = (even, even if odd is None else odd)
        return self.send(value, lambda d, t: (d ^ bits[d % 2]) * self.tensor + t)

    def shift(self, value, by):
        return self.send(value, lambda d, t: d * self.tensor + t + by if 0 <= t + by < self.tensor else None)

    def bit_of(self, even, odd):
        return jnp.where(self.core == 0, (self.id & even) // even, (self.id & odd) // odd)


def tie(value, *others):
    return lax.optimization_barrier((value,) + others)[0]


def half(value, index, axis):
    size = value.shape[axis] // 2
    if isinstance(index, int):
        return lax.slice_in_dim(value, index * size, (index + 1) * size, axis=axis)
    return lax.dynamic_slice_in_dim(value, index * size, size, axis)


def order(bit, first, second, axis):
    return jnp.where(bit == 0, jnp.concatenate([first, second], axis), jnp.concatenate([second, first], axis))


class Summing:
    ROW_FIRST = ((2, 2, 1), (4, 4, 2), (8, 8, 3))
    SPLIT = ((2, 4, 4), (4, 8, 5), (8, 2, 6))

    def __init__(self, links, flags, axis, steps):
        self.links, self.flags, self.axis, self.steps = links, flags, axis, steps

    def send_far(self, far):
        self.far, self.crossed = far, self.links.cross(far)

    def across(self, *after, parts=None):
        self.split(0, self.near, self.crossed if parts is None else jnp.concatenate(parts, 0), after)

    def split(self, step, a, b, after):
        even, odd, which = self.steps[step]
        a, bit = tie(a, *after), self.flags[which]
        part = lambda k: half(a, k, self.axis) + half(b, k, self.axis)
        self.held, self.moved = part(bit), self.links.flip(part(1 - bit), even, odd)

    def scatter(self, *after):
        self.split(1, self.held, self.moved, after)

    def both(self, *after):
        self.held = tie(self.held, *after) + self.moved
        self.moved = self.links.flip(self.held, *self.steps[2][:2])

    def both_add(self, *after):
        self.held = tie(self.held, *after) + self.moved
        self.moved = self.links.flip(self.held, *self.steps[1][:2])

    def gather(self, *after):
        self.held = order(self.flags[self.steps[1][2]], tie(self.held, *after), self.moved, self.axis)
        self.moved = self.links.flip(self.held, *self.steps[0][:2])

    def last(self, *after):
        self.held = order(self.flags[self.steps[0][2]], tie(self.held, *after), self.moved, self.axis)
        self.moved = self.links.flip(self.held, 1)
        return self.held, self.moved, self.links.core


def on_device(tokens, lengths, order_, gain_attn, w_qkv, w_out, gain_mlp, w_in, w_down, cotangent):
    rows, model = tokens.shape
    dp, tensor = lax.axis_size("dp"), lax.axis_size("tensor")
    tensor_id = lax.axis_index("tensor")
    links = Links(dp, tensor)
    paired = tensor == 2 and dp == 16

    slot_count = rows * tensor // MAXLEN
    my_order = lax.dynamic_slice_in_dim(order_, links.id * slot_count, slot_count, 0)
    chosen = my_order[:, None] == jnp.arange(lengths.shape[0], dtype=jnp.int32)[None, :]
    slot_len = jnp.sum(jnp.where(chosen, lengths[None, :], 0), 1)
    slots = jnp.arange(slot_count, dtype=jnp.int32)[None, :]
    block_row = tensor_id * rows + BQ * jnp.arange(rows // BQ, dtype=jnp.int32)
    block_len = jnp.sum(jnp.where((block_row // MAXLEN)[:, None] == slots, slot_len[None, :], 0), 1)
    place = jnp.stack([block_row % MAXLEN, block_len])

    w_qkv = w_qkv.transpose(1, 0, 2)
    w_in = w_in.transpose(1, 2, 0)
    gain_attn, gain_mlp = gain_attn[None], gain_mlp[None]
    if not paired:
        before, after = links.shift(tokens[rows - HALF:], 1), links.shift(tokens[:HALF], -1)
        return general(
            links, place, tokens, before, after, gain_attn, w_qkv, w_out, gain_mlp, w_in, w_down, cotangent
        )

    start = jnp.where(tensor_id == 0, rows - HALF, 0)
    border = links.cross(lax.dynamic_slice_in_dim(tokens, start, HALF, 0))
    core = links.core
    bits = [links.id // bit % 2 for bit in (1, 2, 4, 8)]
    split_bits = [jnp.where(core == 0, bits[i], bits[j]) for i, j in ((1, 2), (2, 3), (3, 1))]
    flags = jnp.stack(bits + split_bits).astype(jnp.int32)
    place = jnp.concatenate([place, jnp.pad(flags, (0, place.shape[1] - flags.shape[0]))[None]], 0)
    width, units = w_out.shape[0], w_down.shape[0]
    size = width // 2
    out_half = half(tie(w_out, border), core, 0)
    stacked = jnp.concatenate([out_half[:, k * size:(k + 1) * size] for k in range(model // size)], 0)
    piece = jnp.concatenate([half(tie(w_qkv, border), core, 2), stacked[None]], 0)
    attn_direct = links.cross(piece)

    normed = norm_rows(tokens, border, border, gain_attn)
    quarter = lambda w, a, b: half(half(w, core, a), bits[1], b)
    in_piece = quarter(tie(w_in, normed), 1, 2)
    in_direct = links.cross(in_piece)
    down_direct = links.cross(half(tie(w_down, in_piece), core, 0))
    q0, k0, v0 = project(normed, w_qkv)
    attended0, logs0 = attend(place, q0, k0, v0)
    attn_parts = (attn_direct, links.flip(tie(attn_direct, attended0), 1))
    q1, k1, v1 = project_parts(normed, attn_parts, after=[attended0])
    attended1, logs1 = attend(place, q1, k1, v1)
    hidden, normed_mlp = mix(tokens, gain_mlp, attended0, w_out, attended1, attn_parts)
    in_direct = tie(in_direct, hidden)
    in_relayed = links.flip(in_direct, 2)
    in_core = links.flip(in_direct, 1)
    gate0, lift0, out_low, branch, pulled = mlp_first(place, normed_mlp, cotangent, w_in, w_down, after=[in_direct])
    in_relayed = tie(in_relayed, branch)
    down_direct = tie(down_direct, branch)
    weights = (
        in_direct, in_relayed, in_core, links.flip(in_relayed, 1), down_direct, links.flip(down_direct, 1),
    )
    gate1, lift1, output, hidden_grad, hidden_low, gain_mlp_grad, back0, back1 = mlp_last(
        place, normed_mlp, cotangent, weights, hidden, gain_mlp, branch, pulled, w_out, attn_parts
    )
    inner = Summing(links, flags, 2, Summing.ROW_FIRST)
    inner_a, inner_b = (Summing(links, flags, 2, Summing.ROW_FIRST) for _ in range(2))
    down = Summing(links, flags, 2, Summing.SPLIT)
    attn = Summing(links, flags, 1, Summing.SPLIT)

    inner_a.send_far(trade_outer(0, False, lift1, normed_mlp, [0], after=[back1]))
    inner_b.send_far(trade_outer(1, False, lift1, normed_mlp, [1], after=[inner_a.far]))
    inner.near = trade_outer(2, True, lift0, normed_mlp, [0, 1], after=[inner_b.far])

    swap = lambda e: jnp.where(core == 0, e, jnp.concatenate([e[:, size:], e[:, :size]], 1))

    def trade_edge(edge):
        chosen = jnp.where(tensor_id == 0, edge[1], edge[0])
        return links.cross(jnp.concatenate([swap(chosen[:, :width]), swap(chosen[:, width:])], 1))

    def add_edge(d, edge):
        held = lax.dynamic_slice(d, (start, width), (HALF, 2 * width))
        return lax.dynamic_update_slice(d, held + edge, (start, width))

    d0, edge0 = attend_back(place, q0, k0, v0, back0, logs0, after=[inner.near])
    edge_other = trade_edge(edge0)
    far = trade_down(3, False, gate1, attended1, out_low, hidden_low, after=[d0, inner_a.crossed])
    down.send_far(tie(far, edge_other))
    inner.across(down.far, parts=[inner_a.crossed, inner_b.crossed])
    d1, edge1 = attend_back(place, q1, k1, v1, back1, logs1, after=[inner.held])
    edge_own = trade_edge(edge1)
    d1 = add_edge(d1, edge_other)
    far = trade_attn(5, False, normed, d1)
    inner.scatter(far)
    attn.send_far(tie(far, edge_own))
    down.near = trade_down(4, True, gate0, attended0, out_low, hidden_low, after=[inner.held])
    inner.both(down.near)
    down.across(inner.held)
    d0 = add_edge(tie(d0, down.held), edge_own)
    attn.near = trade_attn(6, True, normed, d0)
    down.scatter(attn.near)
    inner.both_add(down.held)
    attn.across(inner.held)
    input_grad, gain_attn_grad = pull(tokens, hidden_grad, gain_attn, d0, w_qkv, d1, attn_parts, after=[attn.held])
    gain_total = jnp.concatenate((gain_attn_grad, gain_mlp_grad))
    inner.gather(input_grad)
    down.both(inner.held)
    attn.scatter(down.held)
    gain_total = gain_total + tie(links.cross(gain_total), attn.held)
    down.both_add(attn.held)
    attn.both(down.held)
    gain_total = gain_total + tie(links.flip(gain_total, 1), attn.held)
    down.gather(attn.held)
    attn.both_add(down.held)
    grads_in = inner.last(attn.held)
    grads_down = down.last(grads_in[0])
    gain_total = gain_total + tie(links.flip(gain_total, 2), grads_down[0])
    attn.gather(grads_down[0])
    grad_w_in = assemble(*grads_in, 1, after=[attn.held, gain_total])
    gain_total = gain_total + tie(links.flip(gain_total, 4), grad_w_in)
    grads_attn = attn.last(grad_w_in)
    grad_w_down, grad_w_out = assemble_down(*grads_down, units, after=[grads_attn[0], gain_total])
    gain_total = gain_total + tie(links.flip(gain_total, 8), grad_w_down)
    grad_w_qkv = assemble(*grads_attn, 2, after=[grad_w_down])
    return (
        output,
        input_grad,
        gain_total[0],
        grad_w_qkv.transpose(1, 0, 2),
        grad_w_out,
        gain_total[1],
        grad_w_in.transpose(2, 0, 1),
        grad_w_down,
    )


def general(links, place, tokens, before, after, gain_attn, w_qkv, w_out, gain_mlp, w_in, w_down, cotangent):
    rows = tokens.shape[0]
    w_qkv, w_out, w_in, w_down = (
        lax.all_gather(w, "tensor", axis=axis, tiled=True)
        for w, axis in ((w_qkv, 2), (w_out, 0), (w_in, 1), (w_down, 0))
    )
    normed = norm_rows(tokens, before, after, gain_attn)
    q, k, v = project(normed, w_qkv)
    attended, logs = attend(place, q, k, v)
    hidden, normed_mlp = mix(tokens, gain_mlp, attended, w_out)
    blank = jnp.zeros_like(hidden)
    gate, lift, output, hidden_grad, hidden_low, gain_mlp_grad, back = mlp_last(
        place, normed_mlp, cotangent, (w_in, w_down), hidden, gain_mlp, blank, blank, w_out
    )
    position = jnp.repeat(place[0], BQ) + jnp.tile(jnp.arange(BQ, dtype=jnp.int32), place.shape[1])
    out_low = jnp.where((position < jnp.repeat(place[1], BQ))[:, None], cotangent, jnp.zeros_like(cotangent))
    flags = jnp.zeros((1,), jnp.int32)
    units, width = w_down.shape[0], w_out.shape[0]
    low, high = outer_down(flags, False, gate, attended, out_low, hidden_low)
    down = jnp.concatenate([low[0, :units // 2], high[0, :units // 2]], 0)
    out = jnp.concatenate([low[0, units // 2:], high[0, units // 2:]], 0)
    inner = jnp.concatenate(outer(flags, False, lift, normed_mlp), 1)
    d, edge = attend_back(place, q, k, v, back, logs)
    d = d.at[:HALF, width:].add(links.shift(edge[1], 1)).at[rows - HALF:, width:].add(links.shift(edge[0], -1))
    qkv = jnp.concatenate(outer_attn(flags, False, normed, d), 2)
    input_grad, gain_attn_grad = pull(tokens, hidden_grad, gain_attn, d, w_qkv)
    down, inner, out, qkv = (
        lax.psum(lax.psum_scatter(g, "tensor", scatter_dimension=axis, tiled=True), "dp").astype(jnp.float32)
        for g, axis in ((down, 0), (inner, 1), (out, 0), (qkv, 2))
    )
    gain_total = lax.psum(jnp.concatenate((gain_attn_grad, gain_mlp_grad)), AXES)
    return (
        output, input_grad, gain_total[0], qkv.transpose(1, 0, 2), out, gain_total[1],
        inner.transpose(2, 0, 1), down,
    )


def solution(mesh):
    split = P(AXES, None)
    wide = P(None, None, "tensor")
    tall = P("tensor", None)
    return jax.shard_map(
        on_device,
        mesh=mesh,
        in_specs=(split, P(), P(), P(), wide, tall, P(), wide, tall, split),
        out_specs=(split, split, P(), wide, tall, P(), wide, tall),
        check_vma=False,
    )
```

```python
import functools
import math

import jax
import jax.numpy as jnp
from jax import lax
from jax.experimental import pallas as pl
from jax.experimental.pallas import tpu as pltpu
from jax.sharding import PartitionSpec as P

AXES = ("dp", "tensor")
EPS = 1e-05
HEAD_DIM = 64
HALF = 64
MAXLEN = 1024
BQ = 128
LOW = jnp.bfloat16
NEG = -1e30


def cols_dot(left, right):
    return lax.dot_general(left, right, (((1,), (1,)), ((), ())), preferred_element_type=jnp.float32)


def rows_dot(left, right):
    return lax.dot_general(left, right, (((0,), (0,)), ((), ())), preferred_element_type=jnp.float32)


def plain_dot(left, right):
    return lax.dot_general(left, right, (((1,), (0,)), ((), ())), preferred_element_type=jnp.float32)


def norm_parts(values):
    center = values - jnp.mean(values, -1, keepdims=True)
    rate = lax.rsqrt(jnp.mean(center * center, -1, keepdims=True) + EPS)
    return center * rate, rate


COST = {
    "norm_rows": 6, "project": 9, "project_parts": 9, "attend": 20, "mix": 11, "mlp_first": 39, "mlp_last": 49, "outer": 9,
    "attend_back": 25, "trade_outer": 9, "trade_down": 12, "trade_attn": 10, "outer_down": 12, "outer_attn": 10, "pull": 18,
}
SCALE = 100


def shaped(shape, dtype=LOW):
    return jax.ShapeDtypeStruct(shape, dtype)


def run(body, name, grid, ins, outs, after=(), place=None, scratch=(), flops=0, vmem=56, seen=False, collective=None):
    extra = [a for a in after if a is not None]
    count = len(ins)

    def kernel(*refs):
        lead = refs[:1] if place is not None else ()
        refs = refs[len(lead):]
        body(*lead, *refs[:count], *refs[count + len(extra):])

    def spec(block, index):
        if place is not None and not seen:
            return pl.BlockSpec(block, lambda *a: index(*a[:-1]))
        return pl.BlockSpec(block, index)

    call = pl.pallas_call(
        kernel,
        grid_spec=pltpu.PrefetchScalarGridSpec(
            num_scalar_prefetch=0 if place is None else 1,
            grid=grid,
            in_specs=[spec(b, m) for _, b, m in ins] + [pl.BlockSpec(memory_space=pl.ANY)] * len(extra),
            out_specs=[spec(b, m) for _, b, m in outs],
            scratch_shapes=list(scratch),
        ),
        out_shape=[s for s, _, _ in outs],
        compiler_params=pltpu.CompilerParams(
            vmem_limit_bytes=vmem << 20, collective_id=collective, has_side_effects=collective is not None
        ),
        cost_estimate=pl.CostEstimate(flops=int(COST[name] * SCALE), bytes_accessed=1000, transcendentals=0),
        name=name,
    )
    lead = () if place is None else (place,)
    return call(*lead, *[a for a, _, _ in ins], *extra)


def window_masks(shared, ones, pos0, length):
    j = lax.broadcasted_iota(jnp.int32, (BQ, 2 * BQ), 0)
    i = lax.broadcasted_iota(jnp.int32, (BQ, 2 * BQ), 1) % BQ

    @pl.when(pl.program_id(0) == 0)
    def _():
        shared[0] = j + jnp.where(i <= j, 0, BQ)
        shared[1] = jnp.where(j == (i + HALF) % BQ, 1, 0)
        ones[0] = jnp.where(i <= j, 1.0, 0.0).astype(LOW)
        ones[1] = jnp.where(i == j, 1.0, 0.0).astype(LOW)

    key = shared[0]
    top = jnp.minimum(length, MAXLEN)
    bias = jnp.where(((key >= HALF - pos0) & (key < top - pos0 + HALF)) | (shared[1] > 0), 0.0, NEG)
    lane = lax.broadcasted_iota(jnp.int32, (1, 2 * BQ), 1) % BQ
    last_bias = jnp.where(pos0 + HALF + lane < top, 0.0, NEG)
    return key < BQ, i == j, bias, last_bias


def split_heads(pair):
    lane = lax.broadcasted_iota(jnp.int32, pair.shape, 1)
    zero = jnp.zeros_like(pair)
    return jnp.concatenate([jnp.where(lane < HEAD_DIM, pair, zero), jnp.where(lane >= HEAD_DIM, pair, zero)], 0)


def join_heads(wide, scale=None):
    first, second = wide[:HEAD_DIM, :BQ], wide[HEAD_DIM:, BQ:]
    if scale is not None:
        first, second = first * scale[:, :BQ], second * scale[:, BQ:]
    return jnp.concatenate([first, second], 0).T


def fold(near, diag, wide):
    low = wide[BQ:]
    return jnp.where(near, wide[:BQ], low), jnp.sum(jnp.where(diag, low, 0.0), 0, keepdims=True)


def unfold(ones, tile, last):
    tile = tile.astype(LOW)
    upper = tile * ones[0]
    return jnp.concatenate([upper, (tile - upper) + ones[1] * last.astype(LOW)], 0)


def window_rows(before, here, after, c):
    return jnp.concatenate([before[:, c], here[:, c], after[:, c]], 0)


def attend_kernel(place, q, kb, kh, ka, vb, vh, va, out_ref, log_ref, shared, ones):
    blk = pl.program_id(0)
    near, diag, bias, last_bias = window_masks(shared, ones, place[0, blk], place[1, blk])
    columns = [slice(p * BQ, (p + 1) * BQ) for p in range(out_ref.shape[1] // BQ)]

    def score(c):
        return cols_dot(window_rows(kb, kh, ka, c), split_heads(q[:, c] * 0.125))

    def soft(wide):
        scores, last = fold(near, diag, wide)
        scores, last = scores + bias, last + last_bias
        row_max = jnp.maximum(jnp.max(scores, 0, keepdims=True), last)
        expons, last = jnp.exp(scores - row_max), jnp.exp(last - row_max)
        summed = jnp.sum(expons, 0, keepdims=True) + last
        return unfold(ones, expons, last), row_max, summed

    wides = [score(c) for c in columns]
    softs = [soft(w) for w in wides]
    for pair, c in enumerate(columns):
        probs, row_max, summed = softs[pair]
        out_ref[:, c] = join_heads(rows_dot(window_rows(vb, vh, va, c), probs), 1.0 / summed).astype(LOW)
        log_ref[0, pair:pair + 1] = row_max + jnp.log(summed)


def attend_back_kernel(place, q, kb, kh, ka, vb, vh, va, g_ref, log_ref, d_ref, edge_ref, carry, tail, dq_keep, shared, ones):
    step = pl.program_id(0)
    steps = pl.num_programs(0)
    width = g_ref.shape[1]

    @pl.when(step == 0)
    def _():
        carry[...] = jnp.zeros_like(carry)
        tail[...] = jnp.zeros_like(tail)
        dq_keep[...] = jnp.zeros_like(dq_keep)

    d_ref[:, :width] = dq_keep[...]
    d_ref[:HALF, width:] = tail[...]

    @pl.when(step < steps - 1)
    def _():
        near, diag, bias, last_bias = window_masks(shared, ones, place[0, step], place[1, step])
        columns = [slice(p * BQ, (p + 1) * BQ) for p in range(width // BQ)]

        def start(c):
            queries = split_heads(q[:, c] * 0.125)
            grads = split_heads(g_ref[:, c])
            keyset = window_rows(kb, kh, ka, c)
            return queries, grads, keyset, cols_dot(keyset, queries), cols_dot(window_rows(vb, vh, va, c), grads)

        starts = [start(c) for c in columns]
        for pair, c in enumerate(columns):
            ready = starts[pair]
            v = slice(width + c.start, width + c.stop)
            queries, grads, keyset, wide, wide_grad = ready
            log_row = log_ref[0, pair:pair + 1]
            scores, last = fold(near, diag, wide)
            expons, last = jnp.exp(scores + (bias - log_row)), jnp.exp(last + (last_bias - log_row))
            prob_grad, last_grad = fold(near, diag, wide_grad)
            inner = jnp.sum(expons * prob_grad, 0, keepdims=True) + last * last_grad
            score_grad = unfold(ones, expons * (prob_grad - inner), last * (last_grad - inner))
            probs = unfold(ones, expons, last)
            dq_keep[:, c] = join_heads(rows_dot(keyset, score_grad) * 0.125).astype(LOW)
            for lanes, grad in ((c, plain_dot(score_grad, queries)), (v, plain_dot(probs, grads))):
                done = (carry[:, lanes] + grad[:BQ]).astype(LOW)
                carry[:, lanes] = grad[BQ:]
                d_ref[HALF:, lanes.start + width:lanes.stop + width] = done[:HALF]
                tail[:, lanes] = done[HALF:]

        @pl.when(step == 0)
        def _():
            edge_ref[0] = d_ref[HALF:, width:]

    @pl.when(step == steps - 1)
    def _():
        done = carry[...].astype(LOW)
        d_ref[HALF:, width:] = done[:HALF]
        edge_ref[1] = done[HALF:]


def window_specs(q, k, v, blocks):
    last, width = blocks - 1, k.shape[1]
    here = lambda b: (jnp.minimum(b, last), 0)
    before = lambda b: (jnp.where(b == 0, 2 * blocks, 2 * jnp.minimum(b, last) - 1), 0)
    after = lambda b: (jnp.where(b >= last, 2 * blocks + 1, 2 * b + 2), 0)
    specs = [(q, (BQ, width), here)]
    for value in (k, v):
        specs += [(value, (HALF, width), before), (value, (BQ, width), here), (value, (HALF, width), after)]
    return specs


def attend(place, q, k, v, after=()):
    blocks, width = k.shape[0] // BQ - 1, k.shape[1]
    pairs = width // BQ
    return run(
        attend_kernel, "attend", (blocks,), window_specs(q, k, v, blocks),
        [
            (shaped((blocks * BQ, width)), (BQ, width), lambda b: (b, 0)),
            (shaped((blocks, pairs, 2 * BQ), jnp.float32), (1, pairs, 2 * BQ), lambda b: (b, 0, 0)),
        ],
        after, place, scratch=[pltpu.VMEM((2, BQ, 2 * BQ), jnp.int32), pltpu.VMEM((2, BQ, 2 * BQ), LOW)],
    )


def attend_back(place, q, k, v, grads, logs, after=()):
    blocks, width = grads.shape[0] // BQ, k.shape[1]
    pairs = width // BQ
    last = blocks - 1
    return run(
        attend_back_kernel, "attend_back", (blocks + 1,),
        window_specs(q, k, v, blocks)
        + [
            (grads, (BQ, width), lambda b: (jnp.minimum(b, last), 0)),
            (logs, (1, pairs, 2 * BQ), lambda b: (jnp.minimum(b, last), 0, 0)),
        ],
        [
            (shaped((blocks * BQ, 3 * width)), (BQ, 3 * width), lambda b: (jnp.maximum(b - 1, 0), 0)),
            (shaped((2, HALF, 2 * width)), (2, HALF, 2 * width), lambda b: (0, 0, 0)),
        ],
        after, place,
        scratch=[
            pltpu.VMEM((BQ, 2 * width), jnp.float32),
            pltpu.VMEM((HALF, 2 * width), LOW),
            pltpu.VMEM((BQ, width), LOW),
            pltpu.VMEM((2, BQ, 2 * BQ), jnp.int32),
            pltpu.VMEM((2, BQ, 2 * BQ), LOW),
        ],
        flops=blocks * pairs * BQ * BQ * BQ * 512,
    )


def norm_kernel(tokens, before, after, gain, out):
    step, tile = pl.program_id(0), tokens.shape[0]

    @pl.when(step < pl.num_programs(0) - 1)
    def _():
        out[...] = (norm_parts(tokens[...].astype(jnp.float32))[0] * gain[...]).astype(LOW)

    @pl.when(step == pl.num_programs(0) - 1)
    def _():
        values = jnp.concatenate([before[...], after[...]], 0).astype(jnp.float32)
        out[:BQ] = (norm_parts(values)[0] * gain[...]).astype(LOW)


def norm_rows(tokens, before, after, gain):
    rows, model = tokens.shape
    tile = 3 * BQ
    blocks = rows // tile
    full = lambda i: (0, 0)
    return run(
        norm_kernel, "norm_rows", (blocks + 1,),
        [
            (tokens, (tile, model), lambda i: (jnp.minimum(i, blocks - 1), 0)),
            (before, (HALF, model), full), (after, (HALF, model), full), (gain, (1, model), full),
        ],
        [(shaped((rows + BQ, model)), (tile, model), lambda i: (i, 0))],
    )[0]


def project_kernel(normed, weights, *outs):
    for i, out in enumerate(outs):
        out[...] = plain_dot(normed[...], weights[i]).astype(LOW)


def project(normed, weights, after=()):
    rows, model = normed.shape
    width = weights.shape[2]
    tile = rows // 4 if rows % 64 == 0 else rows
    return run(
        project_kernel, "project", (rows // tile,),
        [(normed, (tile, model), lambda i: (i, 0)), (weights, (3, model, width), lambda i: (0, 0, 0))],
        [(shaped((rows, width)), (tile, width), lambda i: (i, 0))] * 3,
        after, flops=6 * rows * model * width,
    )


def project_parts_kernel(normed, mine, other, *outs):
    size = mine.shape[2]
    for i, out in enumerate(outs):
        out[:, :size] = plain_dot(normed[...], mine[i]).astype(LOW)
        out[:, size:] = plain_dot(normed[...], other[i]).astype(LOW)


def project_parts(normed, parts, after=()):
    rows, model = normed.shape
    size = parts[0].shape[2]
    tile = rows // 4
    return run(
        project_parts_kernel, "project_parts", (rows // tile,),
        [(normed, (tile, model), lambda i: (i, 0))] + [(p, (3, model, size), lambda i: (0, 0, 0)) for p in parts],
        [(shaped((rows, 2 * size)), (tile, 2 * size), lambda i: (i, 0))] * 3,
        after,
    )


def row_tile(rows):
    return 256 if rows % 256 == 0 else 128


def keep_rows(place, step, tile):
    row = lax.broadcasted_iota(jnp.int32, (BQ, 1), 0)
    parts = []
    for i in range(tile // BQ):
        b = step * (tile // BQ) + i
        parts.append(jnp.where(row + place[0, b] < place[1, b], 1.0, 0.0))
    return jnp.concatenate(parts, 0)


def mix_kernel(tokens, gain, attended, weights, *refs):
    attended_more, parts, (hidden, normed) = refs[:1], refs[1:-2], refs[-2:]
    total = tokens[...].astype(jnp.float32) + plain_dot(attended[...], weights[...])
    for side, part in enumerate(parts):
        size = part.shape[0]
        total = total + plain_dot(attended_more[0][:, side * size:(side + 1) * size], part[...])
    hidden[...] = total
    normed[...] = (norm_parts(total)[0] * gain[...]).astype(LOW)


def mix(tokens, gain, attended, weights, more=None, parts=(), after=()):
    rows, model = tokens.shape
    tile = row_tile(rows)
    row, full = (lambda i: (i, 0)), (lambda i: (0, 0))
    width = weights.shape[0]
    return run(
        mix_kernel, "mix", (rows // tile,),
        [(tokens, (tile, model), row), (gain, (1, model), full), (attended, (tile, width), row), (weights, weights.shape, full)]
        + [(attended if more is None else more, (tile, width), row)]
        + [whole(p) for p in parts],
        [(shaped((rows, model), jnp.float32), (tile, model), row), (shaped((rows, model)), (tile, model), row)],
        after,
    )


def gelu_parts(value):
    size = jnp.abs(value)
    bell = jnp.exp(-0.5 * value * value)
    t = 1.0 / (1.0 + (0.3275911 * 2.0 ** -0.5) * size)
    series = t * (0.254829592 + t * (-0.284496736 + t * (1.421413741 + t * (-1.453152027 + t * 1.061405429))))
    tail = 0.5 * series * bell
    below = jnp.where(value < 0, tail, 1.0 - tail)
    return value * below, below + value * bell * ((2.0 * math.pi) ** -0.5)


def mlp_body(place, normed, cotangent, win, wdown, gate_ref, lift_ref):
    tile = normed.shape[0]
    kept = keep_rows(place, pl.program_id(0), tile)
    out_grad = kept * cotangent[...].astype(jnp.float32)
    out_low = out_grad.astype(LOW)
    first = cols_dot(normed[...], win[0])
    second = cols_dot(normed[...], win[1])
    gelu, slope = gelu_parts(first)
    gate = (gelu * second).astype(LOW)
    gate_ref[0] = gate
    branch = plain_dot(gate, wdown[...])
    grad = cols_dot(out_low, wdown[...])
    lift1 = (grad * second * slope).astype(LOW)
    lift2 = (grad * gelu).astype(LOW)
    lift_ref[0] = lift1
    lift_ref[1] = lift2
    pulled = plain_dot(lift1, win[0]) + plain_dot(lift2, win[1])
    return kept, out_grad, out_low, branch, pulled


def mlp_first_kernel(place, normed, cotangent, win, wdown, gate_ref, lift_ref, low_ref, branch_ref, pulled_ref):
    _, _, out_low, branch, pulled = mlp_body(place, normed, cotangent, win, wdown, gate_ref, lift_ref)
    low_ref[...] = out_low
    branch_ref[...] = branch
    pulled_ref[...] = pulled


def norm_back_rows(values, gain, grad):
    unit, rate = norm_parts(values)
    pulled = grad * gain
    mean_one = jnp.mean(pulled, -1, keepdims=True)
    mean_two = jnp.mean(pulled * unit, -1, keepdims=True)
    return rate * (pulled - mean_one - unit * mean_two), jnp.sum(grad * unit, 0, keepdims=True)


def add_gain(gain_ref, part):
    @pl.when(pl.program_id(0) == 0)
    def _():
        gain_ref[...] = jnp.zeros_like(gain_ref)

    gain_ref[...] += part


def mlp_last_kernel(fetched, place, normed, cotangent, *refs):
    if fetched:
        pieces, refs = refs[:6], refs[6:]
        win, wdown = refs[-2:]

        @pl.when(pl.program_id(0) == 0)
        def _():
            units, model = pieces[0].shape[1:]
            for part in range(4):
                rows = slice(part // 2 * units, (part // 2 + 1) * units)
                columns = pl.ds(pl.multiple_of((place[2, 1] ^ (part % 2)) * model, model), model)
                for side in range(2):
                    win[side, rows, columns] = pieces[part][side]
            for side in range(2):
                wdown[side * units:(side + 1) * units] = pieces[4 + side][...]
    else:
        (win, wdown), refs = refs[:2], refs[2:]
    hidden, gain, branch_in, pulled_in, weights = refs[:5]
    parts, refs = (refs[5:7], refs[7:]) if fetched else ((), refs[5:])
    gate_ref, lift_ref, out_ref, grad_ref, low_ref, gain_ref, attn = refs[:7]
    kept, out_grad, _, branch, pulled = mlp_body(place, normed, cotangent, win, wdown, gate_ref, lift_ref)
    out_ref[...] = (kept * (hidden[...] + (branch_in[...] + branch))).astype(LOW)
    back, gain_part = norm_back_rows(hidden[...], gain[...], pulled_in[...] + pulled)
    total = out_grad + back
    grad_ref[...] = total
    low = total.astype(LOW)
    low_ref[...] = low
    attn[...] = cols_dot(low, weights[...]).astype(LOW)
    for side, part in enumerate(parts):
        size = part.shape[0]
        refs[7][:, side * size:(side + 1) * size] = cols_dot(low, part[...]).astype(LOW)
    add_gain(gain_ref, gain_part)


def mlp_specs(normed, cotangent, units):
    rows, model = normed.shape
    tile = row_tile(rows)
    row = lambda i: (i, 0)
    ins = [(normed, (tile, model), row), (cotangent, (tile, model), row)]
    outs = [
        (shaped((1, rows, units)), (1, tile, units), lambda i: (0, i, 0)),
        (shaped((2, rows, units)), (2, tile, units), lambda i: (0, i, 0)),
    ]
    return rows, model, tile, row, ins, outs


def whole(value):
    return (value, value.shape, lambda i: (0,) * value.ndim)


def mlp_first(place, normed, cotangent, win, wdown, after=()):
    rows, model, tile, row, ins, outs = mlp_specs(normed, cotangent, wdown.shape[0])
    outs = outs + [(shaped((rows, model)), (tile, model), row)]
    outs = outs + [(shaped((rows, model), jnp.float32), (tile, model), row)] * 2
    return run(mlp_first_kernel, "mlp_first", (rows // tile,), ins + [whole(win), whole(wdown)], outs, after, place)


def mlp_last(place, normed, cotangent, weights, hidden, gain, branch, pulled, w_out, parts=(), after=()):
    fetched = len(weights) == 6
    units = 2 * weights[4].shape[0] if fetched else weights[1].shape[0]
    rows, model, tile, row, ins, outs = mlp_specs(normed, cotangent, units)
    block = (tile, model)
    ins = ins + [whole(w) for w in weights]
    ins = ins + [(hidden, block, row), whole(gain), (branch, block, row), (pulled, block, row), whole(w_out)]
    ins = ins + [whole(p) for p in parts]
    outs = outs + [
        (shaped((rows, model)), block, row), (shaped((rows, model), jnp.float32), block, row),
        (shaped((rows, model)), block, row), (shaped((1, model), jnp.float32), (1, model), lambda i: (0, 0)),
    ]
    width = w_out.shape[0]
    outs = outs + [(shaped((rows, width)), (tile, width), row)] * (2 if fetched else 1)
    scratch = [pltpu.VMEM((2, units, model), LOW), pltpu.VMEM((units, model), LOW)] if fetched else []
    return run(
        functools.partial(mlp_last_kernel, fetched), "mlp_last", (rows // tile,), ins, outs, after, place, scratch, vmem=60
    )


def store_halves(value, core, keep, send, index):
    size = value.shape[0] // 2
    low, high = value[:size].astype(LOW), value[size:].astype(LOW)
    if core is None:
        keep[index], send[index] = low, high
    else:
        keep[index] = jnp.where(core == 0, low, high)
        send[index] = jnp.where(core == 0, high, low)


def outer_kernel(own, flags, left, right, keep, send):
    store_halves(rows_dot(left[0], right[...]), flags[0] if own else None, keep, send, 0)


def outer(flags, own, left, right, after=(), side=None):
    sides, rows, units = left.shape
    model = right.shape[1]
    tile = min(512, model)
    first = 0 if side is None else side
    sides = sides if side is None else 1
    out = (shaped((sides, units // 2, model)), (1, units // 2, tile), lambda s, j: (s, 0, j))
    return run(
        functools.partial(outer_kernel, own), "outer", (sides, model // tile),
        [(left, (1, rows, units), lambda s, j: (s + first, 0, 0)), (right, (rows, tile), lambda s, j: (0, j))],
        [out, out], after, flags,
    )


def outer_down_kernel(own, flags, gate, attended, low, hidden, keep, send):
    first, second = rows_dot(gate[0], low[...]), rows_dot(attended[...], hidden[...])
    core = flags[0] if own else None
    size = first.shape[0] // 2
    store_halves(first, core, keep.at[:, :size], send.at[:, :size], 0)
    store_halves(second, core, keep.at[:, size:], send.at[:, size:], 0)


def outer_down(flags, own, gate, attended, low, hidden, after=()):
    _, rows, units = gate.shape
    width, model = attended.shape[1], low.shape[1]
    tile = min(512, model)
    part = lambda j: (0, j)
    out = (shaped((1, (units + width) // 2, model)), (1, (units + width) // 2, tile), lambda j: (0, 0, j))
    return run(
        functools.partial(outer_down_kernel, own), "outer_down", (model // tile,),
        [(gate, (1, rows, units), lambda j: (0, 0, 0)), (attended, (rows, width), lambda j: (0, 0)),
         (low, (rows, tile), part), (hidden, (rows, tile), part)],
        [out, out], after, flags,
    )


def outer_attn_kernel(own, flags, normed, grads, keep, send):
    width = grads.shape[1] // 3
    size = width // 2
    for i in range(3):
        value = rows_dot(normed[...], grads[:, i * width:(i + 1) * width])
        low, high = value[:, :size].astype(LOW), value[:, size:].astype(LOW)
        if own:
            low, high = jnp.where(flags[0] == 0, low, high), jnp.where(flags[0] == 0, high, low)
        keep[i] = low
        send[i] = high


def outer_attn(flags, own, normed, grads, after=()):
    rows, width = grads.shape[0], grads.shape[1] // 3
    model = normed.shape[1]
    tile = min(512, model)
    out = (shaped((3, model, width // 2)), (3, tile, width // 2), lambda i: (0, i, 0))
    return run(
        functools.partial(outer_attn_kernel, own), "outer_attn", (model // tile,),
        [(normed, (rows, tile), lambda i: (0, i)), (grads, (rows, 3 * width), lambda i: (0, 0))],
        [out, out], after, flags,
    )


def trade_kernel(tiles, compute, store, *refs):
    ins, out = refs[:-6], refs[-6]
    keep, send, got, send_sems, got_sems = refs[-5:]
    step = pl.program_id(0)
    me = lax.axis_index("dp")
    other = {"dp": me + 1 - 2 * (me % 2)}

    @pl.when(step == 0)
    def _():
        barrier = pltpu.get_barrier_semaphore()
        pl.semaphore_signal(barrier, inc=1, device_id=other, device_id_type=pl.DeviceIdType.MESH)
        pl.semaphore_wait(barrier, 1)

    def move(tile):
        return pltpu.make_async_remote_copy(
            src_ref=send.at[tile], dst_ref=got.at[tile], send_sem=send_sems.at[tile], recv_sem=got_sems.at[tile],
            device_id=other, device_id_type=pl.DeviceIdType.MESH,
        )

    compute(me % 2, ins, keep.at[step], send.at[step])
    move(step).start()

    @pl.when(step == tiles - 1)
    def _():
        for tile in range(tiles):
            move(tile).wait()
            store(out, tile, keep[tile] + got[tile])


def trade(name, collective, tiles, tile_shape, compute, store, ins, shape, after=()):
    buffer = pltpu.VMEM((tiles,) + tile_shape, LOW)
    return run(
        functools.partial(trade_kernel, tiles, compute, store), name, (tiles,), ins,
        [(shaped(shape), shape, lambda t: (0,) * len(shape))], after,
        scratch=[buffer, buffer, buffer, pltpu.SemaphoreType.DMA((tiles,)), pltpu.SemaphoreType.DMA((tiles,))],
        collective=collective,
    )[0]


def keep_and_send(own, core, value, axis, keep, send, index):
    size = value.shape[axis] // 2
    low = lax.slice_in_dim(value, 0, size, axis=axis).astype(LOW)
    high = lax.slice_in_dim(value, size, 2 * size, axis=axis).astype(LOW)
    if own:
        low, high = jnp.where(core == 0, low, high), jnp.where(core == 0, high, low)
    keep[index] = low
    send[index] = high


def store_columns(count, out, tile, value):
    size = value.shape[-1]
    out[tile // count, :, tile % count * size:(tile % count + 1) * size] = value


def trade_outer(collective, own, left, right, sides, after=()):
    _, rows, units = left.shape
    model = right.shape[1]
    tile, count = min(512, model), model // min(512, model)
    first = sides[0]

    def compute(core, ins, keep, send):
        keep_and_send(own, core, rows_dot(ins[0][0], ins[1][...]), 0, keep, send, slice(None))

    return trade(
        "trade_outer", collective, len(sides) * count, (units // 2, tile), compute, functools.partial(store_columns, count),
        [(left, (1, rows, units), lambda t: (first + t // count, 0, 0)), (right, (rows, tile), lambda t: (0, t % count))],
        (len(sides), units // 2, model), after,
    )


def trade_down(collective, own, gate, attended, low, hidden, after=()):
    _, rows, units = gate.shape
    width, model = attended.shape[1], low.shape[1]
    tile, count = min(512, model), model // min(512, model)
    part = lambda t: (0, t)
    size = units // 2

    def compute(core, ins, keep, send):
        gate, attended, low, hidden = ins
        keep_and_send(own, core, rows_dot(gate[0], low[...]), 0, keep, send, slice(0, size))
        keep_and_send(own, core, rows_dot(attended[...], hidden[...]), 0, keep, send, slice(size, size + width // 2))

    return trade(
        "trade_down", collective, count, (size + width // 2, tile), compute, functools.partial(store_columns, count),
        [(gate, (1, rows, units), lambda t: (0, 0, 0)), (attended, (rows, width), lambda t: (0, 0)),
         (low, (rows, tile), part), (hidden, (rows, tile), part)],
        (1, size + width // 2, model), after,
    )


def trade_attn(collective, own, normed, grads, after=()):
    rows, width = grads.shape[0], grads.shape[1] // 3
    model = normed.shape[1]
    tile, count = min(512, model), model // min(512, model)

    def compute(core, ins, keep, send):
        for i in range(3):
            value = rows_dot(ins[0][...], ins[1][:, i * width:(i + 1) * width])
            keep_and_send(own, core, value, 1, keep, send, i)

    def store(out, t, value):
        out[:, t * tile:(t + 1) * tile] = value

    return trade(
        "trade_attn", collective, count, (3, tile, width // 2), compute, store,
        [(normed, (rows, tile), lambda t: (0, t)), (grads, (rows, 3 * width), lambda t: (0, 0))],
        (3, model, width // 2), after,
    )


def pull_kernel(tokens, hidden_grad, gain, grads, weights, *refs):
    more, parts, (out, gain_ref) = refs[:1], refs[1:-2], refs[-2:]
    width = weights.shape[2]
    total = None
    for i in range(3):
        terms = [cols_dot(grads[:, i * width:(i + 1) * width], weights[i])]
        for side, part in enumerate(parts):
            size = part.shape[2]
            first = i * width + side * size
            terms.append(cols_dot(more[0][:, first:first + size], part[i]))
        for term in terms:
            total = term if total is None else total + term
    back, gain_part = norm_back_rows(tokens[...].astype(jnp.float32), gain[...], total)
    out[...] = hidden_grad[...] + back
    add_gain(gain_ref, gain_part)


def pull(tokens, hidden_grad, gain, grads, weights, more=None, parts=(), after=()):
    rows, model = tokens.shape
    tile = row_tile(rows)
    row = lambda i: (i, 0)
    size = grads.shape[1]
    return run(
        pull_kernel, "pull", (rows // tile,),
        [(tokens, (tile, model), row), (hidden_grad, (tile, model), row), whole(gain), (grads, (tile, size), row), whole(weights)]
        + [(grads if more is None else more, (tile, size), row)]
        + [(p, (3,) + p.shape[1:], lambda i: (0, 0, 0)) for p in parts],
        [(shaped((rows, model), jnp.float32), (tile, model), row), (shaped((1, model), jnp.float32), (1, model), lambda i: (0, 0))],
        after,
    )


def assemble_call(body, mine, other, core, outs, after):
    same = lambda i, s: (0,) * mine.ndim
    return pl.pallas_call(
        lambda *refs: body(*refs[:3], *refs[3 + len(after):]),
        grid_spec=pltpu.PrefetchScalarGridSpec(
            num_scalar_prefetch=1, grid=(2,),
            in_specs=[pl.BlockSpec(mine.shape, same)] * 2 + [pl.BlockSpec(memory_space=pl.ANY)] * len(after),
            out_specs=[
                pl.BlockSpec(block, functools.partial(lambda axis, rank, i, s: tuple((i ^ s[0]) * (d == axis) for d in range(rank)), axis, len(block)))
                for _, block, axis in outs
            ],
        ),
        out_shape=[shaped(shape, jnp.float32) for shape, _, _ in outs],
        compiler_params=pltpu.CompilerParams(vmem_limit_bytes=56 << 20),
        name="assemble",
    )(jnp.reshape(core, (1,)).astype(jnp.int32), mine, other, *after)


def assemble_kernel(side, mine, other, out):
    out[...] = jnp.where(pl.program_id(0) == 0, mine[...], other[...]).astype(jnp.float32)


def assemble(mine, other, core, axis, after=()):
    shape = tuple(2 * n if d == axis else n for d, n in enumerate(mine.shape))
    return assemble_call(assemble_kernel, mine, other, core, [(shape, mine.shape, axis)], after)[0]


def assemble_down_kernel(side, mine, other, down, out):
    chosen = jnp.where(pl.program_id(0) == 0, mine[0], other[0]).astype(jnp.float32)
    size = down.shape[0]
    down[...] = chosen[:size]
    out[...] = chosen[size:]


def assemble_down(mine, other, core, units, after=()):
    _, rows, model = mine.shape
    sizes = (units // 2, rows - units // 2)
    return assemble_call(
        assemble_down_kernel, mine, other, core, [((2 * n, model), (n, model), 0) for n in sizes], after
    )


class Links:
    def __init__(self, dp, tensor):
        self.dp, self.tensor = dp, tensor
        self.id = lax.axis_index("dp")
        self.core, self.row = self.id % 2, self.id // 2 % 2

    def send(self, value, target):
        pairs = [
            (d * self.tensor + t, to)
            for d in range(self.dp) for t in range(self.tensor)
            for to in [target(d, t)] if to is not None
        ]
        return lax.ppermute(value, AXES, pairs)

    def cross(self, value):
        return self.send(value, lambda d, t: d * self.tensor + (1 - t))

    def flip(self, value, even, odd=None):
        bits = (even, even if odd is None else odd)
        return self.send(value, lambda d, t: (d ^ bits[d % 2]) * self.tensor + t)

    def shift(self, value, by):
        return self.send(value, lambda d, t: d * self.tensor + t + by if 0 <= t + by < self.tensor else None)

    def bit_of(self, even, odd):
        return jnp.where(self.core == 0, (self.id & even) // even, (self.id & odd) // odd)


def tie(value, *others):
    return lax.optimization_barrier((value,) + others)[0]


def half(value, index, axis):
    size = value.shape[axis] // 2
    if isinstance(index, int):
        return lax.slice_in_dim(value, index * size, (index + 1) * size, axis=axis)
    return lax.dynamic_slice_in_dim(value, index * size, size, axis)


def order(bit, first, second, axis):
    return jnp.where(bit == 0, jnp.concatenate([first, second], axis), jnp.concatenate([second, first], axis))


class Summing:
    ROW_FIRST = ((2, 2, 1), (4, 4, 2), (8, 8, 3))
    SPLIT = ((2, 4, 4), (4, 8, 5), (8, 2, 6))

    def __init__(self, links, flags, axis, steps):
        self.links, self.flags, self.axis, self.steps = links, flags, axis, steps

    def send_far(self, far):
        self.far, self.crossed = far, self.links.cross(far)

    def across(self, *after, parts=None):
        self.split(0, self.near, self.crossed if parts is None else jnp.concatenate(parts, 0), after)

    def split(self, step, a, b, after):
        even, odd, which = self.steps[step]
        a, bit = tie(a, *after), self.flags[which]
        part = lambda k: half(a, k, self.axis) + half(b, k, self.axis)
        self.held, self.moved = part(bit), self.links.flip(part(1 - bit), even, odd)

    def scatter(self, *after):
        self.split(1, self.held, self.moved, after)

    def both(self, *after):
        self.held = tie(self.held, *after) + self.moved
        self.moved = self.links.flip(self.held, *self.steps[2][:2])

    def both_add(self, *after):
        self.held = tie(self.held, *after) + self.moved
        self.moved = self.links.flip(self.held, *self.steps[1][:2])

    def gather(self, *after):
        self.held = order(self.flags[self.steps[1][2]], tie(self.held, *after), self.moved, self.axis)
        self.moved = self.links.flip(self.held, *self.steps[0][:2])

    def last(self, *after):
        self.held = order(self.flags[self.steps[0][2]], tie(self.held, *after), self.moved, self.axis)
        self.moved = self.links.flip(self.held, 1)
        return self.held, self.moved, self.links.core


def on_device(tokens, lengths, order_, gain_attn, w_qkv, w_out, gain_mlp, w_in, w_down, cotangent):
    rows, model = tokens.shape
    dp, tensor = lax.axis_size("dp"), lax.axis_size("tensor")
    tensor_id = lax.axis_index("tensor")
    links = Links(dp, tensor)
    paired = tensor == 2 and dp == 16

    slot_count = rows * tensor // MAXLEN
    my_order = lax.dynamic_slice_in_dim(order_, links.id * slot_count, slot_count, 0)
    chosen = my_order[:, None] == jnp.arange(lengths.shape[0], dtype=jnp.int32)[None, :]
    slot_len = jnp.sum(jnp.where(chosen, lengths[None, :], 0), 1)
    slots = jnp.arange(slot_count, dtype=jnp.int32)[None, :]
    block_row = tensor_id * rows + BQ * jnp.arange(rows // BQ, dtype=jnp.int32)
    block_len = jnp.sum(jnp.where((block_row // MAXLEN)[:, None] == slots, slot_len[None, :], 0), 1)
    place = jnp.stack([block_row % MAXLEN, block_len])

    w_qkv = w_qkv.transpose(1, 0, 2)
    w_in = w_in.transpose(1, 2, 0)
    gain_attn, gain_mlp = gain_attn[None], gain_mlp[None]
    if not paired:
        before, after = links.shift(tokens[rows - HALF:], 1), links.shift(tokens[:HALF], -1)
        return general(
            links, place, tokens, before, after, gain_attn, w_qkv, w_out, gain_mlp, w_in, w_down, cotangent
        )

    start = jnp.where(tensor_id == 0, rows - HALF, 0)
    border = links.cross(lax.dynamic_slice_in_dim(tokens, start, HALF, 0))
    core = links.core
    bits = [links.id // bit % 2 for bit in (1, 2, 4, 8)]
    split_bits = [jnp.where(core == 0, bits[i], bits[j]) for i, j in ((1, 2), (2, 3), (3, 1))]
    flags = jnp.stack(bits + split_bits).astype(jnp.int32)
    place = jnp.concatenate([place, jnp.pad(flags, (0, place.shape[1] - flags.shape[0]))[None]], 0)
    width, units = w_out.shape[0], w_down.shape[0]
    size = width // 2
    attn_direct = links.cross(half(tie(w_qkv, border), core, 2))

    normed = norm_rows(tokens, border, border, gain_attn)
    quarter = lambda w, a, b: half(half(w, core, a), bits[1], b)
    out_piece = half(tie(w_out, normed), core, 0)
    out_direct = links.cross(out_piece)
    q0, k0, v0 = project(normed, w_qkv)
    attended0, logs0 = attend(place, q0, k0, v0)
    attn_parts = (attn_direct, links.flip(tie(attn_direct, attended0), 1))
    q1, k1, v1 = project_parts(normed, attn_parts, after=[attended0])
    out_direct = tie(out_direct, v1)
    in_piece = quarter(tie(w_in, out_direct), 1, 2)
    in_direct = links.cross(in_piece)
    down_direct = links.cross(half(tie(w_down, in_piece), core, 0))
    out_parts = (out_direct, links.flip(out_direct, 1))
    attended1, logs1 = attend(place, q1, k1, v1, after=[out_direct])
    hidden, normed_mlp = mix(tokens, gain_mlp, attended0, w_out, attended1, out_parts)
    in_direct = tie(in_direct, hidden)
    in_relayed = links.flip(in_direct, 2)
    in_core = links.flip(in_direct, 1)
    gate0, lift0, out_low, branch, pulled = mlp_first(place, normed_mlp, cotangent, w_in, w_down, after=[in_direct])
    in_relayed = tie(in_relayed, branch)
    down_direct = tie(down_direct, branch)
    weights = (
        in_direct, in_relayed, in_core, links.flip(in_relayed, 1), down_direct, links.flip(down_direct, 1),
    )
    gate1, lift1, output, hidden_grad, hidden_low, gain_mlp_grad, back0, back1 = mlp_last(
        place, normed_mlp, cotangent, weights, hidden, gain_mlp, branch, pulled, w_out, out_parts
    )
    inner = Summing(links, flags, 2, Summing.ROW_FIRST)
    inner_a, inner_b = (Summing(links, flags, 2, Summing.ROW_FIRST) for _ in range(2))
    down = Summing(links, flags, 2, Summing.SPLIT)
    attn = Summing(links, flags, 1, Summing.SPLIT)

    inner_a.send_far(trade_outer(0, False, lift1, normed_mlp, [0], after=[back1]))
    inner_b.send_far(trade_outer(1, False, lift1, normed_mlp, [1], after=[inner_a.far]))
    inner.near = trade_outer(2, True, lift0, normed_mlp, [0, 1], after=[inner_b.far])

    swap = lambda e: jnp.where(core == 0, e, jnp.concatenate([e[:, size:], e[:, :size]], 1))

    def trade_edge(edge):
        chosen = jnp.where(tensor_id == 0, edge[1], edge[0])
        return links.cross(jnp.concatenate([swap(chosen[:, :width]), swap(chosen[:, width:])], 1))

    def add_edge(d, edge):
        held = lax.dynamic_slice(d, (start, width), (HALF, 2 * width))
        return lax.dynamic_update_slice(d, held + edge, (start, width))

    d0, edge0 = attend_back(place, q0, k0, v0, back0, logs0, after=[inner.near])
    edge_other = trade_edge(edge0)
    far = trade_down(3, False, gate1, attended1, out_low, hidden_low, after=[d0, inner_a.crossed])
    down.send_far(tie(far, edge_other))
    inner.across(down.far, parts=[inner_a.crossed, inner_b.crossed])
    d1, edge1 = attend_back(place, q1, k1, v1, back1, logs1, after=[inner.held])
    edge_own = trade_edge(edge1)
    d1 = add_edge(d1, edge_other)
    far = trade_attn(5, False, normed, d1)
    inner.scatter(far)
    attn.send_far(tie(far, edge_own))
    down.near = trade_down(4, True, gate0, attended0, out_low, hidden_low, after=[inner.held])
    inner.both(down.near)
    down.across(inner.held)
    d0 = add_edge(tie(d0, down.held), edge_own)
    attn.near = trade_attn(6, True, normed, d0)
    down.scatter(attn.near)
    inner.both_add(down.held)
    attn.across(inner.held)
    input_grad, gain_attn_grad = pull(tokens, hidden_grad, gain_attn, d0, w_qkv, d1, attn_parts, after=[attn.held])
    gain_total = jnp.concatenate((gain_attn_grad, gain_mlp_grad))
    inner.gather(input_grad)
    down.both(inner.held)
    attn.scatter(down.held)
    gain_total = gain_total + tie(links.cross(gain_total), attn.held)
    down.both_add(attn.held, gain_total)
    gain_total = gain_total + tie(links.flip(gain_total, 1), down.held)
    attn.both(down.held, gain_total)
    down.gather(attn.held)
    attn.both_add(down.held)
    gain_total = gain_total + tie(links.flip(gain_total, 2), attn.held)
    grads_in = inner.last(attn.held)
    grads_down = down.last(grads_in[0], gain_total)
    gain_total = gain_total + tie(links.flip(gain_total, 4), grads_down[0])
    grad_w_in = assemble(*grads_in, 1, after=[grads_down[0]])
    attn.gather(grad_w_in, gain_total)
    gain_total = gain_total + tie(links.flip(gain_total, 8), attn.held)
    grads_attn = attn.last(attn.held)
    grad_w_down, grad_w_out = assemble_down(*grads_down, units, after=[grads_attn[0]])
    grad_w_qkv = assemble(*grads_attn, 2, after=[grad_w_down, gain_total])
    return (
        output,
        input_grad,
        gain_total[0],
        grad_w_qkv.transpose(1, 0, 2),
        grad_w_out,
        gain_total[1],
        grad_w_in.transpose(2, 0, 1),
        grad_w_down,
    )


def general(links, place, tokens, before, after, gain_attn, w_qkv, w_out, gain_mlp, w_in, w_down, cotangent):
    rows = tokens.shape[0]
    w_qkv, w_out, w_in, w_down = (
        lax.all_gather(w, "tensor", axis=axis, tiled=True)
        for w, axis in ((w_qkv, 2), (w_out, 0), (w_in, 1), (w_down, 0))
    )
    normed = norm_rows(tokens, before, after, gain_attn)
    q, k, v = project(normed, w_qkv)
    attended, logs = attend(place, q, k, v)
    hidden, normed_mlp = mix(tokens, gain_mlp, attended, w_out)
    blank = jnp.zeros_like(hidden)
    gate, lift, output, hidden_grad, hidden_low, gain_mlp_grad, back = mlp_last(
        place, normed_mlp, cotangent, (w_in, w_down), hidden, gain_mlp, blank, blank, w_out
    )
    position = jnp.repeat(place[0], BQ) + jnp.tile(jnp.arange(BQ, dtype=jnp.int32), place.shape[1])
    out_low = jnp.where((position < jnp.repeat(place[1], BQ))[:, None], cotangent, jnp.zeros_like(cotangent))
    flags = jnp.zeros((1,), jnp.int32)
    units, width = w_down.shape[0], w_out.shape[0]
    low, high = outer_down(flags, False, gate, attended, out_low, hidden_low)
    down = jnp.concatenate([low[0, :units // 2], high[0, :units // 2]], 0)
    out = jnp.concatenate([low[0, units // 2:], high[0, units // 2:]], 0)
    inner = jnp.concatenate(outer(flags, False, lift, normed_mlp), 1)
    d, edge = attend_back(place, q, k, v, back, logs)
    d = d.at[:HALF, width:].add(links.shift(edge[1], 1)).at[rows - HALF:, width:].add(links.shift(edge[0], -1))
    qkv = jnp.concatenate(outer_attn(flags, False, normed, d), 2)
    input_grad, gain_attn_grad = pull(tokens, hidden_grad, gain_attn, d, w_qkv)
    down, inner, out, qkv = (
        lax.psum(lax.psum_scatter(g, "tensor", scatter_dimension=axis, tiled=True), "dp").astype(jnp.float32)
        for g, axis in ((down, 0), (inner, 1), (out, 0), (qkv, 2))
    )
    gain_total = lax.psum(jnp.concatenate((gain_attn_grad, gain_mlp_grad)), AXES)
    return (
        output, input_grad, gain_total[0], qkv.transpose(1, 0, 2), out, gain_total[1],
        inner.transpose(2, 0, 1), down,
    )


def solution(mesh):
    split = P(AXES, None)
    wide = P(None, None, "tensor")
    tall = P("tensor", None)
    return jax.shard_map(
        on_device,
        mesh=mesh,
        in_specs=(split, P(), P(), P(), wide, tall, P(), wide, tall, split),
        out_specs=(split, split, P(), wide, tall, P(), wide, tall),
        check_vma=False,
    )
```

```python
import functools
import math

import jax
import jax.numpy as jnp
from jax import lax
from jax.experimental import pallas as pl
from jax.experimental.pallas import tpu as pltpu
from jax.sharding import PartitionSpec as P

AXES = ("dp", "tensor")
EPS = 1e-05
HEAD_DIM = 64
HALF = 64
MAXLEN = 1024
BQ = 128
LOW = jnp.bfloat16
NEG = -1e30


def cols_dot(left, right):
    return lax.dot_general(left, right, (((1,), (1,)), ((), ())), preferred_element_type=jnp.float32)


def rows_dot(left, right):
    return lax.dot_general(left, right, (((0,), (0,)), ((), ())), preferred_element_type=jnp.float32)


def plain_dot(left, right):
    return lax.dot_general(left, right, (((1,), (0,)), ((), ())), preferred_element_type=jnp.float32)


def norm_parts(values):
    center = values - jnp.mean(values, -1, keepdims=True)
    rate = lax.rsqrt(jnp.mean(center * center, -1, keepdims=True) + EPS)
    return center * rate, rate


COST = {
    "norm_rows": 6, "project": 9, "project_parts": 9, "attend": 20, "mix": 11, "mlp_first": 39, "mlp_last": 49, "outer": 9,
    "attend_back": 25, "trade_outer": 9, "trade_down": 12, "trade_attn": 10, "outer_down": 12, "outer_attn": 10, "pull": 18,
}
SCALE = 100


def shaped(shape, dtype=LOW):
    return jax.ShapeDtypeStruct(shape, dtype)


def run(body, name, grid, ins, outs, after=(), place=None, scratch=(), flops=0, vmem=56, seen=False, collective=None):
    extra = [a for a in after if a is not None]
    count = len(ins)

    def kernel(*refs):
        lead = refs[:1] if place is not None else ()
        refs = refs[len(lead):]
        body(*lead, *refs[:count], *refs[count + len(extra):])

    def spec(block, index):
        if place is not None and not seen:
            return pl.BlockSpec(block, lambda *a: index(*a[:-1]))
        return pl.BlockSpec(block, index)

    call = pl.pallas_call(
        kernel,
        grid_spec=pltpu.PrefetchScalarGridSpec(
            num_scalar_prefetch=0 if place is None else 1,
            grid=grid,
            in_specs=[spec(b, m) for _, b, m in ins] + [pl.BlockSpec(memory_space=pl.ANY)] * len(extra),
            out_specs=[spec(b, m) for _, b, m in outs],
            scratch_shapes=list(scratch),
        ),
        out_shape=[s for s, _, _ in outs],
        compiler_params=pltpu.CompilerParams(
            vmem_limit_bytes=vmem << 20, collective_id=collective, has_side_effects=collective is not None
        ),
        cost_estimate=pl.CostEstimate(flops=int(COST[name] * SCALE), bytes_accessed=1000, transcendentals=0),
        name=name,
    )
    lead = () if place is None else (place,)
    return call(*lead, *[a for a, _, _ in ins], *extra)


def window_masks(shared, ones, pos0, length):
    j = lax.broadcasted_iota(jnp.int32, (BQ, 2 * BQ), 0)
    i = lax.broadcasted_iota(jnp.int32, (BQ, 2 * BQ), 1) % BQ

    @pl.when(pl.program_id(0) == 0)
    def _():
        shared[0] = j + jnp.where(i <= j, 0, BQ)
        shared[1] = jnp.where(j == (i + HALF) % BQ, 1, 0)
        ones[0] = jnp.where(i <= j, 1.0, 0.0).astype(LOW)
        ones[1] = jnp.where(i == j, 1.0, 0.0).astype(LOW)

    key = shared[0]
    top = jnp.minimum(length, MAXLEN)
    bias = jnp.where(((key >= HALF - pos0) & (key < top - pos0 + HALF)) | (shared[1] > 0), 0.0, NEG)
    lane = lax.broadcasted_iota(jnp.int32, (1, 2 * BQ), 1) % BQ
    last_bias = jnp.where(pos0 + HALF + lane < top, 0.0, NEG)
    return key < BQ, i == j, bias, last_bias


def split_heads(pair):
    lane = lax.broadcasted_iota(jnp.int32, pair.shape, 1)
    zero = jnp.zeros_like(pair)
    return jnp.concatenate([jnp.where(lane < HEAD_DIM, pair, zero), jnp.where(lane >= HEAD_DIM, pair, zero)], 0)


def join_heads(wide, scale=None):
    first, second = wide[:HEAD_DIM, :BQ], wide[HEAD_DIM:, BQ:]
    if scale is not None:
        first, second = first * scale[:, :BQ], second * scale[:, BQ:]
    return jnp.concatenate([first, second], 0).T


def fold(near, diag, wide):
    low = wide[BQ:]
    return jnp.where(near, wide[:BQ], low), jnp.sum(jnp.where(diag, low, 0.0), 0, keepdims=True)


def unfold(ones, tile, last):
    tile = tile.astype(LOW)
    upper = tile * ones[0]
    return jnp.concatenate([upper, (tile - upper) + ones[1] * last.astype(LOW)], 0)


def window_rows(before, here, after, c):
    return jnp.concatenate([before[:, c], here[:, c], after[:, c]], 0)


def attend_kernel(place, q, kb, kh, ka, vb, vh, va, out_ref, log_ref, shared, ones):
    blk = pl.program_id(0)
    near, diag, bias, last_bias = window_masks(shared, ones, place[0, blk], place[1, blk])
    columns = [slice(p * BQ, (p + 1) * BQ) for p in range(out_ref.shape[1] // BQ)]

    def score(c):
        return cols_dot(window_rows(kb, kh, ka, c), split_heads(q[:, c] * 0.125))

    def soft(wide):
        scores, last = fold(near, diag, wide)
        scores, last = scores + bias, last + last_bias
        row_max = jnp.maximum(jnp.max(scores, 0, keepdims=True), last)
        expons, last = jnp.exp(scores - row_max), jnp.exp(last - row_max)
        summed = jnp.sum(expons, 0, keepdims=True) + last
        return unfold(ones, expons, last), row_max, summed

    wides = [score(c) for c in columns]
    softs = [soft(w) for w in wides]
    for pair, c in enumerate(columns):
        probs, row_max, summed = softs[pair]
        out_ref[:, c] = join_heads(rows_dot(window_rows(vb, vh, va, c), probs), 1.0 / summed).astype(LOW)
        log_ref[0, pair:pair + 1] = row_max + jnp.log(summed)


def attend_back_kernel(place, q, kb, kh, ka, vb, vh, va, g_ref, log_ref, d_ref, edge_ref, carry, tail, dq_keep, shared, ones):
    step = pl.program_id(0)
    steps = pl.num_programs(0)
    width = g_ref.shape[1]

    @pl.when(step == 0)
    def _():
        carry[...] = jnp.zeros_like(carry)
        tail[...] = jnp.zeros_like(tail)
        dq_keep[...] = jnp.zeros_like(dq_keep)

    d_ref[:, :width] = dq_keep[...]
    d_ref[:HALF, width:] = tail[...]

    @pl.when(step < steps - 1)
    def _():
        near, diag, bias, last_bias = window_masks(shared, ones, place[0, step], place[1, step])
        columns = [slice(p * BQ, (p + 1) * BQ) for p in range(width // BQ)]

        def start(c):
            queries = split_heads(q[:, c] * 0.125)
            grads = split_heads(g_ref[:, c])
            keyset = window_rows(kb, kh, ka, c)
            return queries, grads, keyset, cols_dot(keyset, queries), cols_dot(window_rows(vb, vh, va, c), grads)

        starts = [start(c) for c in columns]
        for pair, c in enumerate(columns):
            ready = starts[pair]
            v = slice(width + c.start, width + c.stop)
            queries, grads, keyset, wide, wide_grad = ready
            log_row = log_ref[0, pair:pair + 1]
            scores, last = fold(near, diag, wide)
            expons, last = jnp.exp(scores + (bias - log_row)), jnp.exp(last + (last_bias - log_row))
            prob_grad, last_grad = fold(near, diag, wide_grad)
            inner = jnp.sum(expons * prob_grad, 0, keepdims=True) + last * last_grad
            score_grad = unfold(ones, expons * (prob_grad - inner), last * (last_grad - inner))
            probs = unfold(ones, expons, last)
            dq_keep[:, c] = join_heads(rows_dot(keyset, score_grad) * 0.125).astype(LOW)
            for lanes, grad in ((c, plain_dot(score_grad, queries)), (v, plain_dot(probs, grads))):
                done = (carry[:, lanes] + grad[:BQ]).astype(LOW)
                carry[:, lanes] = grad[BQ:]
                d_ref[HALF:, lanes.start + width:lanes.stop + width] = done[:HALF]
                tail[:, lanes] = done[HALF:]

        @pl.when(step == 0)
        def _():
            edge_ref[0] = d_ref[HALF:, width:]

    @pl.when(step == steps - 1)
    def _():
        done = carry[...].astype(LOW)
        d_ref[HALF:, width:] = done[:HALF]
        edge_ref[1] = done[HALF:]


def window_specs(q, k, v, blocks):
    last, width = blocks - 1, k.shape[1]
    here = lambda b: (jnp.minimum(b, last), 0)
    before = lambda b: (jnp.where(b == 0, 2 * blocks, 2 * jnp.minimum(b, last) - 1), 0)
    after = lambda b: (jnp.where(b >= last, 2 * blocks + 1, 2 * b + 2), 0)
    specs = [(q, (BQ, width), here)]
    for value in (k, v):
        specs += [(value, (HALF, width), before), (value, (BQ, width), here), (value, (HALF, width), after)]
    return specs


def attend(place, q, k, v, after=()):
    blocks, width = k.shape[0] // BQ - 1, k.shape[1]
    pairs = width // BQ
    return run(
        attend_kernel, "attend", (blocks,), window_specs(q, k, v, blocks),
        [
            (shaped((blocks * BQ, width)), (BQ, width), lambda b: (b, 0)),
            (shaped((blocks, pairs, 2 * BQ), jnp.float32), (1, pairs, 2 * BQ), lambda b: (b, 0, 0)),
        ],
        after, place, scratch=[pltpu.VMEM((2, BQ, 2 * BQ), jnp.int32), pltpu.VMEM((2, BQ, 2 * BQ), LOW)],
    )


def attend_back(place, q, k, v, grads, logs, after=()):
    blocks, width = grads.shape[0] // BQ, k.shape[1]
    pairs = width // BQ
    last = blocks - 1
    return run(
        attend_back_kernel, "attend_back", (blocks + 1,),
        window_specs(q, k, v, blocks)
        + [
            (grads, (BQ, width), lambda b: (jnp.minimum(b, last), 0)),
            (logs, (1, pairs, 2 * BQ), lambda b: (jnp.minimum(b, last), 0, 0)),
        ],
        [
            (shaped((blocks * BQ, 3 * width)), (BQ, 3 * width), lambda b: (jnp.maximum(b - 1, 0), 0)),
            (shaped((2, HALF, 2 * width)), (2, HALF, 2 * width), lambda b: (0, 0, 0)),
        ],
        after, place,
        scratch=[
            pltpu.VMEM((BQ, 2 * width), jnp.float32),
            pltpu.VMEM((HALF, 2 * width), LOW),
            pltpu.VMEM((BQ, width), LOW),
            pltpu.VMEM((2, BQ, 2 * BQ), jnp.int32),
            pltpu.VMEM((2, BQ, 2 * BQ), LOW),
        ],
        flops=blocks * pairs * BQ * BQ * BQ * 512,
    )


def norm_kernel(tokens, before, after, gain, out):
    step, tile = pl.program_id(0), tokens.shape[0]

    @pl.when(step < pl.num_programs(0) - 1)
    def _():
        out[...] = (norm_parts(tokens[...].astype(jnp.float32))[0] * gain[...]).astype(LOW)

    @pl.when(step == pl.num_programs(0) - 1)
    def _():
        values = jnp.concatenate([before[...], after[...]], 0).astype(jnp.float32)
        out[:BQ] = (norm_parts(values)[0] * gain[...]).astype(LOW)


def norm_rows(tokens, before, after, gain):
    rows, model = tokens.shape
    tile = 3 * BQ
    blocks = rows // tile
    full = lambda i: (0, 0)
    return run(
        norm_kernel, "norm_rows", (blocks + 1,),
        [
            (tokens, (tile, model), lambda i: (jnp.minimum(i, blocks - 1), 0)),
            (before, (HALF, model), full), (after, (HALF, model), full), (gain, (1, model), full),
        ],
        [(shaped((rows + BQ, model)), (tile, model), lambda i: (i, 0))],
    )[0]


def project_kernel(normed, weights, *outs):
    for i, out in enumerate(outs):
        out[...] = plain_dot(normed[...], weights[i]).astype(LOW)


def project(normed, weights, after=()):
    rows, model = normed.shape
    width = weights.shape[2]
    tile = rows // 4 if rows % 64 == 0 else rows
    return run(
        project_kernel, "project", (rows // tile,),
        [(normed, (tile, model), lambda i: (i, 0)), (weights, (3, model, width), lambda i: (0, 0, 0))],
        [(shaped((rows, width)), (tile, width), lambda i: (i, 0))] * 3,
        after, flops=6 * rows * model * width,
    )


def project_parts_kernel(normed, mine, other, *outs):
    size = mine.shape[2]
    for i, out in enumerate(outs):
        out[:, :size] = plain_dot(normed[...], mine[i]).astype(LOW)
        out[:, size:] = plain_dot(normed[...], other[i]).astype(LOW)


def project_parts(normed, parts, after=()):
    rows, model = normed.shape
    size = parts[0].shape[2]
    tile = rows // 4
    return run(
        project_parts_kernel, "project_parts", (rows // tile,),
        [(normed, (tile, model), lambda i: (i, 0))] + [(p, (3, model, size), lambda i: (0, 0, 0)) for p in parts],
        [(shaped((rows, 2 * size)), (tile, 2 * size), lambda i: (i, 0))] * 3,
        after,
    )


def row_tile(rows):
    return 256 if rows % 256 == 0 else 128


def keep_rows(place, step, tile):
    row = lax.broadcasted_iota(jnp.int32, (BQ, 1), 0)
    parts = []
    for i in range(tile // BQ):
        b = step * (tile // BQ) + i
        parts.append(jnp.where(row + place[0, b] < place[1, b], 1.0, 0.0))
    return jnp.concatenate(parts, 0)


def mix_kernel(tokens, gain, attended, weights, *refs):
    attended_more, parts, (hidden, normed) = refs[:1], refs[1:-2], refs[-2:]
    total = tokens[...].astype(jnp.float32) + plain_dot(attended[...], weights[...])
    for side, part in enumerate(parts):
        size = part.shape[0]
        total = total + plain_dot(attended_more[0][:, side * size:(side + 1) * size], part[...])
    hidden[...] = total
    normed[...] = (norm_parts(total)[0] * gain[...]).astype(LOW)


def mix(tokens, gain, attended, weights, more=None, parts=(), after=()):
    rows, model = tokens.shape
    tile = row_tile(rows)
    row, full = (lambda i: (i, 0)), (lambda i: (0, 0))
    width = weights.shape[0]
    return run(
        mix_kernel, "mix", (rows // tile,),
        [(tokens, (tile, model), row), (gain, (1, model), full), (attended, (tile, width), row), (weights, weights.shape, full)]
        + [(attended if more is None else more, (tile, width), row)]
        + [whole(p) for p in parts],
        [(shaped((rows, model), jnp.float32), (tile, model), row), (shaped((rows, model)), (tile, model), row)],
        after,
    )


def gelu_parts(value):
    size = jnp.abs(value)
    bell = jnp.exp(-0.5 * value * value)
    t = 1.0 / (1.0 + (0.3275911 * 2.0 ** -0.5) * size)
    series = t * (0.254829592 + t * (-0.284496736 + t * (1.421413741 + t * (-1.453152027 + t * 1.061405429))))
    tail = 0.5 * series * bell
    below = jnp.where(value < 0, tail, 1.0 - tail)
    return value * below, below + value * bell * ((2.0 * math.pi) ** -0.5)


def mlp_body(place, normed, cotangent, win, wdown, gate_ref, lift_ref):
    tile = normed.shape[0]
    kept = keep_rows(place, pl.program_id(0), tile)
    out_grad = kept * cotangent[...].astype(jnp.float32)
    out_low = out_grad.astype(LOW)
    first = cols_dot(normed[...], win[0])
    second = cols_dot(normed[...], win[1])
    gelu, slope = gelu_parts(first)
    gate = (gelu * second).astype(LOW)
    gate_ref[0] = gate
    branch = plain_dot(gate, wdown[...])
    grad = cols_dot(out_low, wdown[...])
    lift1 = (grad * second * slope).astype(LOW)
    lift2 = (grad * gelu).astype(LOW)
    lift_ref[0] = lift1
    lift_ref[1] = lift2
    pulled = plain_dot(lift1, win[0]) + plain_dot(lift2, win[1])
    return kept, out_grad, out_low, branch, pulled


def mlp_first_kernel(place, normed, cotangent, win, wdown, gate_ref, lift_ref, low_ref, branch_ref, pulled_ref):
    _, _, out_low, branch, pulled = mlp_body(place, normed, cotangent, win, wdown, gate_ref, lift_ref)
    low_ref[...] = out_low
    branch_ref[...] = branch
    pulled_ref[...] = pulled


def norm_back_rows(values, gain, grad):
    unit, rate = norm_parts(values)
    pulled = grad * gain
    mean_one = jnp.mean(pulled, -1, keepdims=True)
    mean_two = jnp.mean(pulled * unit, -1, keepdims=True)
    return rate * (pulled - mean_one - unit * mean_two), jnp.sum(grad * unit, 0, keepdims=True)


def add_gain(gain_ref, part):
    @pl.when(pl.program_id(0) == 0)
    def _():
        gain_ref[...] = jnp.zeros_like(gain_ref)

    gain_ref[...] += part


def mlp_last_kernel(fetched, place, normed, cotangent, *refs):
    if fetched:
        pieces, refs = refs[:6], refs[6:]
        win, wdown = refs[-2:]

        @pl.when(pl.program_id(0) == 0)
        def _():
            units, model = pieces[0].shape[1:]
            for part in range(4):
                rows = slice(part // 2 * units, (part // 2 + 1) * units)
                columns = pl.ds(pl.multiple_of((place[2, 1] ^ (part % 2)) * model, model), model)
                for side in range(2):
                    win[side, rows, columns] = pieces[part][side]
            for side in range(2):
                wdown[side * units:(side + 1) * units] = pieces[4 + side][...]
    else:
        (win, wdown), refs = refs[:2], refs[2:]
    hidden, gain, branch_in, pulled_in, weights = refs[:5]
    parts, refs = (refs[5:7], refs[7:]) if fetched else ((), refs[5:])
    gate_ref, lift_ref, out_ref, grad_ref, low_ref, gain_ref, attn = refs[:7]
    kept, out_grad, _, branch, pulled = mlp_body(place, normed, cotangent, win, wdown, gate_ref, lift_ref)
    out_ref[...] = (kept * (hidden[...] + (branch_in[...] + branch))).astype(LOW)
    back, gain_part = norm_back_rows(hidden[...], gain[...], pulled_in[...] + pulled)
    total = out_grad + back
    grad_ref[...] = total
    low = total.astype(LOW)
    low_ref[...] = low
    attn[...] = cols_dot(low, weights[...]).astype(LOW)
    for side, part in enumerate(parts):
        size = part.shape[0]
        refs[7][:, side * size:(side + 1) * size] = cols_dot(low, part[...]).astype(LOW)
    add_gain(gain_ref, gain_part)


def mlp_specs(normed, cotangent, units):
    rows, model = normed.shape
    tile = row_tile(rows)
    row = lambda i: (i, 0)
    ins = [(normed, (tile, model), row), (cotangent, (tile, model), row)]
    outs = [
        (shaped((1, rows, units)), (1, tile, units), lambda i: (0, i, 0)),
        (shaped((2, rows, units)), (2, tile, units), lambda i: (0, i, 0)),
    ]
    return rows, model, tile, row, ins, outs


def whole(value):
    return (value, value.shape, lambda i: (0,) * value.ndim)


def mlp_first(place, normed, cotangent, win, wdown, after=()):
    rows, model, tile, row, ins, outs = mlp_specs(normed, cotangent, wdown.shape[0])
    outs = outs + [(shaped((rows, model)), (tile, model), row)]
    outs = outs + [(shaped((rows, model), jnp.float32), (tile, model), row)] * 2
    return run(mlp_first_kernel, "mlp_first", (rows // tile,), ins + [whole(win), whole(wdown)], outs, after, place)


def mlp_last(place, normed, cotangent, weights, hidden, gain, branch, pulled, w_out, parts=(), after=()):
    fetched = len(weights) == 6
    units = 2 * weights[4].shape[0] if fetched else weights[1].shape[0]
    rows, model, tile, row, ins, outs = mlp_specs(normed, cotangent, units)
    block = (tile, model)
    ins = ins + [whole(w) for w in weights]
    ins = ins + [(hidden, block, row), whole(gain), (branch, block, row), (pulled, block, row), whole(w_out)]
    ins = ins + [whole(p) for p in parts]
    outs = outs + [
        (shaped((rows, model)), block, row), (shaped((rows, model), jnp.float32), block, row),
        (shaped((rows, model)), block, row), (shaped((1, model), jnp.float32), (1, model), lambda i: (0, 0)),
    ]
    width = w_out.shape[0]
    outs = outs + [(shaped((rows, width)), (tile, width), row)] * (2 if fetched else 1)
    scratch = [pltpu.VMEM((2, units, model), LOW), pltpu.VMEM((units, model), LOW)] if fetched else []
    return run(
        functools.partial(mlp_last_kernel, fetched), "mlp_last", (rows // tile,), ins, outs, after, place, scratch, vmem=60
    )


def store_halves(value, core, keep, send, index):
    size = value.shape[0] // 2
    low, high = value[:size].astype(LOW), value[size:].astype(LOW)
    if core is None:
        keep[index], send[index] = low, high
    else:
        keep[index] = jnp.where(core == 0, low, high)
        send[index] = jnp.where(core == 0, high, low)


def outer_kernel(own, flags, left, right, keep, send):
    store_halves(rows_dot(left[0], right[...]), flags[0] if own else None, keep, send, 0)


def outer(flags, own, left, right, after=(), side=None):
    sides, rows, units = left.shape
    model = right.shape[1]
    tile = min(512, model)
    first = 0 if side is None else side
    sides = sides if side is None else 1
    out = (shaped((sides, units // 2, model)), (1, units // 2, tile), lambda s, j: (s, 0, j))
    return run(
        functools.partial(outer_kernel, own), "outer", (sides, model // tile),
        [(left, (1, rows, units), lambda s, j: (s + first, 0, 0)), (right, (rows, tile), lambda s, j: (0, j))],
        [out, out], after, flags,
    )


def outer_down_kernel(own, flags, gate, attended, low, hidden, keep, send):
    first, second = rows_dot(gate[0], low[...]), rows_dot(attended[...], hidden[...])
    core = flags[0] if own else None
    size = first.shape[0] // 2
    store_halves(first, core, keep.at[:, :size], send.at[:, :size], 0)
    store_halves(second, core, keep.at[:, size:], send.at[:, size:], 0)


def outer_down(flags, own, gate, attended, low, hidden, after=()):
    _, rows, units = gate.shape
    width, model = attended.shape[1], low.shape[1]
    tile = min(512, model)
    part = lambda j: (0, j)
    out = (shaped((1, (units + width) // 2, model)), (1, (units + width) // 2, tile), lambda j: (0, 0, j))
    return run(
        functools.partial(outer_down_kernel, own), "outer_down", (model // tile,),
        [(gate, (1, rows, units), lambda j: (0, 0, 0)), (attended, (rows, width), lambda j: (0, 0)),
         (low, (rows, tile), part), (hidden, (rows, tile), part)],
        [out, out], after, flags,
    )


def outer_attn_kernel(own, flags, normed, grads, keep, send):
    width = grads.shape[1] // 3
    size = width // 2
    for i in range(3):
        value = rows_dot(normed[...], grads[:, i * width:(i + 1) * width])
        low, high = value[:, :size].astype(LOW), value[:, size:].astype(LOW)
        if own:
            low, high = jnp.where(flags[0] == 0, low, high), jnp.where(flags[0] == 0, high, low)
        keep[i] = low
        send[i] = high


def outer_attn(flags, own, normed, grads, after=()):
    rows, width = grads.shape[0], grads.shape[1] // 3
    model = normed.shape[1]
    tile = min(512, model)
    out = (shaped((3, model, width // 2)), (3, tile, width // 2), lambda i: (0, i, 0))
    return run(
        functools.partial(outer_attn_kernel, own), "outer_attn", (model // tile,),
        [(normed, (rows, tile), lambda i: (0, i)), (grads, (rows, 3 * width), lambda i: (0, 0))],
        [out, out], after, flags,
    )


def trade_kernel(tiles, compute, store, *refs):
    ins, out = refs[:-6], refs[-6]
    keep, send, got, send_sems, got_sems = refs[-5:]
    step = pl.program_id(0)
    me = lax.axis_index("dp")
    other = {"dp": me + 1 - 2 * (me % 2)}

    @pl.when(step == 0)
    def _():
        barrier = pltpu.get_barrier_semaphore()
        pl.semaphore_signal(barrier, inc=1, device_id=other, device_id_type=pl.DeviceIdType.MESH)
        pl.semaphore_wait(barrier, 1)

    def move(tile):
        return pltpu.make_async_remote_copy(
            src_ref=send.at[tile], dst_ref=got.at[tile], send_sem=send_sems.at[tile], recv_sem=got_sems.at[tile],
            device_id=other, device_id_type=pl.DeviceIdType.MESH,
        )

    compute(me % 2, ins, keep.at[step], send.at[step])
    move(step).start()

    @pl.when(step == tiles - 1)
    def _():
        for tile in range(tiles):
            move(tile).wait()
            store(out, tile, keep[tile] + got[tile])


def trade(name, collective, tiles, tile_shape, compute, store, ins, shape, after=()):
    buffer = pltpu.VMEM((tiles,) + tile_shape, LOW)
    return run(
        functools.partial(trade_kernel, tiles, compute, store), name, (tiles,), ins,
        [(shaped(shape), shape, lambda t: (0,) * len(shape))], after,
        scratch=[buffer, buffer, buffer, pltpu.SemaphoreType.DMA((tiles,)), pltpu.SemaphoreType.DMA((tiles,))],
        collective=collective,
    )[0]


def keep_and_send(own, core, value, axis, keep, send, index):
    size = value.shape[axis] // 2
    low = lax.slice_in_dim(value, 0, size, axis=axis).astype(LOW)
    high = lax.slice_in_dim(value, size, 2 * size, axis=axis).astype(LOW)
    if own:
        low, high = jnp.where(core == 0, low, high), jnp.where(core == 0, high, low)
    keep[index] = low
    send[index] = high


def store_columns(count, out, tile, value):
    size = value.shape[-1]
    out[tile // count, :, tile % count * size:(tile % count + 1) * size] = value


def trade_outer(collective, own, left, right, sides, after=()):
    _, rows, units = left.shape
    model = right.shape[1]
    tile, count = min(512, model), model // min(512, model)
    first = sides[0]

    def compute(core, ins, keep, send):
        keep_and_send(own, core, rows_dot(ins[0][0], ins[1][...]), 0, keep, send, slice(None))

    return trade(
        "trade_outer", collective, len(sides) * count, (units // 2, tile), compute, functools.partial(store_columns, count),
        [(left, (1, rows, units), lambda t: (first + t // count, 0, 0)), (right, (rows, tile), lambda t: (0, t % count))],
        (len(sides), units // 2, model), after,
    )


def trade_down(collective, own, gate, attended, low, hidden, after=()):
    _, rows, units = gate.shape
    width, model = attended.shape[1], low.shape[1]
    tile, count = min(512, model), model // min(512, model)
    part = lambda t: (0, t)
    size = units // 2

    def compute(core, ins, keep, send):
        gate, attended, low, hidden = ins
        keep_and_send(own, core, rows_dot(gate[0], low[...]), 0, keep, send, slice(0, size))
        keep_and_send(own, core, rows_dot(attended[...], hidden[...]), 0, keep, send, slice(size, size + width // 2))

    return trade(
        "trade_down", collective, count, (size + width // 2, tile), compute, functools.partial(store_columns, count),
        [(gate, (1, rows, units), lambda t: (0, 0, 0)), (attended, (rows, width), lambda t: (0, 0)),
         (low, (rows, tile), part), (hidden, (rows, tile), part)],
        (1, size + width // 2, model), after,
    )


def trade_attn(collective, own, normed, grads, after=()):
    rows, width = grads.shape[0], grads.shape[1] // 3
    model = normed.shape[1]
    tile, count = min(512, model), model // min(512, model)

    def compute(core, ins, keep, send):
        for i in range(3):
            value = rows_dot(ins[0][...], ins[1][:, i * width:(i + 1) * width])
            keep_and_send(own, core, value, 1, keep, send, i)

    def store(out, t, value):
        out[:, t * tile:(t + 1) * tile] = value

    return trade(
        "trade_attn", collective, count, (3, tile, width // 2), compute, store,
        [(normed, (rows, tile), lambda t: (0, t)), (grads, (rows, 3 * width), lambda t: (0, 0))],
        (3, model, width // 2), after,
    )


def pull_kernel(tokens, hidden_grad, gain, grads, weights, *refs):
    more, parts, (out, gain_ref) = refs[:1], refs[1:-2], refs[-2:]
    width = weights.shape[2]
    total = None
    for i in range(3):
        terms = [cols_dot(grads[:, i * width:(i + 1) * width], weights[i])]
        for side, part in enumerate(parts):
            size = part.shape[2]
            first = i * width + side * size
            terms.append(cols_dot(more[0][:, first:first + size], part[i]))
        for term in terms:
            total = term if total is None else total + term
    back, gain_part = norm_back_rows(tokens[...].astype(jnp.float32), gain[...], total)
    out[...] = hidden_grad[...] + back
    add_gain(gain_ref, gain_part)


def pull(tokens, hidden_grad, gain, grads, weights, more=None, parts=(), after=()):
    rows, model = tokens.shape
    tile = row_tile(rows)
    row = lambda i: (i, 0)
    size = grads.shape[1]
    return run(
        pull_kernel, "pull", (rows // tile,),
        [(tokens, (tile, model), row), (hidden_grad, (tile, model), row), whole(gain), (grads, (tile, size), row), whole(weights)]
        + [(grads if more is None else more, (tile, size), row)]
        + [(p, (3,) + p.shape[1:], lambda i: (0, 0, 0)) for p in parts],
        [(shaped((rows, model), jnp.float32), (tile, model), row), (shaped((1, model), jnp.float32), (1, model), lambda i: (0, 0))],
        after,
    )


def assemble_call(body, mine, other, core, outs, after):
    same = lambda i, s: (0,) * mine.ndim
    return pl.pallas_call(
        lambda *refs: body(*refs[:3], *refs[3 + len(after):]),
        grid_spec=pltpu.PrefetchScalarGridSpec(
            num_scalar_prefetch=1, grid=(2,),
            in_specs=[pl.BlockSpec(mine.shape, same)] * 2 + [pl.BlockSpec(memory_space=pl.ANY)] * len(after),
            out_specs=[
                pl.BlockSpec(block, functools.partial(lambda axis, rank, i, s: tuple((i ^ s[0]) * (d == axis) for d in range(rank)), axis, len(block)))
                for _, block, axis in outs
            ],
        ),
        out_shape=[shaped(shape, jnp.float32) for shape, _, _ in outs],
        compiler_params=pltpu.CompilerParams(vmem_limit_bytes=56 << 20),
        name="assemble",
    )(jnp.reshape(core, (1,)).astype(jnp.int32), mine, other, *after)


def assemble_kernel(side, mine, other, out):
    out[...] = jnp.where(pl.program_id(0) == 0, mine[...], other[...]).astype(jnp.float32)


def assemble(mine, other, core, axis, after=()):
    shape = tuple(2 * n if d == axis else n for d, n in enumerate(mine.shape))
    return assemble_call(assemble_kernel, mine, other, core, [(shape, mine.shape, axis)], after)[0]


def assemble_down_kernel(side, mine, other, down, out):
    chosen = jnp.where(pl.program_id(0) == 0, mine[0], other[0]).astype(jnp.float32)
    size = down.shape[0]
    down[...] = chosen[:size]
    out[...] = chosen[size:]


def assemble_down(mine, other, core, units, after=()):
    _, rows, model = mine.shape
    sizes = (units // 2, rows - units // 2)
    return assemble_call(
        assemble_down_kernel, mine, other, core, [((2 * n, model), (n, model), 0) for n in sizes], after
    )


class Links:
    def __init__(self, dp, tensor):
        self.dp, self.tensor = dp, tensor
        self.id = lax.axis_index("dp")
        self.core, self.row = self.id % 2, self.id // 2 % 2

    def send(self, value, target):
        pairs = [
            (d * self.tensor + t, to)
            for d in range(self.dp) for t in range(self.tensor)
            for to in [target(d, t)] if to is not None
        ]
        return lax.ppermute(value, AXES, pairs)

    def cross(self, value):
        return self.send(value, lambda d, t: d * self.tensor + (1 - t))

    def flip(self, value, even, odd=None):
        bits = (even, even if odd is None else odd)
        return self.send(value, lambda d, t: (d ^ bits[d % 2]) * self.tensor + t)

    def shift(self, value, by):
        return self.send(value, lambda d, t: d * self.tensor + t + by if 0 <= t + by < self.tensor else None)

    def bit_of(self, even, odd):
        return jnp.where(self.core == 0, (self.id & even) // even, (self.id & odd) // odd)


def tie(value, *others):
    return lax.optimization_barrier((value,) + others)[0]


def half(value, index, axis):
    size = value.shape[axis] // 2
    if isinstance(index, int):
        return lax.slice_in_dim(value, index * size, (index + 1) * size, axis=axis)
    return lax.dynamic_slice_in_dim(value, index * size, size, axis)


def order(bit, first, second, axis):
    return jnp.where(bit == 0, jnp.concatenate([first, second], axis), jnp.concatenate([second, first], axis))


class Summing:
    ROW_FIRST = ((2, 2, 1), (4, 4, 2), (8, 8, 3))
    SPLIT = ((2, 4, 4), (4, 8, 5), (8, 2, 6))

    def __init__(self, links, flags, axis, steps):
        self.links, self.flags, self.axis, self.steps = links, flags, axis, steps

    def send_far(self, far):
        self.far, self.crossed = far, self.links.cross(far)

    def across(self, *after, parts=None):
        self.split(0, self.near, self.crossed if parts is None else jnp.concatenate(parts, 0), after)

    def split(self, step, a, b, after):
        even, odd, which = self.steps[step]
        a, bit = tie(a, *after), self.flags[which]
        part = lambda k: half(a, k, self.axis) + half(b, k, self.axis)
        self.held, self.moved = part(bit), self.links.flip(part(1 - bit), even, odd)

    def scatter(self, *after):
        self.split(1, self.held, self.moved, after)

    def both(self, *after):
        self.held = tie(self.held, *after) + self.moved
        self.moved = self.links.flip(self.held, *self.steps[2][:2])

    def both_add(self, *after):
        self.held = tie(self.held, *after) + self.moved
        self.moved = self.links.flip(self.held, *self.steps[1][:2])

    def gather(self, *after):
        self.held = order(self.flags[self.steps[1][2]], tie(self.held, *after), self.moved, self.axis)
        self.moved = self.links.flip(self.held, *self.steps[0][:2])

    def last(self, *after):
        self.held = order(self.flags[self.steps[0][2]], tie(self.held, *after), self.moved, self.axis)
        self.moved = self.links.flip(self.held, 1)
        return self.held, self.moved, self.links.core


def on_device(tokens, lengths, order_, gain_attn, w_qkv, w_out, gain_mlp, w_in, w_down, cotangent):
    rows, model = tokens.shape
    dp, tensor = lax.axis_size("dp"), lax.axis_size("tensor")
    tensor_id = lax.axis_index("tensor")
    links = Links(dp, tensor)
    paired = tensor == 2 and dp == 16

    slot_count = rows * tensor // MAXLEN
    my_order = lax.dynamic_slice_in_dim(order_, links.id * slot_count, slot_count, 0)
    chosen = my_order[:, None] == jnp.arange(lengths.shape[0], dtype=jnp.int32)[None, :]
    slot_len = jnp.sum(jnp.where(chosen, lengths[None, :], 0), 1)
    slots = jnp.arange(slot_count, dtype=jnp.int32)[None, :]
    block_row = tensor_id * rows + BQ * jnp.arange(rows // BQ, dtype=jnp.int32)
    block_len = jnp.sum(jnp.where((block_row // MAXLEN)[:, None] == slots, slot_len[None, :], 0), 1)
    place = jnp.stack([block_row % MAXLEN, block_len])

    w_qkv = w_qkv.transpose(1, 0, 2)
    w_in = w_in.transpose(1, 2, 0)
    gain_attn, gain_mlp = gain_attn[None], gain_mlp[None]
    if not paired:
        before, after = links.shift(tokens[rows - HALF:], 1), links.shift(tokens[:HALF], -1)
        return general(
            links, place, tokens, before, after, gain_attn, w_qkv, w_out, gain_mlp, w_in, w_down, cotangent
        )

    start = jnp.where(tensor_id == 0, rows - HALF, 0)
    border = links.cross(lax.dynamic_slice_in_dim(tokens, start, HALF, 0))
    core = links.core
    bits = [links.id // bit % 2 for bit in (1, 2, 4, 8)]
    split_bits = [jnp.where(core == 0, bits[i], bits[j]) for i, j in ((1, 2), (2, 3), (3, 1))]
    flags = jnp.stack(bits + split_bits).astype(jnp.int32)
    place = jnp.concatenate([place, jnp.pad(flags, (0, place.shape[1] - flags.shape[0]))[None]], 0)
    width, units = w_out.shape[0], w_down.shape[0]
    size = width // 2
    attn_direct = links.cross(half(tie(w_qkv, border), core, 2))

    normed = norm_rows(tokens, border, border, gain_attn)
    quarter = lambda w, a, b: half(half(w, core, a), bits[1], b)
    out_piece = half(tie(w_out, normed), core, 0)
    out_direct = links.cross(out_piece)
    q0, k0, v0 = project(normed, w_qkv)
    attended0, logs0 = attend(place, q0, k0, v0)
    attn_parts = (attn_direct, links.flip(tie(attn_direct, attended0), 1))
    q1, k1, v1 = project_parts(normed, attn_parts, after=[attended0])
    out_direct = tie(out_direct, v1)
    in_piece = quarter(tie(w_in, out_direct), 1, 2)
    in_direct = links.cross(in_piece)
    down_direct = links.cross(half(tie(w_down, in_piece), core, 0))
    out_parts = (out_direct, links.flip(out_direct, 1))
    attended1, logs1 = attend(place, q1, k1, v1, after=[out_direct])
    hidden, normed_mlp = mix(tokens, gain_mlp, attended0, w_out, attended1, out_parts)
    in_direct = tie(in_direct, hidden)
    in_relayed = links.flip(in_direct, 2)
    in_core = links.flip(in_direct, 1)
    gate0, lift0, out_low, branch, pulled = mlp_first(place, normed_mlp, cotangent, w_in, w_down, after=[in_direct])
    in_relayed = tie(in_relayed, branch)
    down_direct = tie(down_direct, branch)
    weights = (
        in_direct, in_relayed, in_core, links.flip(in_relayed, 1), down_direct, links.flip(down_direct, 1),
    )
    gate1, lift1, output, hidden_grad, hidden_low, gain_mlp_grad, back0, back1 = mlp_last(
        place, normed_mlp, cotangent, weights, hidden, gain_mlp, branch, pulled, w_out, out_parts
    )
    inner = Summing(links, flags, 2, Summing.ROW_FIRST)
    inner_a, inner_b = (Summing(links, flags, 2, Summing.ROW_FIRST) for _ in range(2))
    down = Summing(links, flags, 2, Summing.SPLIT)
    attn = Summing(links, flags, 1, Summing.SPLIT)

    inner_a.send_far(trade_outer(0, False, lift1, normed_mlp, [0], after=[back1]))
    inner_b.send_far(trade_outer(1, False, lift1, normed_mlp, [1], after=[inner_a.far]))
    inner.near = trade_outer(2, True, lift0, normed_mlp, [0, 1], after=[inner_b.far])

    swap = lambda e: jnp.where(core == 0, e, jnp.concatenate([e[:, size:], e[:, :size]], 1))

    def trade_edge(edge):
        chosen = jnp.where(tensor_id == 0, edge[1], edge[0])
        return links.cross(jnp.concatenate([swap(chosen[:, :width]), swap(chosen[:, width:])], 1))

    def add_edge(d, edge):
        held = lax.dynamic_slice(d, (start, width), (HALF, 2 * width))
        return lax.dynamic_update_slice(d, held + edge, (start, width))

    d0, edge0 = attend_back(place, q0, k0, v0, back0, logs0, after=[inner.near])
    edge_other = trade_edge(edge0)
    far = trade_down(3, False, gate1, attended1, out_low, hidden_low, after=[d0, inner_a.crossed])
    down.send_far(tie(far, edge_other))
    inner.across(down.far, parts=[inner_a.crossed, inner_b.crossed])
    d1, edge1 = attend_back(place, q1, k1, v1, back1, logs1, after=[inner.held])
    edge_own = trade_edge(edge1)
    d1 = add_edge(d1, edge_other)
    far = trade_attn(5, False, normed, d1)
    inner.scatter(far)
    attn.send_far(tie(far, edge_own))
    down.near = trade_down(4, True, gate0, attended0, out_low, hidden_low, after=[inner.held])
    inner.both(down.near)
    down.across(inner.held)
    d0 = add_edge(tie(d0, down.held), edge_own)
    attn.near = trade_attn(6, True, normed, d0)
    down.scatter(attn.near)
    attn.across(down.held)
    inner.both_add(attn.held)
    input_grad, gain_attn_grad = pull(tokens, hidden_grad, gain_attn, d0, w_qkv, d1, attn_parts, after=[inner.held])
    gain_total = jnp.concatenate((gain_attn_grad, gain_mlp_grad))
    inner.gather(input_grad)
    down.both(inner.held)
    attn.scatter(down.held)
    gain_total = gain_total + tie(links.cross(gain_total), attn.held)
    down.both_add(attn.held, gain_total)
    gain_total = gain_total + tie(links.flip(gain_total, 1), down.held)
    attn.both(down.held, gain_total)
    down.gather(attn.held)
    attn.both_add(down.held)
    gain_total = gain_total + tie(links.flip(gain_total, 2), attn.held)
    grads_in = inner.last(attn.held)
    grads_down = down.last(grads_in[0], gain_total)
    gain_total = gain_total + tie(links.flip(gain_total, 4), grads_down[0])
    grad_w_in = assemble(*grads_in, 1, after=[grads_down[0]])
    attn.gather(grad_w_in, gain_total)
    gain_total = gain_total + tie(links.flip(gain_total, 8), attn.held)
    grads_attn = attn.last(attn.held)
    grad_w_down, grad_w_out = assemble_down(*grads_down, units, after=[grads_attn[0]])
    grad_w_qkv = assemble(*grads_attn, 2, after=[grad_w_down, gain_total])
    return (
        output,
        input_grad,
        gain_total[0],
        grad_w_qkv.transpose(1, 0, 2),
        grad_w_out,
        gain_total[1],
        grad_w_in.transpose(2, 0, 1),
        grad_w_down,
    )


def general(links, place, tokens, before, after, gain_attn, w_qkv, w_out, gain_mlp, w_in, w_down, cotangent):
    rows = tokens.shape[0]
    w_qkv, w_out, w_in, w_down = (
        lax.all_gather(w, "tensor", axis=axis, tiled=True)
        for w, axis in ((w_qkv, 2), (w_out, 0), (w_in, 1), (w_down, 0))
    )
    normed = norm_rows(tokens, before, after, gain_attn)
    q, k, v = project(normed, w_qkv)
    attended, logs = attend(place, q, k, v)
    hidden, normed_mlp = mix(tokens, gain_mlp, attended, w_out)
    blank = jnp.zeros_like(hidden)
    gate, lift, output, hidden_grad, hidden_low, gain_mlp_grad, back = mlp_last(
        place, normed_mlp, cotangent, (w_in, w_down), hidden, gain_mlp, blank, blank, w_out
    )
    position = jnp.repeat(place[0], BQ) + jnp.tile(jnp.arange(BQ, dtype=jnp.int32), place.shape[1])
    out_low = jnp.where((position < jnp.repeat(place[1], BQ))[:, None], cotangent, jnp.zeros_like(cotangent))
    flags = jnp.zeros((1,), jnp.int32)
    units, width = w_down.shape[0], w_out.shape[0]
    low, high = outer_down(flags, False, gate, attended, out_low, hidden_low)
    down = jnp.concatenate([low[0, :units // 2], high[0, :units // 2]], 0)
    out = jnp.concatenate([low[0, units // 2:], high[0, units // 2:]], 0)
    inner = jnp.concatenate(outer(flags, False, lift, normed_mlp), 1)
    d, edge = attend_back(place, q, k, v, back, logs)
    d = d.at[:HALF, width:].add(links.shift(edge[1], 1)).at[rows - HALF:, width:].add(links.shift(edge[0], -1))
    qkv = jnp.concatenate(outer_attn(flags, False, normed, d), 2)
    input_grad, gain_attn_grad = pull(tokens, hidden_grad, gain_attn, d, w_qkv)
    down, inner, out, qkv = (
        lax.psum(lax.psum_scatter(g, "tensor", scatter_dimension=axis, tiled=True), "dp").astype(jnp.float32)
        for g, axis in ((down, 0), (inner, 1), (out, 0), (qkv, 2))
    )
    gain_total = lax.psum(jnp.concatenate((gain_attn_grad, gain_mlp_grad)), AXES)
    return (
        output, input_grad, gain_total[0], qkv.transpose(1, 0, 2), out, gain_total[1],
        inner.transpose(2, 0, 1), down,
    )


def solution(mesh):
    split = P(AXES, None)
    wide = P(None, None, "tensor")
    tall = P("tensor", None)
    return jax.shard_map(
        on_device,
        mesh=mesh,
        in_specs=(split, P(), P(), P(), wide, tall, P(), wide, tall, split),
        out_specs=(split, split, P(), wide, tall, P(), wide, tall),
        check_vma=False,
    )
```
